32 devices in a mesh: band: 4 (over y, x), wave: 8 (over z, core).
Axes of the slice: x: 2, y: 2, z: 4, core: 2. Of those that a mesh axis runs over, the one named last changes fastest.
Arguments:
- spectral: bfloat16 [640, 1408, 8], P('wave', 'band'), may hold values from -0.119628906 to 0.119628906
- legendre: bfloat16 [640, 1280, 1408], P('wave', 'band'), may hold values from -0.15625 to 0.15625
- slot_pair: int32 [640], replicated, may hold values from 0 to 639, each once
- quad_weight: float32 [1280], P('band'), may hold values from 0.4 to 2.5
- depart_code: int32 [1, 2, 1280, 5120], P(None, None, ('band', 'wave')), may hold values from 0 to 15
- stencil_pick: int32 [1, 2, 1280, 5120], P(None, None, ('band', 'wave')), may hold values from 0 to 15
- stencil_weight: float32 [16, 16], replicated, may hold values from -0.05 to 0.175
Outputs:
- arrival: bfloat16 [1, 4, 2, 1280, 5120], P(None, None, None, ('band', 'wave'))
- spectral_out: bfloat16 [640, 1408, 8], P('wave', 'band')
The draws below stay inside these ranges and needn't reach their ends.
Inputs may be any that keep to these rules, and one draw needn't show every extreme that they name: A permutation: slot s holds the wavenumbers slot_pair[s] and 1279 - slot_pair[s]. Decodes to a latitude step depart_code // 4 - 2 and a longitude step depart_code % 4 - 2.
All inputs are finite; a program needn't handle non-finite values.
Results may differ from the reference program's by a relative error of at most 0.02.
Values may be sent and summed in bfloat16 or wider, within the bound.
No kernel may reach another device: no remote copies, remote signals or barrier semaphores. Data moves between devices by JAX's collectives and lax.ppermute only.
A program may use at most 640 MiB of HBM per device.

```python
import math
import jax
import jax.numpy as jnp
from jax import lax

M = 1280
NLATH = 1280
NLON = 5120
FIELDS = 4
LEV = 1
DR = 2
DL = 2
NSTEN = 16
RIM = 3
COLS = 8
SLOTS = 640
NROW = 1408


def touch_ends(values, own_key, low, top_value):
    place = [jax.random.randint(jax.random.fold_in(own_key, axis), (), 0, length) for axis, length in enumerate(values.shape)]
    main_axis = values.shape.index(max(values.shape))
    next_to = place[:main_axis] + [(place[main_axis] + 1) % values.shape[main_axis]] + place[main_axis + 1:]
    return values.at[tuple(place)].set(low).at[tuple(next_to)].set(top_value)


def block_levels(stream_key, dims, cuts, low, high):
    def one(dim, blocks):
        draws = jax.random.uniform(jax.random.fold_in(jax.random.fold_in(stream_key, 6), dim), (blocks,), jnp.float32, low / len(cuts), high / len(cuts))
        return jnp.repeat(jnp.exp(draws), dims[dim] // blocks).reshape((-1,) + (1,) * (len(dims) - dim - 1))

    factor_of = one(*cuts[0])
    for cut in cuts[1:]:
        factor_of = factor_of * one(*cut)
    return factor_of


def scatter_about(rng, extent, spread, bound, split=(), held_as=jnp.bfloat16):
    loudness = block_levels(rng, extent, split, -0.22, 0.18) if split else 1.0
    entries = jax.random.normal(rng, extent, jnp.float32) * spread * loudness
    return jnp.minimum(jnp.maximum(entries, -bound), bound).astype(held_as)


def setup_inputs(seed: int = 0) -> dict:
    key_list = jax.random.split(jax.random.key(seed), 8)
    return {
        "spectral": scatter_about(key_list[0], (SLOTS, NROW, COLS), 0.02, 0.119628906, ((0, 8), (1, 4))),
        "legendre": scatter_about(key_list[1], (SLOTS, NLATH, NROW), NROW ** -0.5, 0.15625, ((0, 8), (1, 4))),
        "slot_pair": jax.random.permutation(key_list[2], SLOTS).astype(jnp.int32),
        "quad_weight": jnp.clip(jnp.exp(math.log(2.5) - 1.8325814 * jax.random.uniform(key_list[3], (NLATH,), jnp.float32) ** block_levels(key_list[3], (NLATH,), ((0, 4),), -0.2, 0.2)), 0.4, 2.5),
        "depart_code": touch_ends(jax.random.randint(key_list[4], (LEV, 2, NLATH, NLON), 0, 4 * DR * DL), jax.random.fold_in(key_list[4], 1), 0, (4 * DR * DL) - 1).astype(jnp.int32),
        "stencil_pick": touch_ends(jax.random.randint(key_list[5], (LEV, 2, NLATH, NLON), 0, NSTEN), jax.random.fold_in(key_list[5], 1), 0, NSTEN - 1).astype(jnp.int32),
        "stencil_weight": jnp.clip(jax.random.uniform(key_list[6], (NSTEN, 16), jnp.float32, -0.05, 0.175), -0.05, 0.175),
    }


def row_weights(pair_ids, row_index, wavenumbers):
    low_count = wavenumbers - pair_ids[:, None]
    higher = row_index[None, :] >= low_count
    in_use = (row_index[None, :] <= wavenumbers).astype(jnp.float32)
    degree = jnp.where(higher, row_index[None, :] - low_count, row_index[None, :])
    parity_sign = 1.0 - 2.0 * (degree % 2).astype(jnp.float32)
    high_part = higher.astype(jnp.float32)
    holder = jnp.stack([1.0 - high_part, high_part], axis=-1) * in_use[..., None]
    hemisphere = jnp.stack([jnp.ones_like(parity_sign), parity_sign], axis=-1)
    return holder[..., :, None] * hemisphere[..., None, :]

def wave_factor(slot_pair, wavenumbers):
    wave_pair = jnp.stack([slot_pair, wavenumbers - 1 - slot_pair], axis=1)
    return jnp.where(wave_pair == 0, 1.0, 2.0).astype(jnp.float32)

def angle_table(slot_pair, wavenumbers, longitudes):
    group_size = math.gcd(slot_pair.shape[0], 40)
    groups = slot_pair.reshape(-1, group_size)
    column = jnp.arange(longitudes, dtype=jnp.int32)

    def build(pair_ids):
        wave_pair = jnp.stack([pair_ids, wavenumbers - 1 - pair_ids], axis=1)
        residue = wave_pair[..., None] * column % longitudes
        angles = residue.astype(jnp.float32) * (2.0 * math.pi / longitudes)
        factor = jnp.where(wave_pair == 0, 1.0, 2.0).astype(jnp.float32)[..., None]
        result = jnp.stack([factor * jnp.cos(angles), -factor * jnp.sin(angles)], axis=2)
        return result.astype(jnp.bfloat16)
    return lax.map(build, groups).reshape(-1, longitudes)

def interpolate(padded, departure, tap_weight):
    levels, fields, hemispheres, padded_rows, longitudes = padded.shape
    height = padded_rows - 2 * RIM
    flat_values = padded.reshape(levels, fields, hemispheres * padded_rows * longitudes)
    row_shift = departure // (2 * DL) - DR
    col_shift = departure % (2 * DL) - DL
    hemi_index = jnp.arange(hemispheres, dtype=jnp.int32)[None, :, None, None]
    lat_index = jnp.arange(height, dtype=jnp.int32)[None, None, :, None]
    lon_index = jnp.arange(longitudes, dtype=jnp.int32)[None, None, None, :]
    running = jnp.zeros((levels, fields, hemispheres, height, longitudes), jnp.float32)
    for tap_index in range(16):
        source_row = lat_index + RIM + row_shift + tap_index // 4 - 1
        source_col = (lon_index + col_shift + tap_index % 4 - 1) % longitudes
        position = ((hemi_index * padded_rows + source_row) * longitudes + source_col).reshape(levels, 1, -1)
        position = jnp.broadcast_to(position, (levels, fields, position.shape[2]))
        picked = jnp.take_along_axis(flat_values, position, axis=2).reshape(running.shape)
        running = running + tap_weight(tap_index)[:, None] * picked.astype(jnp.float32)
    return running

def reference(spectral, legendre, slot_pair, quad_weight, depart_code, stencil_pick, stencil_weight):
    slot_total, row_total, col_total = spectral.shape
    group_size = math.gcd(slot_total, 40)
    masks = row_weights(slot_pair, jnp.arange(row_total, dtype=jnp.int32), M)

    def inverse_group(operands):
        spec_part, legendre_part, mask_part = operands
        masked = spec_part.astype(jnp.float32)[:, :, None, None, :] * mask_part[..., None]
        result = jnp.einsum('sjohc,sij->sohci', masked, legendre_part.astype(jnp.float32))
        return result.astype(jnp.bfloat16)
    fourier = lax.map(inverse_group, (spectral.reshape(-1, group_size, row_total, col_total), legendre.reshape(-1, group_size, NLATH, row_total), masks.reshape(-1, group_size, row_total, 2, 2)))
    fourier = fourier.reshape(slot_total, 2, 2, LEV, FIELDS, 2, NLATH)
    left_rows = fourier.transpose(3, 4, 2, 6, 0, 1, 5).reshape(LEV * FIELDS * 2 * NLATH, slot_total * 4)
    angle_rows = angle_table(slot_pair, M, NLON)
    grid_values = jnp.dot(left_rows, angle_rows, preferred_element_type=jnp.float32)
    grid_values = grid_values.astype(jnp.bfloat16).reshape(LEV, FIELDS, 2, NLATH, NLON)
    pole_rows = jnp.roll(jnp.flip(grid_values[:, :, :, :RIM], 3), NLON // 2, 4)
    equator_rows = jnp.flip(grid_values[:, :, ::-1, NLATH - RIM:], 3)
    padded = jnp.concatenate([pole_rows, grid_values, equator_rows], 3)

    def tap_weight(tap_index):
        return jnp.take(stencil_weight[:, tap_index], stencil_pick, axis=0)
    arrival = interpolate(padded, depart_code, tap_weight).astype(jnp.bfloat16)
    sums = lax.dot_general(arrival.reshape(-1, NLON), angle_rows, (((1,), (1,)), ((), ())), preferred_element_type=jnp.float32)
    sums = sums.reshape(LEV, FIELDS, 2, NLATH, slot_total, 2, 2)
    scaling = quad_weight[:, None, None] / (wave_factor(slot_pair, M)[None] * math.sqrt(NLON))
    coeffs = (sums * scaling[None, None, None, :, :, :, None]).astype(jnp.bfloat16)
    coeffs = coeffs.transpose(4, 5, 2, 0, 1, 6, 3).reshape(slot_total, 2, 2, col_total, NLATH)

    def direct_group(operands):
        legendre_part, coeff_part, mask_part = operands
        partial_sum = jnp.einsum('sij,sohci->sjohc', legendre_part.astype(jnp.float32), coeff_part.astype(jnp.float32))
        joined = jnp.einsum('sjohc,sjoh->sjc', partial_sum, mask_part, precision=lax.Precision.HIGHEST)
        return joined.astype(jnp.bfloat16)
    spectral_out = lax.map(direct_group, (legendre.reshape(-1, group_size, NLATH, row_total), coeffs.reshape(-1, group_size, 2, 2, col_total, NLATH), masks.reshape(-1, group_size, row_total, 2, 2)))
    spectral_out = spectral_out.reshape(slot_total, row_total, col_total)
    return (arrival, spectral_out)
```

```python
import functools
import math

import jax
import jax.numpy as jnp
import numpy as np
from jax import lax
from jax.experimental import pallas as pl
from jax.experimental.pallas import tpu as pltpu
from jax.sharding import PartitionSpec as P

M = 1280
NLON = 5120
HALF = NLON // 2
FIELDS = 4
NSTEN = 16
RIM = 3
COLS = 8
GROUP = 8
WIDE = GROUP * 4 * COLS
RUN = 5
SUB = 8
REACH = RUN + 2 * RIM
BLOCKS = NLON // 128
TILES = 10
F32 = jnp.float32
BF16 = jnp.bfloat16
VMEM_LIMIT = 60 * 2**20


def dot_nt(left, right):
    return lax.dot_general(left, right, (((1,), (1,)), ((), ())), preferred_element_type=F32)


def lane_order():
    index = np.arange(WIDE).reshape(GROUP, 2, 2, FIELDS, 2).transpose(1, 2, 3, 0, 4).reshape(-1)
    matrix = np.zeros((WIDE, WIDE), np.float32)
    matrix[index, np.arange(WIDE)] = 1.0
    return jnp.asarray(matrix, BF16)


def row_masks(pair, rows):
    row = lax.broadcasted_iota(jnp.int32, (1, rows), 1)
    low_count = M - pair
    higher = row >= low_count
    degree = jnp.where(higher, row - low_count, row)
    sign = (1 - 2 * (degree & 1)).astype(F32)
    in_use = row <= M
    side = jnp.where(higher, 1, 0) ^ (pair & 1)
    even = jnp.where(in_use & (side == 0), 1.0, 0.0)
    odd = jnp.where(in_use & (side == 1), 1.0, 0.0)
    return even, odd, sign


def forward_kernel(height, pair_ref, spec_ref, leg_ref, out_ref, rhs_ref, acc_ref):
    group = pl.program_id(0)
    rows = spec_ref.shape[2]
    sub = height // RUN

    @pl.when(group == 0)
    def _():
        rhs_ref[...] = jnp.zeros_like(rhs_ref)

    for u in range(GROUP):
        even, odd, sign = row_masks(pair_ref[group * GROUP + u], rows)
        spec = spec_ref[u].astype(F32)
        south = spec * sign
        parts = [spec * even, south * even, spec * odd, south * odd]
        rhs_ref[u, 32 * u : 32 * u + 32, :] = jnp.concatenate(parts, axis=0).astype(BF16)
        part = dot_nt(leg_ref[u], rhs_ref[u])
        for half in range(2):
            piece = part[:, 128 * half : 128 * half + 128]
            if u == 0:
                acc_ref[half] = piece
            else:
                acc_ref[half] += piece
    for dest in range(out_ref.shape[0]):
        halves = []
        for half in range(2):
            pieces = [
                acc_ref[half, pl.ds(dest * height + k, sub, stride=RUN), :] for k in range(RUN)
            ]
            halves.append(jnp.concatenate(pieces, axis=0))
        out_ref[dest, 0] = jnp.concatenate(halves, axis=1).astype(BF16)


def legendre_forward(pairs, spec, legendre, waves):
    slots, lats, rows = legendre.shape
    groups = slots // GROUP
    height = lats // waves
    return pl.pallas_call(
        functools.partial(forward_kernel, height),
        out_shape=jax.ShapeDtypeStruct((waves, groups, height, WIDE), BF16),
        grid=(groups,),
        in_specs=[
            pl.BlockSpec(memory_space=pltpu.SMEM),
            pl.BlockSpec((GROUP, COLS, rows), lambda g: (g, 0, 0)),
            pl.BlockSpec((GROUP, lats, rows), lambda g: (g, 0, 0)),
        ],
        out_specs=pl.BlockSpec((waves, 1, height, WIDE), lambda g: (0, g, 0, 0)),
        scratch_shapes=[
            pltpu.VMEM((GROUP, WIDE, rows), BF16),
            pltpu.VMEM((2, lats, 128), F32),
        ],
        compiler_params=pltpu.CompilerParams(vmem_limit_bytes=VMEM_LIMIT),
        cost_estimate=pl.CostEstimate(
            flops=2 * slots * lats * rows * WIDE,
            bytes_accessed=2 * slots * lats * rows,
            transcendentals=0,
        ),
        name="legendre_forward",
    )(pairs, spec, legendre)


def backward_kernel(height, pair_ref, perm_ref, coef_ref, leg_ref, out_ref, rows_ref):
    group = pl.program_id(0)
    rows = leg_ref.shape[2]
    sub = height // RUN
    for source in range(coef_ref.shape[0]):
        block = coef_ref[source, 0].astype(F32)
        for k in range(RUN):
            for half in range(2):
                rows_ref[half, pl.ds(source * height + k, sub, stride=RUN), :] = block[
                    k * sub : (k + 1) * sub, 128 * half : 128 * half + 128
                ]
    natural = jnp.concatenate([rows_ref[0], rows_ref[1]], axis=1).astype(BF16)
    turned = dot_nt(perm_ref[...], natural).astype(BF16)
    sums = []
    for u in range(GROUP):
        even, odd, sign = row_masks(pair_ref[group * GROUP + u], rows)
        raw = jnp.dot(turned[32 * u : 32 * u + 32], leg_ref[u], preferred_element_type=F32)
        low = raw[0:8] + sign * raw[8:16]
        high = raw[16:24] + sign * raw[24:32]
        sums.append(low * even + high * odd)
        if u % 2 == 1:
            out_ref[8 * (u - 1) : 8 * (u + 1), :] = jnp.concatenate(sums[-2:], axis=0).astype(BF16)


def legendre_backward(pairs, perm, coefs, legendre):
    slots, lats, rows = legendre.shape
    waves, groups, height, _ = coefs.shape
    return pl.pallas_call(
        functools.partial(backward_kernel, height),
        out_shape=jax.ShapeDtypeStruct((slots * COLS, rows), BF16),
        grid=(groups,),
        in_specs=[
            pl.BlockSpec(memory_space=pltpu.SMEM),
            pl.BlockSpec((WIDE, WIDE), lambda g: (0, 0)),
            pl.BlockSpec((waves, 1, height, WIDE), lambda g: (0, g, 0, 0)),
            pl.BlockSpec((GROUP, lats, rows), lambda g: (g, 0, 0)),
        ],
        out_specs=pl.BlockSpec((GROUP * COLS, rows), lambda g: (g, 0)),
        scratch_shapes=[pltpu.VMEM((2, lats, 128), F32)],
        compiler_params=pltpu.CompilerParams(vmem_limit_bytes=VMEM_LIMIT),
        cost_estimate=pl.CostEstimate(
            flops=2 * slots * lats * rows * 32,
            bytes_accessed=2 * slots * lats * rows,
            transcendentals=0,
        ),
        name="legendre_backward",
    )(pairs, perm, coefs, legendre)


def table_kernel(cos_ref, sin_ref, step_cos_ref, step_sin_ref, out_ref):
    def body(i, carry):
        rows = pl.ds(pl.multiple_of(i * 16, 16), 16)
        c, s = cos_ref[rows, :], sin_ref[rows, :]
        step_c, step_s = step_cos_ref[rows, :], step_sin_ref[rows, :]
        for tile in range(HALF // 128):
            out_ref[rows, 128 * tile : 128 * tile + 128] = c.astype(BF16)
            if tile < HALF // 128 - 1:
                c, s = c * step_c - s * step_s, s * step_c + c * step_s
        return carry

    lax.fori_loop(0, out_ref.shape[0] // 16, body, 0)


def angle_tables(slot_pair):
    flipped = M - 1 - slot_pair
    odd = slot_pair % 2 == 1
    waves = jnp.stack([jnp.where(odd, flipped, slot_pair), jnp.where(odd, slot_pair, flipped)])
    factor = jnp.where(waves == 0, 1.0, 2.0).astype(F32)
    waves2 = jnp.broadcast_to(waves[..., None], waves.shape + (2,)).reshape(-1)
    factor2 = jnp.broadcast_to(factor[..., None], factor.shape + (2,)).reshape(-1)
    part = jnp.arange(waves2.shape[0], dtype=jnp.int32) % 2
    column = jnp.arange(128, dtype=jnp.int32)
    unit = 2.0 * math.pi / NLON
    turn = (waves2[:, None] * column[None, :] + (NLON // 4) * part[:, None]) % NLON
    angle = turn.astype(F32) * unit
    first_cos = factor2[:, None] * jnp.cos(angle)
    first_sin = factor2[:, None] * jnp.sin(angle)
    step = ((waves2 * 128) % NLON).astype(F32) * unit
    shape = (waves2.shape[0], 128)
    step_cos = jnp.broadcast_to(jnp.cos(step)[:, None], shape)
    step_sin = jnp.broadcast_to(jnp.sin(step)[:, None], shape)
    spec = pl.BlockSpec((256, 128), lambda i: (i, 0))
    table = pl.pallas_call(
        table_kernel,
        out_shape=jax.ShapeDtypeStruct((shape[0], HALF), BF16),
        grid=(shape[0] // 256,),
        in_specs=[spec] * 4,
        out_specs=pl.BlockSpec((256, HALF), lambda i: (i, 0)),
        cost_estimate=pl.CostEstimate(
            flops=6 * shape[0] * HALF, bytes_accessed=2 * shape[0] * HALF, transcendentals=0
        ),
        name="angle_tables",
    )(first_cos, first_sin, step_cos, step_sin)
    scale = 1.0 / (factor * math.sqrt(NLON))
    scale2 = jnp.broadcast_to(scale[:, None, :, None], (2, 8) + (scale.shape[1], 2))
    return table.reshape(2, shape[0] // 2, HALF), scale2.reshape(2, 8, -1)


def swap_blocks(tiles, lane):
    tiles = list(tiles)
    for d in (4, 2, 1):
        low = (lane // (16 * d)) % 2 == 0
        for i in range(8):
            if i & d:
                continue
            a, b = tiles[i], tiles[i + d]
            tiles[i] = jnp.where(low, a, pltpu.roll(b, 16 * d, 1))
            tiles[i + d] = jnp.where(low, pltpu.roll(a, 128 - 16 * d, 1), b)
    return tiles


def middle_kernel(
    sub, edge_ref, recv_ref, halo_ref, perm_ref, taps_ref, scale_ref, weight_ref,
    table_hbm, depart_hbm, pick_hbm,
    arrival_ref, coef_ref,
    table_ref, depart_ref, pick_ref, left_ref, plus_ref, minus_ref, grid_ref, shift_ref,
    stage_ref, code_ref, moved_ref, pair_ref, sums_ref, sems,
):
    copies = [
        pltpu.make_async_copy(table_hbm, table_ref, sems.at[0]),
        pltpu.make_async_copy(depart_hbm, depart_ref, sems.at[1]),
        pltpu.make_async_copy(pick_hbm, pick_ref, sems.at[2]),
    ]
    for copy in copies:
        copy.start()
    own = FIELDS * RUN * 16
    is_first, is_last = edge_ref[0], edge_ref[1]

    def gather_rows(tile, carry):
        lane = lax.broadcasted_iota(jnp.int32, (1, 128), 1)
        lanes = pl.ds(pl.multiple_of(tile * 128, 128), 128)
        height = RUN * SUB
        rows = pl.ds(pl.multiple_of(tile * 8 * height, 8 * height), 8 * height)
        mixed = jnp.dot(recv_ref[rows, :], perm_ref[...], preferred_element_type=F32)
        edge_rows = pl.ds(pl.multiple_of(tile * 64, 64), 64)
        edges = jnp.dot(halo_ref[edge_rows, :], perm_ref[...], preferred_element_type=F32)
        for par in range(2):
            cols = slice(128 * par, 128 * par + 128)
            tiles = swap_blocks([mixed[b * height : (b + 1) * height, cols] for b in range(8)], lane)
            for f in range(FIELDS):
                for k in range(RUN):
                    at = (f * RUN + k) * 16
                    block = [tiles[h * 4 + f][8 * k : 8 * k + 8] for h in range(2)]
                    left_ref[par, at : at + 16, lanes] = jnp.concatenate(block, axis=0).astype(BF16)
            ends = swap_blocks([edges[8 * b : 8 * b + 8, cols] for b in range(8)], lane)
            row = lax.broadcasted_iota(jnp.int32, (8, 128), 0)
            if par == 1:
                sign = jnp.where((row < RIM) & (is_first == 1), -1.0, 1.0)
                ends = [end * sign for end in ends]
            across = (row >= RIM) & (is_last == 1)
            for f in range(FIELDS):
                block = [jnp.where(across, ends[(1 - h) * 4 + f], ends[h * 4 + f]) for h in range(2)]
                at = own + f * 16
                left_ref[par, at : at + 16, lanes] = jnp.concatenate(block, axis=0).astype(BF16)
        return carry

    lax.fori_loop(0, TILES, gather_rows, 0)
    copies[0].wait()

    def to_grid(tile, carry):
        cols = pl.ds(pl.multiple_of(tile * 256, 256), 256)
        even = jnp.dot(left_ref[0], table_ref[0, :, cols], preferred_element_type=F32)
        odd = jnp.dot(left_ref[1], table_ref[1, :, cols], preferred_element_type=F32)
        plus_ref[...] = even + odd
        minus_ref[...] = even - odd
        place = lax.broadcasted_iota(jnp.int32, (8, 256), 0)
        for side, ref in enumerate((plus_ref, minus_ref)):
            to = pl.ds(pl.multiple_of(128 + side * HALF + tile * 256, 128), 256)
            for f in range(FIELDS):
                for k in range(RUN):
                    at = (f * RUN + k) * 16
                    grid_ref[f * REACH + RIM + k, :, to] = ref[at : at + 16, :].astype(BF16)
                for k in range(RIM):
                    before, after = [], []
                    for h in range(2):
                        end = own + f * 16 + 8 * h
                        at = (f * RUN + k + RUN - RIM) * 16 + 8 * h
                        rolled = pltpu.roll(ref[at : at + 8, :], 1, 0)
                        before.append(jnp.where(place == 0, ref[end + k : end + k + 1, :], rolled))
                        at = (f * RUN + k) * 16 + 8 * h
                        rolled = pltpu.roll(ref[at : at + 8, :], 7, 0)
                        end = end + RIM
                        after.append(
                            jnp.where(place == sub - 1, ref[end + k : end + k + 1, :], rolled)
                        )
                    grid_ref[f * REACH + k, :, to] = jnp.concatenate(before, 0).astype(BF16)
                    grid_ref[f * REACH + RIM + RUN + k, :, to] = jnp.concatenate(after, 0).astype(
                        BF16
                    )
        return carry

    lax.fori_loop(0, HALF // 256, to_grid, 0)
    grid_ref[:, :, 0:128] = grid_ref[:, :, NLON : NLON + 128]
    grid_ref[:, :, NLON + 128 : NLON + 256] = grid_ref[:, :, 128:256]
    copies[1].wait()
    copies[2].wait()

    def interpolate(tile, carry):
        lanes = pl.ds(pl.multiple_of(tile * 128, 128), 128)
        window = pl.ds(pl.multiple_of(tile * 128, 128), 384)
        for row in range(FIELDS * REACH):
            wide = grid_ref[row, :, window]
            for c in range(-RIM, RIM + 1):
                shift_ref[c + RIM, row] = wide[:, 128 + c : 256 + c]
        for h in range(2):
            code_ref[h] = pick_ref[h, :, lanes] * 16 + depart_ref[h, :, lanes]
        for k in range(RUN):
            index, column = [], []
            for h in range(2):
                code = code_ref[h, pl.ds(k, SUB, stride=RUN), :]
                index.append(code >> 2)
                column.append(code & 3)
            column = jnp.concatenate(column, axis=0).astype(F32).astype(BF16)
            hits = [column == jnp.asarray(d, BF16) for d in range(4)]
            totals = [jnp.zeros((16, 128), F32) for _ in range(FIELDS)]
            for r in range(7):
                weights = []
                for b in range(4):
                    entry = taps_ref[r * 4 + b]
                    found = [jnp.take_along_axis(entry, index[h], axis=1) for h in range(2)]
                    weights.append(jnp.concatenate(found, axis=0).astype(BF16))
                factors = []
                for c in range(-RIM, RIM + 1):
                    factor = jnp.zeros((16, 128), BF16)
                    for d in range(4):
                        b = c - (d - 2) + 1
                        if 0 <= b < 4:
                            factor = jnp.where(hits[d], weights[b], factor)
                    factors.append(factor)
                for f in range(FIELDS):
                    row = f * REACH + k + r
                    part = factors[0] * shift_ref[0, row]
                    for c in range(1, 7):
                        part = part + factors[c] * shift_ref[c, row]
                    totals[f] = totals[f] + part.astype(F32)
            for f in range(FIELDS):
                at = (f * RUN + k) * 16
                moved_ref[at : at + 16, lanes] = totals[f].astype(BF16)
                for h in range(2):
                    stage_ref[f * 2 + h, pl.ds(k, SUB, stride=RUN), :] = totals[f][
                        8 * h : 8 * h + 8
                    ]
        for f in range(FIELDS):
            for h in range(2):
                arrival_ref[f, h, :, lanes] = stage_ref[f * 2 + h].astype(BF16)
        return carry

    lax.fori_loop(0, BLOCKS, interpolate, 0)

    def fold(tile, carry):
        lanes = pl.ds(pl.multiple_of(tile * 128, 128), 128)
        other = pl.ds(pl.multiple_of(tile * 128 + HALF, 128), 128)
        a, b = moved_ref[:, lanes].astype(F32), moved_ref[:, other].astype(F32)
        pair_ref[0, :, lanes] = (a + b).astype(BF16)
        pair_ref[1, :, lanes] = (a - b).astype(BF16)
        return carry

    lax.fori_loop(0, HALF // 128, fold, 0)

    def to_waves(tile, carry):
        cols = pl.ds(pl.multiple_of(tile * 256, 256), 256)
        for par in range(2):
            out = dot_nt(pair_ref[par], table_ref[par, cols, :])
            out = out * scale_ref[par, 0:1, cols]
            for half in range(2):
                part = out[:, 128 * half : 128 * half + 128] * weight_ref[...]
                sums_ref[par, tile * 2 + half] = part
        return carry

    lax.fori_loop(0, TILES // 2, to_waves, 0)

    def scatter_rows(tile, carry):
        lane = lax.broadcasted_iota(jnp.int32, (1, 128), 1)
        height = RUN * SUB
        halves = []
        for par in range(2):
            tiles = []
            for h in range(2):
                for f in range(FIELDS):
                    pieces = []
                    for k in range(RUN):
                        at = (f * RUN + k) * 16 + 8 * h
                        pieces.append(sums_ref[par, tile, at : at + 8, :])
                    tiles.append(jnp.concatenate(pieces, axis=0))
            halves.append(jnp.concatenate(swap_blocks(tiles, lane), axis=0))
        rows = pl.ds(pl.multiple_of(tile * 8 * height, 8 * height), 8 * height)
        coef_ref[rows, :] = jnp.concatenate(halves, axis=1).astype(BF16)
        return carry

    lax.fori_loop(0, TILES, scatter_rows, 0)


def transport(sub, edge, recv, halo, perm, taps, scale, weight, table, depart, pick):
    rows, width = recv.shape
    lats = RUN * SUB
    left = FIELDS * (RUN + 1) * 16
    own = FIELDS * RUN * 16
    slots2 = table.shape[1]
    vmem = pl.BlockSpec(memory_space=pltpu.VMEM)
    anywhere = pl.BlockSpec(memory_space=pl.ANY)
    return pl.pallas_call(
        functools.partial(middle_kernel, sub),
        out_shape=(
            jax.ShapeDtypeStruct((FIELDS, 2, lats, NLON), BF16),
            jax.ShapeDtypeStruct((rows, width), BF16),
        ),
        in_specs=[pl.BlockSpec(memory_space=pltpu.SMEM)] + [vmem] * 6 + [anywhere] * 3,
        out_specs=(vmem, vmem),
        scratch_shapes=[
            pltpu.VMEM((2, slots2, HALF), BF16),
            pltpu.VMEM((2, lats, NLON), jnp.int32),
            pltpu.VMEM((2, lats, NLON), jnp.int32),
            pltpu.VMEM((2, left, slots2), BF16),
            pltpu.VMEM((left, 256), F32),
            pltpu.VMEM((left, 256), F32),
            pltpu.VMEM((FIELDS * REACH, 16, NLON + 256), BF16),
            pltpu.VMEM((7, FIELDS * REACH, 16, 128), BF16),
            pltpu.VMEM((FIELDS * 2, lats, 128), F32),
            pltpu.VMEM((2, lats, 128), jnp.int32),
            pltpu.VMEM((own, NLON), BF16),
            pltpu.VMEM((2, own, HALF), BF16),
            pltpu.VMEM((2, TILES, own, 128), F32),
            pltpu.SemaphoreType.DMA((3,)),
        ],
        compiler_params=pltpu.CompilerParams(vmem_limit_bytes=VMEM_LIMIT),
        cost_estimate=pl.CostEstimate(
            flops=8 * left * slots2 * HALF,
            bytes_accessed=2 * rows * width * 8 + 4 * slots2 * HALF,
            transcendentals=0,
        ),
        name="transport",
    )(edge, recv, halo, perm, taps, scale, weight, table, depart, pick)


def tap_tables(stencil_weight):
    zero = jnp.zeros((NSTEN,), F32)
    rows = []
    for r in range(-3, 4):
        for b in range(4):
            picks = []
            for dy in range(-2, 2):
                a = r - dy + 1
                picks.append(stencil_weight[:, 4 * a + b] if 0 <= a < 4 else zero)
            rows.append(jnp.stack(picks, axis=1).reshape(-1))
    table = jnp.stack(rows)
    table = jnp.concatenate([table, jnp.zeros_like(table)], axis=1)
    return jnp.broadcast_to(table[:, None, :], (28, 8, 128))


def exchange(array, axis, distance):
    devices = lax.axis_size(axis)
    return lax.ppermute(array, axis, [(i, i ^ distance) for i in range(devices)])


def gather_rows(spectral):
    devices = lax.axis_size("band")
    band = lax.axis_index("band")
    turned = spectral.transpose(0, 2, 1)
    pieces = [turned] + [exchange(turned, "band", d) for d in range(1, devices)]
    stacked = jnp.stack(pieces)
    ordered = [
        lax.dynamic_index_in_dim(stacked, band ^ b, 0, keepdims=False) for b in range(devices)
    ]
    return jnp.concatenate(ordered, axis=2)


def scatter_sums(sums, slots, row_local):
    devices = lax.axis_size("band")
    band = lax.axis_index("band")
    shaped = sums.reshape(slots, COLS, -1)
    parts = jnp.stack(
        [shaped[:, :, b * row_local : (b + 1) * row_local] for b in range(devices)]
    )
    total = lax.dynamic_index_in_dim(parts, band, 0, keepdims=False).astype(F32)
    for d in range(1, devices):
        piece = lax.dynamic_index_in_dim(parts, band ^ d, 0, keepdims=False)
        total = total + exchange(piece, "band", d).astype(F32)
    return total.astype(BF16).transpose(0, 2, 1)


def per_device(
    spectral, legendre, slot_pair, quad_weight, depart_code, stencil_pick, stencil_weight
):
    slots, row_local, _ = spectral.shape
    height = depart_code.shape[2]
    waves = lax.axis_size("wave")
    sub = height // RUN
    groups = slots // GROUP
    wave_rank = lax.axis_index("wave")
    lat_rank = lax.axis_index(("band", "wave"))
    lat_devices = lax.axis_size(("band", "wave"))
    my_pairs = lax.dynamic_slice_in_dim(slot_pair, wave_rank * slots, slots)
    perm = lane_order()

    spec = gather_rows(spectral)
    sent = legendre_forward(my_pairs, spec, legendre, waves)
    table, scale = angle_tables(slot_pair)
    taps = tap_tables(stencil_weight)
    recv = lax.all_to_all(sent, "wave", split_axis=0, concat_axis=0, tiled=True)

    blocks = waves * groups
    shaped = recv.reshape(blocks, RUN, sub, WIDE)
    first = shaped[:, :RIM, 0]
    last = shaped[:, RUN - RIM :, sub - 1]
    up = [(i, i + 1) for i in range(lat_devices - 1)]
    down = [(i + 1, i) for i in range(lat_devices - 1)]
    before = lax.ppermute(last, ("band", "wave"), up)
    after = lax.ppermute(first, ("band", "wave"), down)
    is_first, is_last = lat_rank == 0, lat_rank == lat_devices - 1
    halo = [jnp.where(is_first, first[:, RIM - 1 - i], before[:, i]) for i in range(RIM)]
    halo += [jnp.where(is_last, last[:, RIM - 1 - i], after[:, i]) for i in range(RIM)]
    halo += [jnp.zeros_like(halo[0])] * (8 - 2 * RIM)
    halo = jnp.stack(halo, axis=1).reshape(blocks * 8, WIDE)
    edge = jnp.stack([is_first, is_last]).astype(jnp.int32)

    depart, pick = depart_code[0], stencil_pick[0]
    my_weight = lax.dynamic_slice_in_dim(quad_weight, wave_rank * height, height)
    weight = my_weight.reshape(sub, RUN).T
    if sub != SUB:
        gap = SUB - sub
        shaped = jnp.pad(shaped, ((0, 0), (0, 0), (0, gap), (0, 0)))
        depart = jnp.pad(depart, ((0, 0), (0, RUN * gap), (0, 0)))
        pick = jnp.pad(pick, ((0, 0), (0, RUN * gap), (0, 0)))
        weight = jnp.pad(weight, ((0, 0), (0, gap)))
    weight = jnp.broadcast_to(weight[None, :, None, :, None], (FIELDS, RUN, 2, SUB, 128))
    arrival, coefs = transport(
        sub,
        edge,
        shaped.reshape(blocks * RUN * SUB, WIDE),
        halo,
        perm,
        taps,
        scale,
        weight.reshape(-1, 128),
        table,
        depart,
        pick,
    )
    arrival = arrival[None, :, :, :height]
    coefs = coefs.reshape(blocks, RUN, SUB, WIDE)[:, :, :sub].reshape(waves, groups, height, WIDE)
    by_wave = lax.all_to_all(coefs, "wave", split_axis=0, concat_axis=0, tiled=True)
    sums = legendre_backward(my_pairs, perm, by_wave, legendre)
    return (arrival, scatter_sums(sums, slots, row_local))


def solution(mesh):
    in_specs = (
        P("wave", "band", None),
        P("wave", "band", None),
        P(),
        P("band"),
        P(None, None, ("band", "wave"), None),
        P(None, None, ("band", "wave"), None),
        P(),
    )
    out_specs = (P(None, None, None, ("band", "wave"), None), P("wave", "band", None))
    return jax.shard_map(
        per_device, mesh=mesh, in_specs=in_specs, out_specs=out_specs, check_vma=False
    )
```

```python
import functools
import math

import jax
import jax.numpy as jnp
import numpy as np
from jax import lax
from jax.experimental import pallas as pl
from jax.experimental.pallas import tpu as pltpu
from jax.sharding import PartitionSpec as P

M = 1280
NLON = 5120
HALF = NLON // 2
FIELDS = 4
NSTEN = 16
RIM = 3
COLS = 8
GROUP = 8
WIDE = GROUP * 4 * COLS
RUN = 5
SUB = 8
REACH = RUN + 2 * RIM
BLOCKS = NLON // 128
TILES = 10
F32 = jnp.float32
BF16 = jnp.bfloat16
VMEM_LIMIT = 60 * 2**20


def dot_nt(left, right):
    return lax.dot_general(left, right, (((1,), (1,)), ((), ())), preferred_element_type=F32)


def lane_order():
    index = np.arange(WIDE).reshape(GROUP, 2, 2, FIELDS, 2).transpose(1, 2, 3, 0, 4).reshape(-1)
    matrix = np.zeros((WIDE, WIDE), np.float32)
    matrix[index, np.arange(WIDE)] = 1.0
    return jnp.asarray(matrix, BF16)


def row_masks(pair, rows):
    row = lax.broadcasted_iota(jnp.int32, (1, rows), 1)
    low_count = M - pair
    higher = row >= low_count
    degree = jnp.where(higher, row - low_count, row)
    sign = (1 - 2 * (degree & 1)).astype(F32)
    in_use = row <= M
    side = jnp.where(higher, 1, 0) ^ (pair & 1)
    even = jnp.where(in_use & (side == 0), 1.0, 0.0)
    odd = jnp.where(in_use & (side == 1), 1.0, 0.0)
    return even, odd, sign


def forward_kernel(height, base, pair_ref, spec_ref, leg_ref, out_ref, acc_ref):
    group = pl.program_id(0) + base
    rows = spec_ref.shape[2]
    sub = height // RUN

    pieces = []
    for u in range(GROUP):
        even, odd, sign = row_masks(pair_ref[group * GROUP + u], rows)
        spec = spec_ref[u].astype(F32)
        south = spec * sign
        parts = [spec * even, south * even, spec * odd, south * odd]
        masked = jnp.concatenate(parts, axis=0).astype(BF16)
        pieces.append(dot_nt(leg_ref[u], masked))
        if u % 4 == 3:
            acc_ref[u // 4] = jnp.concatenate(pieces[-4:], axis=1)
    for dest in range(out_ref.shape[0]):
        halves = []
        for half in range(2):
            pieces = [
                acc_ref[half, pl.ds(dest * height + k, sub, stride=RUN), :] for k in range(RUN)
            ]
            halves.append(jnp.concatenate(pieces, axis=0))
        out_ref[dest, 0] = jnp.concatenate(halves, axis=1).astype(BF16)


def legendre_forward(pairs, spec, legendre, waves, part, parts):
    slots, lats, rows = legendre.shape
    groups = slots // GROUP // parts
    base = part * groups
    height = lats // waves
    return pl.pallas_call(
        functools.partial(forward_kernel, height, base),
        out_shape=jax.ShapeDtypeStruct((waves, groups, height, WIDE), BF16),
        grid=(groups,),
        in_specs=[
            pl.BlockSpec(memory_space=pltpu.SMEM),
            pl.BlockSpec((GROUP, COLS, rows), lambda g: (g + base, 0, 0)),
            pl.BlockSpec((GROUP, lats, rows), lambda g: (g + base, 0, 0)),
        ],
        out_specs=pl.BlockSpec((waves, 1, height, WIDE), lambda g: (0, g, 0, 0)),
        scratch_shapes=[pltpu.VMEM((2, lats, 128), F32)],
        compiler_params=pltpu.CompilerParams(vmem_limit_bytes=VMEM_LIMIT),
        cost_estimate=pl.CostEstimate(
            flops=2 * groups * GROUP * lats * rows * 32,
            bytes_accessed=2 * groups * GROUP * lats * rows,
            transcendentals=0,
        ),
        name="legendre_forward",
    )(pairs, spec, legendre)


def backward_kernel(height, base, pair_ref, perm_ref, coef_ref, leg_ref, out_ref, rows_ref):
    group = pl.program_id(0) + base
    rows = leg_ref.shape[2]
    sub = height // RUN
    for source in range(coef_ref.shape[0]):
        block = coef_ref[source, 0].astype(F32)
        for k in range(RUN):
            for half in range(2):
                rows_ref[half, pl.ds(source * height + k, sub, stride=RUN), :] = block[
                    k * sub : (k + 1) * sub, 128 * half : 128 * half + 128
                ]
    natural = jnp.concatenate([rows_ref[0], rows_ref[1]], axis=1).astype(BF16)
    turned = dot_nt(perm_ref[...], natural).astype(BF16)
    sums = []
    for u in range(GROUP):
        even, odd, sign = row_masks(pair_ref[group * GROUP + u], rows)
        raw = jnp.dot(turned[32 * u : 32 * u + 32], leg_ref[u], preferred_element_type=F32)
        low = raw[0:8] + sign * raw[8:16]
        high = raw[16:24] + sign * raw[24:32]
        sums.append(low * even + high * odd)
        if u % 2 == 1:
            out_ref[8 * (u - 1) : 8 * (u + 1), :] = jnp.concatenate(sums[-2:], axis=0).astype(BF16)


def legendre_backward(pairs, perm, coefs, legendre, part):
    _, lats, rows = legendre.shape
    waves, groups, height, _ = coefs.shape
    slots = groups * GROUP
    base = part * groups
    return pl.pallas_call(
        functools.partial(backward_kernel, height, base),
        out_shape=jax.ShapeDtypeStruct((slots * COLS, rows), BF16),
        grid=(groups,),
        in_specs=[
            pl.BlockSpec(memory_space=pltpu.SMEM),
            pl.BlockSpec((WIDE, WIDE), lambda g: (0, 0)),
            pl.BlockSpec((waves, 1, height, WIDE), lambda g: (0, g, 0, 0)),
            pl.BlockSpec((GROUP, lats, rows), lambda g: (g + base, 0, 0)),
        ],
        out_specs=pl.BlockSpec((GROUP * COLS, rows), lambda g: (g, 0)),
        scratch_shapes=[pltpu.VMEM((2, lats, 128), F32)],
        compiler_params=pltpu.CompilerParams(vmem_limit_bytes=VMEM_LIMIT),
        cost_estimate=pl.CostEstimate(
            flops=2 * slots * lats * rows * 32,
            bytes_accessed=2 * slots * lats * rows,
            transcendentals=0,
        ),
        name="legendre_backward",
    )(pairs, perm, coefs, legendre)


def table_kernel(cos_ref, sin_ref, step_cos_ref, step_sin_ref, out_ref):
    def body(i, carry):
        rows = pl.ds(pl.multiple_of(i * 16, 16), 16)
        c, s = cos_ref[rows, :], sin_ref[rows, :]
        step_c, step_s = step_cos_ref[rows, :], step_sin_ref[rows, :]
        for tile in range(HALF // 128):
            out_ref[rows, 128 * tile : 128 * tile + 128] = c.astype(BF16)
            if tile < HALF // 128 - 1:
                c, s = c * step_c - s * step_s, s * step_c + c * step_s
        return carry

    lax.fori_loop(0, out_ref.shape[0] // 16, body, 0)


def angle_tables(slot_pair):
    flipped = M - 1 - slot_pair
    odd = slot_pair % 2 == 1
    waves = jnp.stack([jnp.where(odd, flipped, slot_pair), jnp.where(odd, slot_pair, flipped)])
    factor = jnp.where(waves == 0, 1.0, 2.0).astype(F32)
    waves2 = jnp.broadcast_to(waves[..., None], waves.shape + (2,)).reshape(-1)
    factor2 = jnp.broadcast_to(factor[..., None], factor.shape + (2,)).reshape(-1)
    part = jnp.arange(waves2.shape[0], dtype=jnp.int32) % 2
    column = jnp.arange(128, dtype=jnp.int32)
    unit = 2.0 * math.pi / NLON
    turn = (waves2[:, None] * column[None, :] + (NLON // 4) * part[:, None]) % NLON
    angle = turn.astype(F32) * unit
    first_cos = factor2[:, None] * jnp.cos(angle)
    first_sin = factor2[:, None] * jnp.sin(angle)
    step = ((waves2 * 128) % NLON).astype(F32) * unit
    shape = (waves2.shape[0], 128)
    step_cos = jnp.broadcast_to(jnp.cos(step)[:, None], shape)
    step_sin = jnp.broadcast_to(jnp.sin(step)[:, None], shape)
    spec = pl.BlockSpec((256, 128), lambda i: (i, 0))
    table = pl.pallas_call(
        table_kernel,
        out_shape=jax.ShapeDtypeStruct((shape[0], HALF), BF16),
        grid=(shape[0] // 256,),
        in_specs=[spec] * 4,
        out_specs=pl.BlockSpec((256, HALF), lambda i: (i, 0)),
        cost_estimate=pl.CostEstimate(
            flops=6 * shape[0] * HALF, bytes_accessed=2 * shape[0] * HALF, transcendentals=0
        ),
        name="angle_tables",
    )(first_cos, first_sin, step_cos, step_sin)
    scale = 1.0 / (factor * math.sqrt(NLON))
    scale2 = jnp.broadcast_to(scale[:, None, :, None], (2, 8) + (scale.shape[1], 2))
    return table.reshape(2, shape[0] // 2, HALF), scale2.reshape(2, 8, -1)


def swap_blocks(tiles, lane):
    tiles = list(tiles)
    for d in (4, 2, 1):
        low = (lane // (16 * d)) % 2 == 0
        for i in range(8):
            if i & d:
                continue
            a, b = tiles[i], tiles[i + d]
            tiles[i] = jnp.where(low, a, pltpu.roll(b, 16 * d, 1))
            tiles[i + d] = jnp.where(low, pltpu.roll(a, 128 - 16 * d, 1), b)
    return tiles


def middle_kernel(
    sub, parts, edge_ref, halo_ref, perm_ref, taps_ref, scale_ref, weight_ref,
    table_hbm, depart_hbm, pick_hbm, *refs,
):
    recv_refs, arrival_ref, coef_refs = refs[:parts], refs[parts], refs[parts + 1 : 2 * parts + 1]
    (
    table_ref, depart_ref, pick_ref, left_ref, plus_ref, minus_ref, grid_ref, shift_ref,
    stage_ref, code_ref, moved_ref, pair_ref, sums_ref, sems,
    ) = refs[2 * parts + 1 :]
    per_part = TILES // parts
    copies = [
        pltpu.make_async_copy(table_hbm, table_ref, sems.at[0]),
        pltpu.make_async_copy(depart_hbm, depart_ref, sems.at[1]),
        pltpu.make_async_copy(pick_hbm, pick_ref, sems.at[2]),
    ]
    for copy in copies:
        copy.start()
    own = FIELDS * RUN * 16
    is_first, is_last = edge_ref[0], edge_ref[1]

    def gather_rows(part, step, carry):
        tile = part * per_part + step
        lane = lax.broadcasted_iota(jnp.int32, (1, 128), 1)
        lanes = pl.ds(pl.multiple_of(tile * 128, 128), 128)
        height = RUN * SUB
        rows = pl.ds(pl.multiple_of(step * 8 * height, 8 * height), 8 * height)
        mixed = jnp.dot(recv_refs[part][rows, :], perm_ref[...], preferred_element_type=F32)
        edge_rows = pl.ds(pl.multiple_of(tile * 64, 64), 64)
        edges = jnp.dot(halo_ref[edge_rows, :], perm_ref[...], preferred_element_type=F32)
        for par in range(2):
            cols = slice(128 * par, 128 * par + 128)
            tiles = swap_blocks([mixed[b * height : (b + 1) * height, cols] for b in range(8)], lane)
            for f in range(FIELDS):
                for k in range(RUN):
                    at = (f * RUN + k) * 16
                    block = [tiles[h * 4 + f][8 * k : 8 * k + 8] for h in range(2)]
                    left_ref[par, at : at + 16, lanes] = jnp.concatenate(block, axis=0).astype(BF16)
            ends = swap_blocks([edges[8 * b : 8 * b + 8, cols] for b in range(8)], lane)
            row = lax.broadcasted_iota(jnp.int32, (8, 128), 0)
            if par == 1:
                sign = jnp.where((row < RIM) & (is_first == 1), -1.0, 1.0)
                ends = [end * sign for end in ends]
            across = (row >= RIM) & (is_last == 1)
            for f in range(FIELDS):
                block = [jnp.where(across, ends[(1 - h) * 4 + f], ends[h * 4 + f]) for h in range(2)]
                at = own + f * 16
                left_ref[par, at : at + 16, lanes] = jnp.concatenate(block, axis=0).astype(BF16)
        return carry

    for part in range(parts):
        lax.fori_loop(0, per_part, functools.partial(gather_rows, part), 0)
    copies[0].wait()

    def to_grid(tile, carry):
        cols = pl.ds(pl.multiple_of(tile * 256, 256), 256)
        even = jnp.dot(left_ref[0], table_ref[0, :, cols], preferred_element_type=F32)
        odd = jnp.dot(left_ref[1], table_ref[1, :, cols], preferred_element_type=F32)
        plus_ref[...] = even + odd
        minus_ref[...] = even - odd
        place = lax.broadcasted_iota(jnp.int32, (8, 256), 0)
        for side, ref in enumerate((plus_ref, minus_ref)):
            to = pl.ds(pl.multiple_of(128 + side * HALF + tile * 256, 128), 256)
            for f in range(FIELDS):
                for k in range(RUN):
                    at = (f * RUN + k) * 16
                    grid_ref[f * REACH + RIM + k, :, to] = ref[at : at + 16, :].astype(BF16)
                for k in range(RIM):
                    before, after = [], []
                    for h in range(2):
                        end = own + f * 16 + 8 * h
                        at = (f * RUN + k + RUN - RIM) * 16 + 8 * h
                        rolled = pltpu.roll(ref[at : at + 8, :], 1, 0)
                        before.append(jnp.where(place == 0, ref[end + k : end + k + 1, :], rolled))
                        at = (f * RUN + k) * 16 + 8 * h
                        rolled = pltpu.roll(ref[at : at + 8, :], 7, 0)
                        end = end + RIM
                        after.append(
                            jnp.where(place == sub - 1, ref[end + k : end + k + 1, :], rolled)
                        )
                    grid_ref[f * REACH + k, :, to] = jnp.concatenate(before, 0).astype(BF16)
                    grid_ref[f * REACH + RIM + RUN + k, :, to] = jnp.concatenate(after, 0).astype(
                        BF16
                    )
        return carry

    lax.fori_loop(0, HALF // 256, to_grid, 0)
    grid_ref[:, :, 0:128] = grid_ref[:, :, NLON : NLON + 128]
    grid_ref[:, :, NLON + 128 : NLON + 256] = grid_ref[:, :, 128:256]
    copies[1].wait()
    copies[2].wait()

    def interpolate(tile, carry):
        lanes = pl.ds(pl.multiple_of(tile * 128, 128), 128)
        window = pl.ds(pl.multiple_of(tile * 128, 128), 384)
        for row in range(FIELDS * REACH):
            wide = grid_ref[row, :, window]
            for c in range(-RIM, RIM + 1):
                shift_ref[c + RIM, row] = wide[:, 128 + c : 256 + c]
        for h in range(2):
            code_ref[h] = pick_ref[h, :, lanes] * 16 + depart_ref[h, :, lanes]
        for k in range(RUN):
            index, column = [], []
            for h in range(2):
                code = code_ref[h, pl.ds(k, SUB, stride=RUN), :]
                index.append(code >> 2)
                column.append(code & 3)
            column = jnp.concatenate(column, axis=0).astype(F32).astype(BF16)
            hits = [column == jnp.asarray(d, BF16) for d in range(4)]
            totals = [jnp.zeros((16, 128), F32) for _ in range(FIELDS)]
            for r in range(7):
                weights = []
                for b in range(4):
                    entry = taps_ref[r * 4 + b]
                    found = [jnp.take_along_axis(entry, index[h], axis=1) for h in range(2)]
                    weights.append(jnp.concatenate(found, axis=0).astype(BF16))
                factors = []
                for c in range(-RIM, RIM + 1):
                    factor = jnp.zeros((16, 128), BF16)
                    for d in range(4):
                        b = c - (d - 2) + 1
                        if 0 <= b < 4:
                            factor = jnp.where(hits[d], weights[b], factor)
                    factors.append(factor)
                for f in range(FIELDS):
                    row = f * REACH + k + r
                    part = factors[0] * shift_ref[0, row]
                    for c in range(1, 7):
                        part = part + factors[c] * shift_ref[c, row]
                    totals[f] = totals[f] + part.astype(F32)
            for f in range(FIELDS):
                at = (f * RUN + k) * 16
                moved_ref[at : at + 16, lanes] = totals[f].astype(BF16)
                for h in range(2):
                    stage_ref[f * 2 + h, pl.ds(k, SUB, stride=RUN), :] = totals[f][
                        8 * h : 8 * h + 8
                    ]
        for f in range(FIELDS):
            for h in range(2):
                arrival_ref[f, h, :, lanes] = stage_ref[f * 2 + h].astype(BF16)
        return carry

    lax.fori_loop(0, BLOCKS, interpolate, 0)

    def fold(tile, carry):
        lanes = pl.ds(pl.multiple_of(tile * 128, 128), 128)
        other = pl.ds(pl.multiple_of(tile * 128 + HALF, 128), 128)
        a, b = moved_ref[:, lanes].astype(F32), moved_ref[:, other].astype(F32)
        pair_ref[0, :, lanes] = (a + b).astype(BF16)
        pair_ref[1, :, lanes] = (a - b).astype(BF16)
        return carry

    lax.fori_loop(0, HALF // 128, fold, 0)

    def to_waves(tile, carry):
        cols = pl.ds(pl.multiple_of(tile * 256, 256), 256)
        for par in range(2):
            out = dot_nt(pair_ref[par], table_ref[par, cols, :])
            out = out * scale_ref[par, 0:1, cols]
            for half in range(2):
                part = out[:, 128 * half : 128 * half + 128] * weight_ref[...]
                sums_ref[par, tile * 2 + half] = part
        return carry

    lax.fori_loop(0, TILES // 2, to_waves, 0)

    def scatter_rows(part, step, carry):
        tile = part * per_part + step
        lane = lax.broadcasted_iota(jnp.int32, (1, 128), 1)
        height = RUN * SUB
        halves = []
        for par in range(2):
            tiles = []
            for h in range(2):
                for f in range(FIELDS):
                    pieces = []
                    for k in range(RUN):
                        at = (f * RUN + k) * 16 + 8 * h
                        pieces.append(sums_ref[par, tile, at : at + 8, :])
                    tiles.append(jnp.concatenate(pieces, axis=0))
            halves.append(jnp.concatenate(swap_blocks(tiles, lane), axis=0))
        rows = pl.ds(pl.multiple_of(step * 8 * height, 8 * height), 8 * height)
        coef_refs[part][rows, :] = jnp.concatenate(halves, axis=1).astype(BF16)
        return carry

    for part in range(parts):
        lax.fori_loop(0, per_part, functools.partial(scatter_rows, part), 0)


def transport(sub, edge, recv, halo, perm, taps, scale, weight, table, depart, pick):
    parts = len(recv)
    rows, width = recv[0].shape
    lats = RUN * SUB
    left = FIELDS * (RUN + 1) * 16
    own = FIELDS * RUN * 16
    slots2 = table.shape[1]
    vmem = pl.BlockSpec(memory_space=pltpu.VMEM)
    anywhere = pl.BlockSpec(memory_space=pl.ANY)
    return pl.pallas_call(
        functools.partial(middle_kernel, sub, parts),
        out_shape=(
            jax.ShapeDtypeStruct((FIELDS, 2, lats, NLON), BF16),
            *[jax.ShapeDtypeStruct((rows, width), BF16)] * parts,
        ),
        in_specs=[pl.BlockSpec(memory_space=pltpu.SMEM)] + [vmem] * 5 + [anywhere] * 3 + [vmem] * parts,
        out_specs=(vmem,) * (parts + 1),
        scratch_shapes=[
            pltpu.VMEM((2, slots2, HALF), BF16),
            pltpu.VMEM((2, lats, NLON), jnp.int32),
            pltpu.VMEM((2, lats, NLON), jnp.int32),
            pltpu.VMEM((2, left, slots2), BF16),
            pltpu.VMEM((left, 256), F32),
            pltpu.VMEM((left, 256), F32),
            pltpu.VMEM((FIELDS * REACH, 16, NLON + 256), BF16),
            pltpu.VMEM((7, FIELDS * REACH, 16, 128), BF16),
            pltpu.VMEM((FIELDS * 2, lats, 128), F32),
            pltpu.VMEM((2, lats, 128), jnp.int32),
            pltpu.VMEM((own, NLON), BF16),
            pltpu.VMEM((2, own, HALF), BF16),
            pltpu.VMEM((2, TILES, own, 128), F32),
            pltpu.SemaphoreType.DMA((3,)),
        ],
        compiler_params=pltpu.CompilerParams(vmem_limit_bytes=VMEM_LIMIT),
        cost_estimate=pl.CostEstimate(
            flops=8 * left * slots2 * HALF,
            bytes_accessed=2 * rows * width * 8 + 4 * slots2 * HALF,
            transcendentals=0,
        ),
        name="transport",
    )(edge, halo, perm, taps, scale, weight, table, depart, pick, *recv)


def tap_tables(stencil_weight):
    zero = jnp.zeros((NSTEN,), F32)
    rows = []
    for r in range(-3, 4):
        for b in range(4):
            picks = []
            for dy in range(-2, 2):
                a = r - dy + 1
                picks.append(stencil_weight[:, 4 * a + b] if 0 <= a < 4 else zero)
            rows.append(jnp.stack(picks, axis=1).reshape(-1))
    table = jnp.stack(rows)
    table = jnp.concatenate([table, jnp.zeros_like(table)], axis=1)
    return jnp.broadcast_to(table[:, None, :], (28, 8, 128))


def exchange(array, axis, distance):
    devices = lax.axis_size(axis)
    return lax.ppermute(array, axis, [(i, i ^ distance) for i in range(devices)])


def gather_rows(spectral):
    devices = lax.axis_size("band")
    band = lax.axis_index("band")
    turned = spectral.transpose(0, 2, 1)
    pieces = [turned] + [exchange(turned, "band", d) for d in range(1, devices)]
    stacked = jnp.stack(pieces)
    ordered = [
        lax.dynamic_index_in_dim(stacked, band ^ b, 0, keepdims=False) for b in range(devices)
    ]
    return jnp.concatenate(ordered, axis=2)


def scatter_sums(sums, slots, row_local):
    devices = lax.axis_size("band")
    band = lax.axis_index("band")
    shaped = sums.reshape(slots, COLS, -1)
    parts = jnp.stack(
        [shaped[:, :, b * row_local : (b + 1) * row_local] for b in range(devices)]
    )
    total = lax.dynamic_index_in_dim(parts, band, 0, keepdims=False).astype(F32)
    for d in range(1, devices):
        piece = lax.dynamic_index_in_dim(parts, band ^ d, 0, keepdims=False)
        total = total + exchange(piece, "band", d).astype(F32)
    return total.astype(BF16).transpose(0, 2, 1)


def per_device(
    spectral, legendre, slot_pair, quad_weight, depart_code, stencil_pick, stencil_weight
):
    slots, row_local, _ = spectral.shape
    height = depart_code.shape[2]
    waves = lax.axis_size("wave")
    sub = height // RUN
    groups = slots // GROUP
    wave_rank = lax.axis_index("wave")
    lat_rank = lax.axis_index(("band", "wave"))
    lat_devices = lax.axis_size(("band", "wave"))
    my_pairs = lax.dynamic_slice_in_dim(slot_pair, wave_rank * slots, slots)
    perm = lane_order()

    parts = 2 if groups % 2 == 0 else 1
    blocks = waves * groups
    arriving = slot_pair.reshape(waves, parts, -1).swapaxes(0, 1).reshape(-1)

    spec = gather_rows(spectral)
    table, scale = angle_tables(arriving)
    taps = tap_tables(stencil_weight)
    my_weight = lax.dynamic_slice_in_dim(quad_weight, wave_rank * height, height)
    weight = my_weight.reshape(sub, RUN).T
    if sub != SUB:
        weight = jnp.pad(weight, ((0, 0), (0, SUB - sub)))
    weight = jnp.broadcast_to(weight[None, :, None, :, None], (FIELDS, RUN, 2, SUB, 128))
    weight = weight.reshape(-1, 128)
    is_first, is_last = lat_rank == 0, lat_rank == lat_devices - 1
    edge = jnp.stack([is_first, is_last]).astype(jnp.int32)
    spec, table, scale, taps, weight, edge, my_pairs = lax.optimization_barrier(
        (spec, table, scale, taps, weight, edge, my_pairs)
    )
    received = []
    for part in range(parts):
        sent = legendre_forward(my_pairs, spec, legendre, waves, part, parts)
        if received:
            sent, received[-1] = lax.optimization_barrier((sent, received[-1]))
        received.append(
            lax.all_to_all(sent, "wave", split_axis=0, concat_axis=0, tiled=True)
        )
    recv = [r.reshape(-1, height, WIDE) for r in received]
    first = jnp.concatenate([r[:, 0 : RIM * sub : sub] for r in recv])
    last = jnp.concatenate([r[:, (RUN - RIM + 1) * sub - 1 :: sub] for r in recv])
    up = [(i, i + 1) for i in range(lat_devices - 1)]
    down = [(i + 1, i) for i in range(lat_devices - 1)]
    before = lax.ppermute(last, ("band", "wave"), up)
    after = lax.ppermute(first, ("band", "wave"), down)
    halo = [jnp.where(is_first, first[:, RIM - 1 - i], before[:, i]) for i in range(RIM)]
    halo += [jnp.where(is_last, last[:, RIM - 1 - i], after[:, i]) for i in range(RIM)]
    halo += [jnp.zeros_like(halo[0])] * (8 - 2 * RIM)
    halo = jnp.stack(halo, axis=1).reshape(blocks * 8, WIDE)

    depart, pick = depart_code[0], stencil_pick[0]
    if sub != SUB:
        gap = SUB - sub
        recv = [r.reshape(-1, RUN, sub, WIDE) for r in recv]
        recv = [jnp.pad(r, ((0, 0), (0, 0), (0, gap), (0, 0))) for r in recv]
        depart = jnp.pad(depart, ((0, 0), (0, RUN * gap), (0, 0)))
        pick = jnp.pad(pick, ((0, 0), (0, RUN * gap), (0, 0)))
    arrival, *coefs = transport(
        sub,
        edge,
        [r.reshape(-1, WIDE) for r in recv],
        halo,
        perm,
        taps,
        scale,
        weight,
        table,
        depart,
        pick,
    )
    arrival = arrival[None, :, :, :height]
    coefs = [c.reshape(-1, RUN, SUB, WIDE)[:, :, :sub] for c in coefs]
    outs, by_wave = [], None
    for part in range(parts):
        leaving = coefs[part].reshape(waves, groups // parts, height, WIDE)
        if part:
            leaving, by_wave = lax.optimization_barrier((leaving, by_wave))
        ready = by_wave
        by_wave = lax.all_to_all(leaving, "wave", split_axis=0, concat_axis=0, tiled=True)
        if part:
            outs.append(legendre_backward(my_pairs, perm, ready, legendre, part - 1))
    outs.append(legendre_backward(my_pairs, perm, by_wave, legendre, parts - 1))
    outs = [scatter_sums(sums, slots // parts, row_local) for sums in outs]
    return (arrival, jnp.concatenate(outs))


def solution(mesh):
    in_specs = (
        P("wave", "band", None),
        P("wave", "band", None),
        P(),
        P("band"),
        P(None, None, ("band", "wave"), None),
        P(None, None, ("band", "wave"), None),
        P(),
    )
    out_specs = (P(None, None, None, ("band", "wave"), None), P("wave", "band", None))
    return jax.shard_map(
        per_device, mesh=mesh, in_specs=in_specs, out_specs=out_specs, check_vma=False
    )
```

```python
import functools
import math

import jax
import jax.numpy as jnp
import numpy as np
from jax import lax
from jax.experimental import pallas as pl
from jax.experimental.pallas import tpu as pltpu
from jax.sharding import PartitionSpec as P

M = 1280
NLON = 5120
HALF = NLON // 2
FIELDS = 4
NSTEN = 16
RIM = 3
COLS = 8
GROUP = 8
WIDE = GROUP * 4 * COLS
RUN = 5
SUB = 8
REACH = RUN + 2 * RIM
TILES = 10
CHUNK = 512
FINE = CHUNK // 128
CHUNKS = NLON // CHUNK
STEP = 4
F32 = jnp.float32
BF16 = jnp.bfloat16
VMEM_LIMIT = 60 * 2**20


def dot_nt(left, right):
    return lax.dot_general(left, right, (((1,), (1,)), ((), ())), preferred_element_type=F32)


def lane_order():
    index = np.arange(WIDE).reshape(GROUP, 2, 2, FIELDS, 2).transpose(1, 2, 3, 4, 0).reshape(-1)
    matrix = np.zeros((WIDE, WIDE), np.float32)
    matrix[index, np.arange(WIDE)] = 1.0
    return jnp.asarray(matrix, BF16)


def longitude_order():
    position = np.arange(CHUNK)
    longitude = FINE * (position % 128) + position // 128
    matrix = np.zeros((CHUNK, CHUNK), np.float32)
    matrix[longitude, position] = 1.0
    return jnp.asarray(np.stack([matrix, matrix.T]), BF16)


def row_masks(pair, rows):
    row = lax.broadcasted_iota(jnp.int32, (1, rows), 1)
    low_count = M - pair
    higher = row >= low_count
    degree = jnp.where(higher, row - low_count, row)
    sign = (1 - 2 * (degree & 1)).astype(F32)
    in_use = row <= M
    side = jnp.where(higher, 1, 0) ^ (pair & 1)
    even = jnp.where(in_use & (side == 0), 1.0, 0.0)
    odd = jnp.where(in_use & (side == 1), 1.0, 0.0)
    return even, odd, sign


def forward_kernel(height, base, pair_ref, spec_ref, leg_ref, out_ref, acc_ref):
    group, step = pl.program_id(0) + base, pl.program_id(1)
    rows = spec_ref.shape[2]
    sub = height // RUN

    pieces = []
    for u in range(STEP):
        even, odd, sign = row_masks(pair_ref[group * GROUP + step * STEP + u], rows)
        spec = spec_ref[u].astype(F32)
        south = spec * sign
        parts = [spec * even, south * even, spec * odd, south * odd]
        masked = jnp.concatenate(parts, axis=0).astype(BF16)
        pieces.append(dot_nt(leg_ref[u], masked))
    acc_ref[step] = jnp.concatenate(pieces, axis=1)

    @pl.when(step == GROUP // STEP - 1)
    def _():
        for dest in range(out_ref.shape[0]):
            halves = []
            for half in range(2):
                pieces = [
                    acc_ref[half, pl.ds(dest * height + k, sub, stride=RUN), :]
                    for k in range(RUN)
                ]
                halves.append(jnp.concatenate(pieces, axis=0))
            out_ref[dest, 0] = jnp.concatenate(halves, axis=1).astype(BF16)


def legendre_forward(pairs, spec, legendre, waves, part, parts):
    slots, lats, rows = legendre.shape
    groups = slots // GROUP // parts
    base = part * groups
    height = lats // waves
    return pl.pallas_call(
        functools.partial(forward_kernel, height, base),
        out_shape=jax.ShapeDtypeStruct((waves, groups, height, WIDE), BF16),
        grid=(groups, GROUP // STEP),
        in_specs=[
            pl.BlockSpec(memory_space=pltpu.SMEM),
            pl.BlockSpec((STEP, COLS, rows), lambda g, t: (2 * (g + base) + t, 0, 0)),
            pl.BlockSpec((STEP, lats, rows), lambda g, t: (2 * (g + base) + t, 0, 0)),
        ],
        out_specs=pl.BlockSpec((waves, 1, height, WIDE), lambda g, t: (0, g, 0, 0)),
        scratch_shapes=[pltpu.VMEM((2, lats, 128), F32)],
        compiler_params=pltpu.CompilerParams(vmem_limit_bytes=VMEM_LIMIT),
        cost_estimate=pl.CostEstimate(
            flops=2 * groups * GROUP * lats * rows * 32,
            bytes_accessed=2 * groups * GROUP * lats * rows,
            transcendentals=0,
        ),
        name="legendre_forward",
    )(pairs, spec, legendre)


def backward_kernel(
    height, base, pair_ref, perm_ref, coef_ref, leg_ref, out_ref, rows_ref, turned_ref
):
    group, step = pl.program_id(0) + base, pl.program_id(1)
    rows = leg_ref.shape[2]
    sub = height // RUN

    @pl.when(step == 0)
    def _():
        for source in range(coef_ref.shape[0]):
            block = coef_ref[source, 0].astype(F32)
            for k in range(RUN):
                for half in range(2):
                    rows_ref[half, pl.ds(source * height + k, sub, stride=RUN), :] = block[
                        k * sub : (k + 1) * sub, 128 * half : 128 * half + 128
                    ]
        natural = jnp.concatenate([rows_ref[0], rows_ref[1]], axis=1).astype(BF16)
        turned_ref[...] = dot_nt(perm_ref[...], natural).astype(BF16)

    sums = []
    for u in range(STEP):
        even, odd, sign = row_masks(pair_ref[group * GROUP + step * STEP + u], rows)
        at = pl.ds(pl.multiple_of(step * (32 * STEP) + 32 * u, 32), 32)
        raw = jnp.dot(turned_ref[at, :], leg_ref[u], preferred_element_type=F32)
        low = raw[0:8] + sign * raw[8:16]
        high = raw[16:24] + sign * raw[24:32]
        sums.append(low * even + high * odd)
    out_ref[...] = jnp.concatenate(sums, axis=0).astype(BF16)


def legendre_backward(pairs, perm, coefs, legendre, part):
    _, lats, rows = legendre.shape
    waves, groups, height, _ = coefs.shape
    slots = groups * GROUP
    base = part * groups
    return pl.pallas_call(
        functools.partial(backward_kernel, height, base),
        out_shape=jax.ShapeDtypeStruct((slots * COLS, rows), BF16),
        grid=(groups, GROUP // STEP),
        in_specs=[
            pl.BlockSpec(memory_space=pltpu.SMEM),
            pl.BlockSpec((WIDE, WIDE), lambda g, t: (0, 0)),
            pl.BlockSpec((waves, 1, height, WIDE), lambda g, t: (0, g, 0, 0)),
            pl.BlockSpec((STEP, lats, rows), lambda g, t: (2 * (g + base) + t, 0, 0)),
        ],
        out_specs=pl.BlockSpec((STEP * COLS, rows), lambda g, t: (2 * g + t, 0)),
        scratch_shapes=[pltpu.VMEM((2, lats, 128), F32), pltpu.VMEM((WIDE, lats), BF16)],
        compiler_params=pltpu.CompilerParams(vmem_limit_bytes=VMEM_LIMIT),
        cost_estimate=pl.CostEstimate(
            flops=2 * slots * lats * rows * 32,
            bytes_accessed=2 * slots * lats * rows,
            transcendentals=0,
        ),
        name="legendre_backward",
    )(pairs, perm, coefs, legendre)


def table_kernel(cos_ref, sin_ref, step_ref, out_ref):
    def rotate(c, s, step_c, step_s):
        return c * step_c - s * step_s, s * step_c + c * step_s

    def body(i, carry):
        rows = pl.ds(pl.multiple_of(i * GROUP, GROUP), GROUP)
        to = pl.ds(pl.multiple_of(i * 2 * GROUP, 2 * GROUP), 2 * GROUP)
        steps = step_ref[rows, :]
        steps = [jnp.broadcast_to(steps[:, n : n + 1], (GROUP, 128)) for n in range(4)]
        first = cos_ref[rows, :], sin_ref[rows, :]
        for j in range(FINE):
            c, s = first
            for chunk in range(HALF // CHUNK):
                at = chunk * CHUNK + j * 128
                out_ref[to, at : at + 128] = jnp.concatenate([c, -s], axis=0).astype(BF16)
                if chunk < HALF // CHUNK - 1:
                    c, s = rotate(c, s, *steps[2:])
            if j < FINE - 1:
                first = rotate(*first, *steps[:2])
        return carry

    lax.fori_loop(0, cos_ref.shape[0] // GROUP, body, 0)


def angle_tables(slot_pair):
    flipped = M - 1 - slot_pair
    odd = slot_pair % 2 == 1
    waves = jnp.concatenate([jnp.where(odd, flipped, slot_pair), jnp.where(odd, slot_pair, flipped)])
    factor = jnp.where(waves == 0, 1.0, 2.0).astype(F32)
    unit = 2.0 * math.pi / NLON

    def angle(columns):
        columns = jnp.asarray(columns, jnp.int32)
        return (waves[:, None] * columns[None, :] % NLON).astype(F32) * unit

    lanes = angle(FINE * np.arange(128))
    first_cos = factor[:, None] * jnp.cos(lanes)
    first_sin = factor[:, None] * jnp.sin(lanes)
    moves = angle([1, 1, CHUNK, CHUNK])
    steps = jnp.where(jnp.arange(4) % 2 == 0, jnp.cos(moves), jnp.sin(moves))
    count = waves.shape[0]
    table = pl.pallas_call(
        table_kernel,
        out_shape=jax.ShapeDtypeStruct((2 * count, HALF), BF16),
        grid=(count // 128,),
        in_specs=[
            pl.BlockSpec((128, 128), lambda i: (i, 0)),
            pl.BlockSpec((128, 128), lambda i: (i, 0)),
            pl.BlockSpec((128, 4), lambda i: (i, 0)),
        ],
        out_specs=pl.BlockSpec((256, HALF), lambda i: (i, 0)),
        cost_estimate=pl.CostEstimate(
            flops=6 * count * HALF, bytes_accessed=4 * count * HALF, transcendentals=0
        ),
        name="angle_tables",
    )(first_cos, first_sin, steps)
    scale = (1.0 / (factor * math.sqrt(NLON))).reshape(2, 1, -1, 1, GROUP)
    scale = jnp.broadcast_to(scale, (2, 8, count // 2 // GROUP, 2, GROUP))
    return table.reshape(2, count, HALF), scale.reshape(2, 8, count)


def swap_blocks(tiles, lane):
    tiles = list(tiles)
    for d in (4, 2, 1):
        low = (lane // (16 * d)) % 2 == 0
        for i in range(8):
            if i & d:
                continue
            a, b = tiles[i], tiles[i + d]
            tiles[i] = jnp.where(low, a, pltpu.roll(b, 16 * d, 1))
            tiles[i + d] = jnp.where(low, pltpu.roll(a, 128 - 16 * d, 1), b)
    return tiles


def middle_kernel(
    sub, parts, edge_ref, halo_ref, perm_ref, order_ref, taps_ref, scale_ref, weight_ref,
    table_hbm, depart_hbm, pick_hbm, *refs,
):
    recv_refs, arrival_ref, coef_refs = refs[:parts], refs[parts], refs[parts + 1 : 2 * parts + 1]
    (
        table_ref, depart_ref, pick_ref, left_ref, plus_ref, minus_ref, grid_ref, near_ref,
        stage_ref, code_ref, moved_ref, pair_ref, sums_ref, sems,
    ) = refs[2 * parts + 1 :]
    per_part = TILES // parts
    copies = [
        pltpu.make_async_copy(table_hbm, table_ref, sems.at[0]),
        pltpu.make_async_copy(depart_hbm, depart_ref, sems.at[1]),
        pltpu.make_async_copy(pick_hbm, pick_ref, sems.at[2]),
    ]
    for copy in copies:
        copy.start()
    own = FIELDS * RUN * 16
    is_first, is_last = edge_ref[0], edge_ref[1]

    def gather_rows(part, step, carry):
        tile = part * per_part + step
        lane = lax.broadcasted_iota(jnp.int32, (1, 128), 1)
        lanes = pl.ds(pl.multiple_of(tile * 128, 128), 128)
        height = RUN * SUB
        rows = pl.ds(pl.multiple_of(step * 8 * height, 8 * height), 8 * height)
        mixed = jnp.dot(recv_refs[part][rows, :], perm_ref[...], preferred_element_type=F32)
        edge_rows = pl.ds(pl.multiple_of(tile * 64, 64), 64)
        edges = jnp.dot(halo_ref[edge_rows, :], perm_ref[...], preferred_element_type=F32)
        for par in range(2):
            cols = slice(128 * par, 128 * par + 128)
            tiles = swap_blocks([mixed[b * height : (b + 1) * height, cols] for b in range(8)], lane)
            for f in range(FIELDS):
                for k in range(RUN):
                    at = (f * RUN + k) * 16
                    block = [tiles[h * 4 + f][8 * k : 8 * k + 8] for h in range(2)]
                    left_ref[par, at : at + 16, lanes] = jnp.concatenate(block, axis=0).astype(BF16)
            ends = swap_blocks([edges[8 * b : 8 * b + 8, cols] for b in range(8)], lane)
            row = lax.broadcasted_iota(jnp.int32, (8, 128), 0)
            if par == 1:
                sign = jnp.where((row < RIM) & (is_first == 1), -1.0, 1.0)
                ends = [end * sign for end in ends]
            across = (row >= RIM) & (is_last == 1)
            for f in range(FIELDS):
                block = [jnp.where(across, ends[(1 - h) * 4 + f], ends[h * 4 + f]) for h in range(2)]
                at = own + f * 16
                left_ref[par, at : at + 16, lanes] = jnp.concatenate(block, axis=0).astype(BF16)
        return carry

    for part in range(parts):
        lax.fori_loop(0, per_part, functools.partial(gather_rows, part), 0)
    copies[0].wait()

    def to_grid(tile, carry):
        cols = pl.ds(pl.multiple_of(tile * 256, 256), 256)
        even = jnp.dot(left_ref[0], table_ref[0, :, cols], preferred_element_type=F32)
        odd = jnp.dot(left_ref[1], table_ref[1, :, cols], preferred_element_type=F32)
        plus_ref[...] = even + odd
        minus_ref[...] = even - odd
        place = lax.broadcasted_iota(jnp.int32, (8, 256), 0)
        for side, ref in enumerate((plus_ref, minus_ref)):
            to = pl.ds(pl.multiple_of(side * HALF + tile * 256, 256), 256)
            for f in range(FIELDS):
                for k in range(RUN):
                    at = (f * RUN + k) * 16
                    grid_ref[f * REACH + RIM + k, :, to] = ref[at : at + 16, :].astype(BF16)
                for k in range(RIM):
                    before, after = [], []
                    for h in range(2):
                        end = own + f * 16 + 8 * h
                        at = (f * RUN + k + RUN - RIM) * 16 + 8 * h
                        rolled = pltpu.roll(ref[at : at + 8, :], 1, 0)
                        before.append(jnp.where(place == 0, ref[end + k : end + k + 1, :], rolled))
                        at = (f * RUN + k) * 16 + 8 * h
                        rolled = pltpu.roll(ref[at : at + 8, :], 7, 0)
                        end = end + RIM
                        after.append(
                            jnp.where(place == sub - 1, ref[end + k : end + k + 1, :], rolled)
                        )
                    grid_ref[f * REACH + k, :, to] = jnp.concatenate(before, 0).astype(BF16)
                    grid_ref[f * REACH + RIM + RUN + k, :, to] = jnp.concatenate(after, 0).astype(
                        BF16
                    )
        return carry

    lax.fori_loop(0, HALF // 256, to_grid, 0)
    copies[1].wait()
    copies[2].wait()

    def interpolate(chunk, carry):
        lanes = pl.ds(pl.multiple_of(chunk * CHUNK, CHUNK), CHUNK)
        lane = lax.broadcasted_iota(jnp.int32, (16, 128), 1)
        previous = jnp.where(chunk == 0, CHUNKS - 1, chunk - 1)
        following = jnp.where(chunk == CHUNKS - 1, 0, chunk + 1)

        def neighbours(row, carry):
            for j in range(FINE):
                here = grid_ref[row, :, pl.ds(pl.multiple_of(chunk * CHUNK + j * 128, 128), 128)]
                near_ref[row, :, (RIM + j) * 128 : (RIM + j + 1) * 128] = here
                here = here.astype(F32)
                if j >= FINE - RIM:
                    at = pl.ds(pl.multiple_of(previous * CHUNK + j * 128, 128), 128)
                    there = grid_ref[row, :, at].astype(F32)
                    mixed = pltpu.roll(jnp.where(lane == 127, there, here), 1, 1)
                    slot = j - (FINE - RIM)
                    near_ref[row, :, slot * 128 : slot * 128 + 128] = mixed.astype(BF16)
                if j < RIM:
                    at = pl.ds(pl.multiple_of(following * CHUNK + j * 128, 128), 128)
                    there = grid_ref[row, :, at].astype(F32)
                    mixed = pltpu.roll(jnp.where(lane == 0, there, here), 127, 1)
                    slot = RIM + FINE + j
                    near_ref[row, :, slot * 128 : slot * 128 + 128] = mixed.astype(BF16)
            return carry

        lax.fori_loop(0, FIELDS * REACH, neighbours, 0, unroll=4)
        code = pick_ref[:, :, lanes] * 16 + depart_ref[:, :, lanes]
        code = code.reshape(2 * RUN * SUB, CHUNK).astype(F32).astype(BF16)
        code = jnp.dot(code, order_ref[0], preferred_element_type=F32).astype(jnp.int32)
        for j in range(FINE):
            code_ref[j] = code[:, 128 * j : 128 * j + 128]

        def points(j, carry):
            at_lanes = pl.ds(pl.multiple_of(chunk * CHUNK + j * 128, 128), 128)
            for k in range(RUN):
                index, column = [], []
                for h in range(2):
                    code = code_ref[j, pl.ds(h * RUN * SUB + k, SUB, stride=RUN), :]
                    index.append(code >> 2)
                    column.append(code & 3)
                column = jnp.concatenate(column, axis=0).astype(F32).astype(BF16)
                hits = [column == jnp.asarray(d, BF16) for d in range(4)]
                totals = [jnp.zeros((16, 128), F32) for _ in range(FIELDS)]
                for r in range(7):
                    weights = []
                    for b in range(4):
                        entry = taps_ref[r * 4 + b]
                        found = [jnp.take_along_axis(entry, index[h], axis=1) for h in range(2)]
                        weights.append(jnp.concatenate(found, axis=0).astype(BF16))
                    factors = []
                    for c in range(-RIM, RIM + 1):
                        factor = jnp.zeros((16, 128), BF16)
                        for d in range(4):
                            b = c - (d - 2) + 1
                            if 0 <= b < 4:
                                factor = jnp.where(hits[d], weights[b], factor)
                        factors.append(factor)
                    for f in range(FIELDS):
                        row = f * REACH + k + r
                        part = None
                        for c in range(7):
                            near = near_ref[row, :, pl.ds(pl.multiple_of((j + c) * 128, 128), 128)]
                            part = factors[c] * near if part is None else part + factors[c] * near
                        totals[f] = totals[f] + part.astype(F32)
                for f in range(FIELDS):
                    at = (f * RUN + k) * 16
                    moved_ref[at : at + 16, at_lanes] = totals[f].astype(BF16)
            return carry

        lax.fori_loop(0, FINE, points, 0)
        natural = jnp.dot(moved_ref[:, lanes], order_ref[1], preferred_element_type=F32)
        for j in range(FINE):
            for f in range(FIELDS):
                for k in range(RUN):
                    for h in range(2):
                        at = (f * RUN + k) * 16 + 8 * h
                        stage_ref[j, f * 2 + h, pl.ds(k, SUB, stride=RUN), :] = natural[
                            at : at + 8, 128 * j : 128 * j + 128
                        ]
        for f in range(FIELDS):
            for h in range(2):
                rows = [stage_ref[j, f * 2 + h] for j in range(FINE)]
                arrival_ref[f, h, :, lanes] = jnp.concatenate(rows, axis=1).astype(BF16)
        return carry

    lax.fori_loop(0, CHUNKS, interpolate, 0)

    def fold(tile, carry):
        lanes = pl.ds(pl.multiple_of(tile * 128, 128), 128)
        other = pl.ds(pl.multiple_of(tile * 128 + HALF, 128), 128)
        a, b = moved_ref[:, lanes].astype(F32), moved_ref[:, other].astype(F32)
        pair_ref[0, :, lanes] = (a + b).astype(BF16)
        pair_ref[1, :, lanes] = (a - b).astype(BF16)
        return carry

    lax.fori_loop(0, HALF // 128, fold, 0)

    def to_waves(tile, carry):
        cols = pl.ds(pl.multiple_of(tile * 256, 256), 256)
        for par in range(2):
            out = dot_nt(pair_ref[par], table_ref[par, cols, :])
            out = out * scale_ref[par, 0:1, cols]
            for half in range(2):
                part = out[:, 128 * half : 128 * half + 128] * weight_ref[...]
                sums_ref[par, tile * 2 + half] = part
        return carry

    lax.fori_loop(0, TILES // 2, to_waves, 0)

    def scatter_rows(part, step, carry):
        tile = part * per_part + step
        lane = lax.broadcasted_iota(jnp.int32, (1, 128), 1)
        height = RUN * SUB
        halves = []
        for par in range(2):
            tiles = []
            for h in range(2):
                for f in range(FIELDS):
                    pieces = []
                    for k in range(RUN):
                        at = (f * RUN + k) * 16 + 8 * h
                        pieces.append(sums_ref[par, tile, at : at + 8, :])
                    tiles.append(jnp.concatenate(pieces, axis=0))
            halves.append(jnp.concatenate(swap_blocks(tiles, lane), axis=0))
        rows = pl.ds(pl.multiple_of(step * 8 * height, 8 * height), 8 * height)
        coef_refs[part][rows, :] = jnp.concatenate(halves, axis=1).astype(BF16)
        return carry

    for part in range(parts):
        lax.fori_loop(0, per_part, functools.partial(scatter_rows, part), 0)


def transport(sub, edge, recv, halo, perm, order, taps, scale, weight, table, depart, pick):
    parts = len(recv)
    rows, width = recv[0].shape
    lats = RUN * SUB
    left = FIELDS * (RUN + 1) * 16
    own = FIELDS * RUN * 16
    slots2 = table.shape[1]
    vmem = pl.BlockSpec(memory_space=pltpu.VMEM)
    anywhere = pl.BlockSpec(memory_space=pl.ANY)
    return pl.pallas_call(
        functools.partial(middle_kernel, sub, parts),
        out_shape=(
            jax.ShapeDtypeStruct((FIELDS, 2, lats, NLON), BF16),
            *[jax.ShapeDtypeStruct((rows, width), BF16)] * parts,
        ),
        in_specs=[pl.BlockSpec(memory_space=pltpu.SMEM)] + [vmem] * 6 + [anywhere] * 3 + [vmem] * parts,
        out_specs=(vmem,) * (parts + 1),
        scratch_shapes=[
            pltpu.VMEM((2, slots2, HALF), BF16),
            pltpu.VMEM((2, lats, NLON), jnp.int32),
            pltpu.VMEM((2, lats, NLON), jnp.int32),
            pltpu.VMEM((2, left, slots2), BF16),
            pltpu.VMEM((left, 256), F32),
            pltpu.VMEM((left, 256), F32),
            pltpu.VMEM((FIELDS * REACH, 16, NLON), BF16),
            pltpu.VMEM((FIELDS * REACH, 16, CHUNK + 2 * RIM * 128), BF16),
            pltpu.VMEM((FINE, FIELDS * 2, lats, 128), F32),
            pltpu.VMEM((FINE, 2 * lats, 128), jnp.int32),
            pltpu.VMEM((own, NLON), BF16),
            pltpu.VMEM((2, own, HALF), BF16),
            pltpu.VMEM((2, TILES, own, 128), F32),
            pltpu.SemaphoreType.DMA((3,)),
        ],
        compiler_params=pltpu.CompilerParams(vmem_limit_bytes=VMEM_LIMIT),
        cost_estimate=pl.CostEstimate(
            flops=8 * left * slots2 * HALF,
            bytes_accessed=2 * rows * width * 8 + 4 * slots2 * HALF,
            transcendentals=0,
        ),
        name="transport",
    )(edge, halo, perm, order, taps, scale, weight, table, depart, pick, *recv)


def tap_tables(stencil_weight):
    choose = np.zeros((16, 7, 4, 4), np.float32)
    for r in range(7):
        for d in range(4):
            a = (r - 3) - (d - 2) + 1
            if 0 <= a < 4:
                for b in range(4):
                    choose[4 * a + b, r, b, d] = 1.0
    table = jnp.einsum("tw,wnd->ntd", stencil_weight, choose.reshape(16, 28, 4), precision="highest")
    table = jnp.pad(table.reshape(28, 4 * NSTEN), ((0, 0), (0, 128 - 4 * NSTEN)))
    return jnp.broadcast_to(table[:, None, :], (28, 8, 128))


def exchange(array, axis, distance):
    devices = lax.axis_size(axis)
    return lax.ppermute(array, axis, [(i, i ^ distance) for i in range(devices)])


def gather_rows(spectral):
    devices = lax.axis_size("band")
    band = lax.axis_index("band")
    turned = spectral.transpose(0, 2, 1)
    pieces = [turned] + [exchange(turned, "band", d) for d in range(1, devices)]
    stacked = jnp.stack(pieces)
    ordered = [
        lax.dynamic_index_in_dim(stacked, band ^ b, 0, keepdims=False) for b in range(devices)
    ]
    return jnp.concatenate(ordered, axis=2)


def scatter_sums(sums, slots, row_local):
    devices = lax.axis_size("band")
    band = lax.axis_index("band")
    shaped = sums.reshape(slots, COLS, -1)
    parts = jnp.stack(
        [shaped[:, :, b * row_local : (b + 1) * row_local] for b in range(devices)]
    )
    total = lax.dynamic_index_in_dim(parts, band, 0, keepdims=False).astype(F32)
    for d in range(1, devices):
        piece = lax.dynamic_index_in_dim(parts, band ^ d, 0, keepdims=False)
        total = total + exchange(piece, "band", d).astype(F32)
    return total.astype(BF16).transpose(0, 2, 1)


def per_device(
    spectral, legendre, slot_pair, quad_weight, depart_code, stencil_pick, stencil_weight
):
    slots, row_local, _ = spectral.shape
    height = depart_code.shape[2]
    waves = lax.axis_size("wave")
    sub = height // RUN
    groups = slots // GROUP
    wave_rank = lax.axis_index("wave")
    lat_rank = lax.axis_index(("band", "wave"))
    lat_devices = lax.axis_size(("band", "wave"))
    my_pairs = lax.dynamic_slice_in_dim(slot_pair, wave_rank * slots, slots)
    perm = lane_order()

    parts = 2 if groups % 2 == 0 else 1
    blocks = waves * groups
    arriving = slot_pair.reshape(waves, parts, -1).swapaxes(0, 1).reshape(-1)

    spec = gather_rows(spectral)
    table, scale = angle_tables(arriving)
    taps = tap_tables(stencil_weight)
    my_weight = lax.dynamic_slice_in_dim(quad_weight, wave_rank * height, height)
    weight = my_weight.reshape(sub, RUN).T
    if sub != SUB:
        weight = jnp.pad(weight, ((0, 0), (0, SUB - sub)))
    weight = jnp.broadcast_to(weight[None, :, None, :, None], (FIELDS, RUN, 2, SUB, 128))
    weight = weight.reshape(-1, 128)
    is_first, is_last = lat_rank == 0, lat_rank == lat_devices - 1
    edge = jnp.stack([is_first, is_last]).astype(jnp.int32)
    spec, table, scale, taps, weight, edge, my_pairs = lax.optimization_barrier(
        (spec, table, scale, taps, weight, edge, my_pairs)
    )
    received = []
    for part in range(parts):
        sent = legendre_forward(my_pairs, spec, legendre, waves, part, parts)
        if received:
            sent, received[-1] = lax.optimization_barrier((sent, received[-1]))
        received.append(
            lax.all_to_all(sent, "wave", split_axis=0, concat_axis=0, tiled=True)
        )
    recv = [r.reshape(-1, height, WIDE) for r in received]
    first = jnp.concatenate([r[:, 0 : RIM * sub : sub] for r in recv])
    last = jnp.concatenate([r[:, (RUN - RIM + 1) * sub - 1 :: sub] for r in recv])
    up = [(i, i + 1) for i in range(lat_devices - 1)]
    down = [(i + 1, i) for i in range(lat_devices - 1)]
    before = lax.ppermute(last, ("band", "wave"), up)
    after = lax.ppermute(first, ("band", "wave"), down)
    halo = [jnp.where(is_first, first[:, RIM - 1 - i], before[:, i]) for i in range(RIM)]
    halo += [jnp.where(is_last, last[:, RIM - 1 - i], after[:, i]) for i in range(RIM)]
    halo += [jnp.zeros_like(halo[0])] * (8 - 2 * RIM)
    halo = jnp.stack(halo, axis=1).reshape(blocks * 8, WIDE)

    depart, pick = depart_code[0], stencil_pick[0]
    if sub != SUB:
        gap = SUB - sub
        recv = [r.reshape(-1, RUN, sub, WIDE) for r in recv]
        recv = [jnp.pad(r, ((0, 0), (0, 0), (0, gap), (0, 0))) for r in recv]
        depart = jnp.pad(depart, ((0, 0), (0, RUN * gap), (0, 0)))
        pick = jnp.pad(pick, ((0, 0), (0, RUN * gap), (0, 0)))
    arrival, *coefs = transport(
        sub,
        edge,
        [r.reshape(-1, WIDE) for r in recv],
        halo,
        perm,
        longitude_order(),
        taps,
        scale,
        weight,
        table,
        depart,
        pick,
    )
    arrival = arrival[None, :, :, :height]
    coefs = [c.reshape(-1, RUN, SUB, WIDE)[:, :, :sub] for c in coefs]
    outs, by_wave = [], None
    for part in range(parts):
        leaving = coefs[part].reshape(waves, groups // parts, height, WIDE)
        if part:
            leaving, by_wave = lax.optimization_barrier((leaving, by_wave))
        ready = by_wave
        by_wave = lax.all_to_all(leaving, "wave", split_axis=0, concat_axis=0, tiled=True)
        if part:
            outs.append(legendre_backward(my_pairs, perm, ready, legendre, part - 1))
    outs.append(legendre_backward(my_pairs, perm, by_wave, legendre, parts - 1))
    outs = [scatter_sums(sums, slots // parts, row_local) for sums in outs]
    return (arrival, jnp.concatenate(outs))


def solution(mesh):
    in_specs = (
        P("wave", "band", None),
        P("wave", "band", None),
        P(),
        P("band"),
        P(None, None, ("band", "wave"), None),
        P(None, None, ("band", "wave"), None),
        P(),
    )
    out_specs = (P(None, None, None, ("band", "wave"), None), P("wave", "band", None))
    return jax.shard_map(
        per_device, mesh=mesh, in_specs=in_specs, out_specs=out_specs, check_vma=False
    )
```

```python
import functools
import math

import jax
import jax.numpy as jnp
import numpy as np
from jax import lax
from jax.experimental import pallas as pl
from jax.experimental.pallas import tpu as pltpu
from jax.sharding import PartitionSpec as P

M = 1280
NLON = 5120
HALF = NLON // 2
FIELDS = 4
NSTEN = 16
RIM = 3
COLS = 8
GROUP = 8
WIDE = GROUP * 4 * COLS
RUN = 5
SUB = 8
REACH = RUN + 2 * RIM
TILES = 10
CHUNK = 512
FINE = CHUNK // 128
CHUNKS = NLON // CHUNK
STEP = 8
REACH_TAPS = (2 * RIM + 1) ** 2
F32 = jnp.float32
BF16 = jnp.bfloat16
VMEM_LIMIT = 60 * 2**20


def dot_nt(left, right):
    return lax.dot_general(left, right, (((1,), (1,)), ((), ())), preferred_element_type=F32)


def lane_order():
    index = np.arange(WIDE).reshape(GROUP, 2, 2, FIELDS, 2).transpose(1, 2, 3, 4, 0).reshape(-1)
    matrix = np.zeros((WIDE, WIDE), np.float32)
    matrix[index, np.arange(WIDE)] = 1.0
    return jnp.asarray(matrix, BF16)


def longitude_order():
    position = np.arange(CHUNK)
    longitude = FINE * (position % 128) + position // 128
    matrix = np.zeros((CHUNK, CHUNK), np.float32)
    matrix[longitude, position] = 1.0
    return jnp.asarray(matrix, BF16), jnp.asarray(matrix.T, BF16)


def row_masks(pair, rows):
    row = lax.broadcasted_iota(jnp.int32, (1, rows), 1)
    low_count = M - pair
    higher = row >= low_count
    degree = jnp.where(higher, row - low_count, row)
    sign = (1 - 2 * (degree & 1)).astype(F32)
    in_use = row <= M
    side = jnp.where(higher, 1, 0) ^ (pair & 1)
    even = jnp.where(in_use & (side == 0), 1.0, 0.0)
    odd = jnp.where(in_use & (side == 1), 1.0, 0.0)
    return even, odd, sign


def forward_kernel(height, base, pair_ref, spec_ref, leg_ref, out_ref, acc_ref):
    group, step = pl.program_id(0) + base, pl.program_id(1)
    rows = spec_ref.shape[2]
    sub = height // RUN

    pieces = []
    for u in range(STEP):
        even, odd, sign = row_masks(pair_ref[group * GROUP + step * STEP + u], rows)
        spec = spec_ref[u].astype(F32)
        south = spec * sign
        parts = [spec * even, south * even, spec * odd, south * odd]
        masked = jnp.concatenate(parts, axis=0).astype(BF16)
        pieces.append(dot_nt(leg_ref[u], masked))
    for half in range(STEP // 4):
        acc_ref[step * (STEP // 4) + half] = jnp.concatenate(pieces[4 * half : 4 * half + 4], axis=1)

    @pl.when(step == GROUP // STEP - 1)
    def _():
        for dest in range(out_ref.shape[0]):
            halves = []
            for half in range(2):
                pieces = [
                    acc_ref[half, pl.ds(dest * height + k, sub, stride=RUN), :]
                    for k in range(RUN)
                ]
                halves.append(jnp.concatenate(pieces, axis=0))
            out_ref[dest, 0] = jnp.concatenate(halves, axis=1).astype(BF16)


def legendre_forward(pairs, spec, legendre, waves, part, parts):
    slots, lats, rows = legendre.shape
    groups = slots // GROUP // parts
    base = part * groups
    height = lats // waves
    return pl.pallas_call(
        functools.partial(forward_kernel, height, base),
        out_shape=jax.ShapeDtypeStruct((waves, groups, height, WIDE), BF16),
        grid=(groups, GROUP // STEP),
        in_specs=[
            pl.BlockSpec(memory_space=pltpu.SMEM),
            pl.BlockSpec((STEP, COLS, rows), lambda g, t: (GROUP // STEP * (g + base) + t, 0, 0)),
            pl.BlockSpec((STEP, lats, rows), lambda g, t: (GROUP // STEP * (g + base) + t, 0, 0)),
        ],
        out_specs=pl.BlockSpec((waves, 1, height, WIDE), lambda g, t: (0, g, 0, 0)),
        scratch_shapes=[pltpu.VMEM((2, lats, 128), F32)],
        compiler_params=pltpu.CompilerParams(vmem_limit_bytes=VMEM_LIMIT),
        cost_estimate=pl.CostEstimate(
            flops=2 * groups * GROUP * lats * rows * 32,
            bytes_accessed=2 * groups * GROUP * lats * rows,
            transcendentals=0,
        ),
        name="legendre_forward",
    )(pairs, spec, legendre)


def backward_kernel(
    height, base, pair_ref, perm_ref, coef_ref, leg_ref, out_ref, rows_ref, turned_ref
):
    group, step = pl.program_id(0) + base, pl.program_id(1)
    rows = leg_ref.shape[2]
    sub = height // RUN

    @pl.when(step == 0)
    def _():
        for source in range(coef_ref.shape[0]):
            block = coef_ref[source, 0].astype(F32)
            for k in range(RUN):
                for half in range(2):
                    rows_ref[half, pl.ds(source * height + k, sub, stride=RUN), :] = block[
                        k * sub : (k + 1) * sub, 128 * half : 128 * half + 128
                    ]
        natural = jnp.concatenate([rows_ref[0], rows_ref[1]], axis=1).astype(BF16)
        turned_ref[...] = dot_nt(perm_ref[...], natural).astype(BF16)

    sums = []
    for u in range(STEP):
        even, odd, sign = row_masks(pair_ref[group * GROUP + step * STEP + u], rows)
        at = pl.ds(pl.multiple_of(step * (32 * STEP) + 32 * u, 32), 32)
        raw = jnp.dot(turned_ref[at, :], leg_ref[u], preferred_element_type=F32)
        low = raw[0:8] + sign * raw[8:16]
        high = raw[16:24] + sign * raw[24:32]
        sums.append(low * even + high * odd)
    out_ref[...] = jnp.concatenate(sums, axis=0).astype(BF16)


def legendre_backward(pairs, perm, coefs, legendre, part):
    _, lats, rows = legendre.shape
    waves, groups, height, _ = coefs.shape
    slots = groups * GROUP
    base = part * groups
    return pl.pallas_call(
        functools.partial(backward_kernel, height, base),
        out_shape=jax.ShapeDtypeStruct((slots * COLS, rows), BF16),
        grid=(groups, GROUP // STEP),
        in_specs=[
            pl.BlockSpec(memory_space=pltpu.SMEM),
            pl.BlockSpec((WIDE, WIDE), lambda g, t: (0, 0)),
            pl.BlockSpec((waves, 1, height, WIDE), lambda g, t: (0, g, 0, 0)),
            pl.BlockSpec((STEP, lats, rows), lambda g, t: (GROUP // STEP * (g + base) + t, 0, 0)),
        ],
        out_specs=pl.BlockSpec((STEP * COLS, rows), lambda g, t: (GROUP // STEP * g + t, 0)),
        scratch_shapes=[pltpu.VMEM((2, lats, 128), F32), pltpu.VMEM((WIDE, lats), BF16)],
        compiler_params=pltpu.CompilerParams(vmem_limit_bytes=VMEM_LIMIT),
        cost_estimate=pl.CostEstimate(
            flops=2 * slots * lats * rows * 32,
            bytes_accessed=2 * slots * lats * rows,
            transcendentals=0,
        ),
        name="legendre_backward",
    )(pairs, perm, coefs, legendre)


def table_kernel(cos_ref, sin_ref, step_ref, out_ref):
    batch = 4 * GROUP

    def rotate(c, s, step_c, step_s):
        return c * step_c - s * step_s, s * step_c + c * step_s

    def body(i, carry):
        rows = pl.ds(pl.multiple_of(i * batch, batch), batch)
        steps = step_ref[rows, :]
        steps = [jnp.broadcast_to(steps[:, n : n + 1], (batch, 128)) for n in range(4)]
        first = cos_ref[rows, :], sin_ref[rows, :]
        for j in range(FINE):
            c, s = first
            for chunk in range(HALF // CHUNK):
                at = chunk * CHUNK + j * 128
                parts = []
                for g in range(batch // GROUP):
                    parts += [c[GROUP * g : GROUP * g + GROUP], -s[GROUP * g : GROUP * g + GROUP]]
                to = pl.ds(pl.multiple_of(i * 2 * batch, 2 * batch), 2 * batch)
                out_ref[to, at : at + 128] = jnp.concatenate(parts, axis=0).astype(BF16)
                if chunk < HALF // CHUNK - 1:
                    c, s = rotate(c, s, *steps[2:])
            if j < FINE - 1:
                first = rotate(*first, *steps[:2])
        return carry

    lax.fori_loop(0, cos_ref.shape[0] // batch, body, 0)


def angle_tables(slot_pair):
    flipped = M - 1 - slot_pair
    odd = slot_pair % 2 == 1
    waves = jnp.concatenate([jnp.where(odd, flipped, slot_pair), jnp.where(odd, slot_pair, flipped)])
    factor = jnp.where(waves == 0, 1.0, 2.0).astype(F32)
    unit = 2.0 * math.pi / NLON

    def angle(columns):
        columns = jnp.asarray(columns, jnp.int32)
        return (waves[:, None] * columns[None, :] % NLON).astype(F32) * unit

    lanes = angle(FINE * np.arange(128))
    first_cos = factor[:, None] * jnp.cos(lanes)
    first_sin = factor[:, None] * jnp.sin(lanes)
    moves = angle([1, 1, CHUNK, CHUNK])
    steps = jnp.where(jnp.arange(4) % 2 == 0, jnp.cos(moves), jnp.sin(moves))
    count = waves.shape[0]
    table = pl.pallas_call(
        table_kernel,
        out_shape=jax.ShapeDtypeStruct((2 * count, HALF), BF16),
        grid=(count // 128,),
        in_specs=[
            pl.BlockSpec((128, 128), lambda i: (i, 0)),
            pl.BlockSpec((128, 128), lambda i: (i, 0)),
            pl.BlockSpec((128, 4), lambda i: (i, 0)),
        ],
        out_specs=pl.BlockSpec((256, HALF), lambda i: (i, 0)),
        cost_estimate=pl.CostEstimate(
            flops=6 * count * HALF, bytes_accessed=4 * count * HALF, transcendentals=0
        ),
        name="angle_tables",
    )(first_cos, first_sin, steps)
    scale = (1.0 / (factor * math.sqrt(NLON))).reshape(2, 1, -1, 1, GROUP)
    scale = jnp.broadcast_to(scale, (2, 8, count // 2 // GROUP, 2, GROUP))
    return table.reshape(2, count, HALF), scale.reshape(2, 8, count)


def swap_blocks(tiles, lane):
    tiles = list(tiles)
    for d in (4, 2, 1):
        low = (lane // (16 * d)) % 2 == 0
        for i in range(8):
            if i & d:
                continue
            a, b = tiles[i], tiles[i + d]
            tiles[i] = jnp.where(low, a, pltpu.roll(b, 16 * d, 1))
            tiles[i + d] = jnp.where(low, pltpu.roll(a, 128 - 16 * d, 1), b)
    return tiles


def middle_kernel(
    sub, parts, edge_ref, halo_ref, perm_ref, order_ref, scale_ref, weight_ref,
    table_hbm, factor_hbm, *refs,
):
    recv_refs, arrival_ref, coef_refs = refs[:parts], refs[parts], refs[parts + 1 : 2 * parts + 1]
    (
        table_ref, factor_ref, left_ref, plus_ref, minus_ref, grid_ref, near_ref,
        stage_ref, moved_ref, pair_ref, sums_ref, table_sem, factor_sems,
    ) = refs[2 * parts + 1 :]
    per_part = TILES // parts
    table_copy = pltpu.make_async_copy(table_hbm, table_ref, table_sem)
    table_copy.start()
    pltpu.make_async_copy(factor_hbm.at[0], factor_ref.at[0], factor_sems.at[0]).start()
    own = FIELDS * RUN * 16
    is_first, is_last = edge_ref[0], edge_ref[1]

    def gather_rows(part, step, carry):
        tile = part * per_part + step
        lane = lax.broadcasted_iota(jnp.int32, (1, 128), 1)
        lanes = pl.ds(pl.multiple_of(tile * 128, 128), 128)
        height = RUN * SUB
        rows = pl.ds(pl.multiple_of(step * 8 * height, 8 * height), 8 * height)
        mixed = jnp.dot(recv_refs[part][rows, :], perm_ref[...], preferred_element_type=F32)
        edge_rows = pl.ds(pl.multiple_of(tile * 64, 64), 64)
        edges = jnp.dot(halo_ref[edge_rows, :], perm_ref[...], preferred_element_type=F32)
        for par in range(2):
            cols = slice(128 * par, 128 * par + 128)
            tiles = swap_blocks([mixed[b * height : (b + 1) * height, cols] for b in range(8)], lane)
            for f in range(FIELDS):
                for k in range(RUN):
                    at = (f * RUN + k) * 16
                    block = [tiles[h * 4 + f][8 * k : 8 * k + 8] for h in range(2)]
                    left_ref[par, at : at + 16, lanes] = jnp.concatenate(block, axis=0).astype(BF16)
            ends = swap_blocks([edges[8 * b : 8 * b + 8, cols] for b in range(8)], lane)
            row = lax.broadcasted_iota(jnp.int32, (8, 128), 0)
            if par == 1:
                sign = jnp.where((row < RIM) & (is_first == 1), -1.0, 1.0)
                ends = [end * sign for end in ends]
            across = (row >= RIM) & (is_last == 1)
            for f in range(FIELDS):
                block = [jnp.where(across, ends[(1 - h) * 4 + f], ends[h * 4 + f]) for h in range(2)]
                at = own + f * 16
                left_ref[par, at : at + 16, lanes] = jnp.concatenate(block, axis=0).astype(BF16)
        return carry

    for part in range(parts):
        lax.fori_loop(0, per_part, functools.partial(gather_rows, part), 0)
    table_copy.wait()

    def to_grid(tile, carry):
        cols = pl.ds(pl.multiple_of(tile * 256, 256), 256)
        even = jnp.dot(left_ref[0], table_ref[0, :, cols], preferred_element_type=F32)
        odd = jnp.dot(left_ref[1], table_ref[1, :, cols], preferred_element_type=F32)
        plus_ref[...] = even + odd
        minus_ref[...] = even - odd
        place = lax.broadcasted_iota(jnp.int32, (8, 256), 0)
        for side, ref in enumerate((plus_ref, minus_ref)):
            to = pl.ds(pl.multiple_of(side * HALF + tile * 256, 256), 256)
            for f in range(FIELDS):
                for k in range(RUN):
                    at = (f * RUN + k) * 16
                    grid_ref[f * REACH + RIM + k, :, to] = ref[at : at + 16, :].astype(BF16)
                for k in range(RIM):
                    before, after = [], []
                    for h in range(2):
                        end = own + f * 16 + 8 * h
                        at = (f * RUN + k + RUN - RIM) * 16 + 8 * h
                        rolled = pltpu.roll(ref[at : at + 8, :], 1, 0)
                        before.append(jnp.where(place == 0, ref[end + k : end + k + 1, :], rolled))
                        at = (f * RUN + k) * 16 + 8 * h
                        rolled = pltpu.roll(ref[at : at + 8, :], 7, 0)
                        end = end + RIM
                        after.append(
                            jnp.where(place == sub - 1, ref[end + k : end + k + 1, :], rolled)
                        )
                    grid_ref[f * REACH + k, :, to] = jnp.concatenate(before, 0).astype(BF16)
                    grid_ref[f * REACH + RIM + RUN + k, :, to] = jnp.concatenate(after, 0).astype(
                        BF16
                    )
        return carry

    lax.fori_loop(0, HALF // 256, to_grid, 0)
    def fetch(chunk, slot):
        return pltpu.make_async_copy(
            factor_hbm.at[chunk], factor_ref.at[slot], factor_sems.at[slot]
        )

    def interpolate(chunk, carry):
        lanes = pl.ds(pl.multiple_of(chunk * CHUNK, CHUNK), CHUNK)
        lane = lax.broadcasted_iota(jnp.int32, (16, 128), 1)
        previous = jnp.where(chunk == 0, CHUNKS - 1, chunk - 1)
        following = jnp.where(chunk == CHUNKS - 1, 0, chunk + 1)
        slot = lax.rem(chunk, 2)

        @pl.when(chunk + 1 < CHUNKS)
        def _():
            fetch(chunk + 1, 1 - slot).start()

        def neighbours(row, carry):
            for j in range(FINE):
                here = grid_ref[row, :, pl.ds(pl.multiple_of(chunk * CHUNK + j * 128, 128), 128)]
                near_ref[row, :, (RIM + j) * 128 : (RIM + j + 1) * 128] = here
                here = here.astype(F32)
                if j >= FINE - RIM:
                    at = pl.ds(pl.multiple_of(previous * CHUNK + j * 128, 128), 128)
                    there = grid_ref[row, :, at].astype(F32)
                    mixed = pltpu.roll(jnp.where(lane == 127, there, here), 1, 1)
                    to = (j - (FINE - RIM)) * 128
                    near_ref[row, :, to : to + 128] = mixed.astype(BF16)
                if j < RIM:
                    at = pl.ds(pl.multiple_of(following * CHUNK + j * 128, 128), 128)
                    there = grid_ref[row, :, at].astype(F32)
                    mixed = pltpu.roll(jnp.where(lane == 0, there, here), 127, 1)
                    to = (RIM + FINE + j) * 128
                    near_ref[row, :, to : to + 128] = mixed.astype(BF16)
            return carry

        lax.fori_loop(0, FIELDS * REACH, neighbours, 0, unroll=4)
        fetch(chunk, slot).wait()

        def points(j, carry):
            at_lanes = pl.ds(pl.multiple_of(chunk * CHUNK + j * 128, 128), 128)
            for k in range(RUN):
                totals = [None] * FIELDS
                for r in range(7):
                    factors = [factor_ref[slot, j, k, r * 7 + c] for c in range(7)]
                    for f in range(FIELDS):
                        row = f * REACH + k + r
                        part = None
                        for c in range(7):
                            near = near_ref[row, :, pl.ds(pl.multiple_of((j + c) * 128, 128), 128)]
                            part = factors[c] * near if part is None else part + factors[c] * near
                        part = part.astype(F32)
                        totals[f] = part if totals[f] is None else totals[f] + part
                for f in range(FIELDS):
                    at = (f * RUN + k) * 16
                    moved_ref[at : at + 16, at_lanes] = totals[f].astype(BF16)
            return carry

        lax.fori_loop(0, FINE, points, 0)
        natural = jnp.dot(moved_ref[:, lanes], order_ref[...], preferred_element_type=F32)
        for j in range(FINE):
            for f in range(FIELDS):
                for k in range(RUN):
                    for h in range(2):
                        at = (f * RUN + k) * 16 + 8 * h
                        stage_ref[j, f * 2 + h, pl.ds(k, SUB, stride=RUN), :] = natural[
                            at : at + 8, 128 * j : 128 * j + 128
                        ]
        for f in range(FIELDS):
            for h in range(2):
                rows = [stage_ref[j, f * 2 + h] for j in range(FINE)]
                arrival_ref[f, h, :, lanes] = jnp.concatenate(rows, axis=1).astype(BF16)
        return carry

    lax.fori_loop(0, CHUNKS, interpolate, 0)

    def fold(tile, carry):
        lanes = pl.ds(pl.multiple_of(tile * 128, 128), 128)
        other = pl.ds(pl.multiple_of(tile * 128 + HALF, 128), 128)
        a, b = moved_ref[:, lanes].astype(F32), moved_ref[:, other].astype(F32)
        pair_ref[0, :, lanes] = (a + b).astype(BF16)
        pair_ref[1, :, lanes] = (a - b).astype(BF16)
        return carry

    lax.fori_loop(0, HALF // 128, fold, 0)

    def to_waves(tile, carry):
        cols = pl.ds(pl.multiple_of(tile * 256, 256), 256)
        for par in range(2):
            out = dot_nt(pair_ref[par], table_ref[par, cols, :])
            out = out * scale_ref[par, 0:1, cols]
            for half in range(2):
                part = out[:, 128 * half : 128 * half + 128] * weight_ref[...]
                sums_ref[par, tile * 2 + half] = part
        return carry

    lax.fori_loop(0, TILES // 2, to_waves, 0)

    def scatter_rows(part, step, carry):
        tile = part * per_part + step
        lane = lax.broadcasted_iota(jnp.int32, (1, 128), 1)
        height = RUN * SUB
        halves = []
        for par in range(2):
            tiles = []
            for h in range(2):
                for f in range(FIELDS):
                    pieces = []
                    for k in range(RUN):
                        at = (f * RUN + k) * 16 + 8 * h
                        pieces.append(sums_ref[par, tile, at : at + 8, :])
                    tiles.append(jnp.concatenate(pieces, axis=0))
            halves.append(jnp.concatenate(swap_blocks(tiles, lane), axis=0))
        rows = pl.ds(pl.multiple_of(step * 8 * height, 8 * height), 8 * height)
        coef_refs[part][rows, :] = jnp.concatenate(halves, axis=1).astype(BF16)
        return carry

    for part in range(parts):
        lax.fori_loop(0, per_part, functools.partial(scatter_rows, part), 0)


def transport(sub, edge, recv, halo, perm, order, scale, weight, table, factors):
    parts = len(recv)
    rows, width = recv[0].shape
    lats = RUN * SUB
    left = FIELDS * (RUN + 1) * 16
    own = FIELDS * RUN * 16
    slots2 = table.shape[1]
    vmem = pl.BlockSpec(memory_space=pltpu.VMEM)
    anywhere = pl.BlockSpec(memory_space=pl.ANY)
    return pl.pallas_call(
        functools.partial(middle_kernel, sub, parts),
        out_shape=(
            jax.ShapeDtypeStruct((FIELDS, 2, lats, NLON), BF16),
            *[jax.ShapeDtypeStruct((rows, width), BF16)] * parts,
        ),
        in_specs=[pl.BlockSpec(memory_space=pltpu.SMEM)] + [vmem] * 5 + [anywhere] * 2 + [vmem] * parts,
        out_specs=(vmem,) * (parts + 1),
        scratch_shapes=[
            pltpu.VMEM((2, slots2, HALF), BF16),
            pltpu.VMEM((2,) + factors.shape[1:], BF16),
            pltpu.VMEM((2, left, slots2), BF16),
            pltpu.VMEM((left, 256), F32),
            pltpu.VMEM((left, 256), F32),
            pltpu.VMEM((FIELDS * REACH, 16, NLON), BF16),
            pltpu.VMEM((FIELDS * REACH, 16, CHUNK + 2 * RIM * 128), BF16),
            pltpu.VMEM((FINE, FIELDS * 2, lats, 128), F32),
            pltpu.VMEM((own, NLON), BF16),
            pltpu.VMEM((2, own, HALF), BF16),
            pltpu.VMEM((2, TILES, own, 128), F32),
            pltpu.SemaphoreType.DMA,
            pltpu.SemaphoreType.DMA((2,)),
        ],
        compiler_params=pltpu.CompilerParams(vmem_limit_bytes=VMEM_LIMIT),
        cost_estimate=pl.CostEstimate(
            flops=8 * left * slots2 * HALF,
            bytes_accessed=2 * rows * width * 8 + 4 * slots2 * HALF,
            transcendentals=0,
        ),
        name="transport",
    )(edge, halo, perm, order, scale, weight, table, factors, *recv)


def factor_kernel(depart_ref, pick_ref, order_ref, taps_ref, out_ref, code_ref):
    code = pick_ref[...] * 16 + depart_ref[...]
    code = code.reshape(2 * RUN * SUB, CHUNK).astype(F32).astype(BF16)
    code = jnp.dot(code, order_ref[...], preferred_element_type=F32).astype(jnp.int32)
    for j in range(FINE):
        code_ref[j] = code[:, 128 * j : 128 * j + 128]

    def points(j, carry):
        for k in range(RUN):
            index, column = [], []
            for h in range(2):
                code = code_ref[j, pl.ds(h * RUN * SUB + k, SUB, stride=RUN), :]
                index.append(code >> 2)
                column.append(code & 3)
            column = jnp.concatenate(column, axis=0).astype(F32).astype(BF16)
            hits = [column == jnp.asarray(d, BF16) for d in range(4)]
            for r in range(2 * RIM + 1):
                weights = []
                for b in range(4):
                    entry = taps_ref[r * 4 + b]
                    found = [jnp.take_along_axis(entry, index[h], axis=1) for h in range(2)]
                    weights.append(jnp.concatenate(found, axis=0).astype(BF16))
                for c in range(-RIM, RIM + 1):
                    factor = jnp.zeros((16, 128), BF16)
                    for d in range(4):
                        b = c - (d - 2) + 1
                        if 0 <= b < 4:
                            factor = jnp.where(hits[d], weights[b], factor)
                    out_ref[0, j, k, r * 7 + c + RIM] = factor
        return carry

    lax.fori_loop(0, FINE, points, 0)


def stencil_factors(depart, pick, order, taps):
    hemispheres, lats, longitudes = depart.shape
    chunks = longitudes // CHUNK
    shape = (FINE, RUN, REACH_TAPS, 16, 128)
    code = pl.BlockSpec((hemispheres, lats, CHUNK), lambda i: (0, 0, i))
    return pl.pallas_call(
        factor_kernel,
        out_shape=jax.ShapeDtypeStruct((chunks,) + shape, BF16),
        grid=(chunks,),
        in_specs=[
            code,
            code,
            pl.BlockSpec(order.shape, lambda i: (0, 0)),
            pl.BlockSpec(taps.shape, lambda i: (0, 0, 0)),
        ],
        out_specs=pl.BlockSpec((1,) + shape, lambda i: (i, 0, 0, 0, 0, 0)),
        scratch_shapes=[pltpu.VMEM((FINE, 2 * lats, 128), jnp.int32)],
        compiler_params=pltpu.CompilerParams(vmem_limit_bytes=VMEM_LIMIT),
        cost_estimate=pl.CostEstimate(
            flops=2 * REACH_TAPS * 4 * depart.size,
            bytes_accessed=2 * REACH_TAPS * depart.size,
            transcendentals=0,
        ),
        name="stencil_factors",
    )(depart, pick, order, taps)


def tap_tables(stencil_weight):
    choose = np.zeros((16, 7, 4, 4), np.float32)
    for r in range(7):
        for d in range(4):
            a = (r - 3) - (d - 2) + 1
            if 0 <= a < 4:
                for b in range(4):
                    choose[4 * a + b, r, b, d] = 1.0
    table = jnp.einsum("tw,wnd->ntd", stencil_weight, choose.reshape(16, 28, 4), precision="highest")
    table = jnp.pad(table.reshape(28, 4 * NSTEN), ((0, 0), (0, 128 - 4 * NSTEN)))
    return jnp.broadcast_to(table[:, None, :], (28, 8, 128))


def exchange(array, axis, distance):
    devices = lax.axis_size(axis)
    return lax.ppermute(array, axis, [(i, i ^ distance) for i in range(devices)])


def gather_rows(spectral):
    devices = lax.axis_size("band")
    band = lax.axis_index("band")
    turned = spectral.transpose(0, 2, 1)
    pieces = [turned] + [exchange(turned, "band", d) for d in range(1, devices)]
    stacked = jnp.stack(pieces)
    ordered = [
        lax.dynamic_index_in_dim(stacked, band ^ b, 0, keepdims=False) for b in range(devices)
    ]
    return jnp.concatenate(ordered, axis=2)


def scatter_sums(sums, slots, row_local):
    devices = lax.axis_size("band")
    band = lax.axis_index("band")
    shaped = sums.reshape(slots, COLS, -1)
    parts = jnp.stack(
        [shaped[:, :, b * row_local : (b + 1) * row_local] for b in range(devices)]
    )
    total = lax.dynamic_index_in_dim(parts, band, 0, keepdims=False).astype(F32)
    for d in range(1, devices):
        piece = lax.dynamic_index_in_dim(parts, band ^ d, 0, keepdims=False)
        total = total + exchange(piece, "band", d).astype(F32)
    return total.astype(BF16).transpose(0, 2, 1)


def per_device(
    spectral, legendre, slot_pair, quad_weight, depart_code, stencil_pick, stencil_weight
):
    slots, row_local, _ = spectral.shape
    height = depart_code.shape[2]
    waves = lax.axis_size("wave")
    sub = height // RUN
    groups = slots // GROUP
    wave_rank = lax.axis_index("wave")
    lat_rank = lax.axis_index(("band", "wave"))
    lat_devices = lax.axis_size(("band", "wave"))
    my_pairs = lax.dynamic_slice_in_dim(slot_pair, wave_rank * slots, slots)
    perm = lane_order()

    parts = 2 if groups % 2 == 0 else 1
    blocks = waves * groups
    arriving = slot_pair.reshape(waves, parts, -1).swapaxes(0, 1).reshape(-1)

    spec = gather_rows(spectral)
    table, scale = angle_tables(arriving)
    taps = tap_tables(stencil_weight)
    my_weight = lax.dynamic_slice_in_dim(quad_weight, wave_rank * height, height)
    weight = my_weight.reshape(sub, RUN).T
    if sub != SUB:
        weight = jnp.pad(weight, ((0, 0), (0, SUB - sub)))
    weight = jnp.broadcast_to(weight[None, :, None, :, None], (FIELDS, RUN, 2, SUB, 128))
    weight = weight.reshape(-1, 128)
    is_first, is_last = lat_rank == 0, lat_rank == lat_devices - 1
    edge = jnp.stack([is_first, is_last]).astype(jnp.int32)
    spec, table, scale, taps, weight, edge, my_pairs = lax.optimization_barrier(
        (spec, table, scale, taps, weight, edge, my_pairs)
    )
    depart, pick = depart_code[0], stencil_pick[0]
    if sub != SUB:
        gap = SUB - sub
        depart = jnp.pad(depart, ((0, 0), (0, RUN * gap), (0, 0)))
        pick = jnp.pad(pick, ((0, 0), (0, RUN * gap), (0, 0)))
    to_lanes, to_longitudes = longitude_order()
    received = []
    for part in range(parts):
        sent = legendre_forward(my_pairs, spec, legendre, waves, part, parts)
        if received:
            sent, received[-1] = lax.optimization_barrier((sent, received[-1]))
        if part == parts - 1:
            sent, depart = lax.optimization_barrier((sent, depart))
            factors = stencil_factors(depart, pick, to_lanes, taps)
        received.append(
            lax.all_to_all(sent, "wave", split_axis=0, concat_axis=0, tiled=True)
        )
    recv = [r.reshape(-1, height, WIDE) for r in received]
    first = jnp.concatenate([r[:, 0 : RIM * sub : sub] for r in recv])
    last = jnp.concatenate([r[:, (RUN - RIM + 1) * sub - 1 :: sub] for r in recv])
    up = [(i, i + 1) for i in range(lat_devices - 1)]
    down = [(i + 1, i) for i in range(lat_devices - 1)]
    before = lax.ppermute(last, ("band", "wave"), up)
    after = lax.ppermute(first, ("band", "wave"), down)
    halo = [jnp.where(is_first, first[:, RIM - 1 - i], before[:, i]) for i in range(RIM)]
    halo += [jnp.where(is_last, last[:, RIM - 1 - i], after[:, i]) for i in range(RIM)]
    halo += [jnp.zeros_like(halo[0])] * (8 - 2 * RIM)
    halo = jnp.stack(halo, axis=1).reshape(blocks * 8, WIDE)

    if sub != SUB:
        recv = [r.reshape(-1, RUN, sub, WIDE) for r in recv]
        recv = [jnp.pad(r, ((0, 0), (0, 0), (0, gap), (0, 0))) for r in recv]
    arrival, *coefs = transport(
        sub,
        edge,
        [r.reshape(-1, WIDE) for r in recv],
        halo,
        perm,
        to_longitudes,
        scale,
        weight,
        table,
        factors,
    )
    arrival = arrival[None, :, :, :height]
    coefs = [c.reshape(-1, RUN, SUB, WIDE)[:, :, :sub] for c in coefs]
    outs, by_wave = [], None
    for part in range(parts):
        leaving = coefs[part].reshape(waves, groups // parts, height, WIDE)
        if part:
            leaving, by_wave = lax.optimization_barrier((leaving, by_wave))
        ready = by_wave
        by_wave = lax.all_to_all(leaving, "wave", split_axis=0, concat_axis=0, tiled=True)
        if part:
            outs.append(legendre_backward(my_pairs, perm, ready, legendre, part - 1))
    outs.append(legendre_backward(my_pairs, perm, by_wave, legendre, parts - 1))
    outs = [scatter_sums(sums, slots // parts, row_local) for sums in outs]
    return (arrival, jnp.concatenate(outs))


def solution(mesh):
    in_specs = (
        P("wave", "band", None),
        P("wave", "band", None),
        P(),
        P("band"),
        P(None, None, ("band", "wave"), None),
        P(None, None, ("band", "wave"), None),
        P(),
    )
    out_specs = (P(None, None, None, ("band", "wave"), None), P("wave", "band", None))
    return jax.shard_map(
        per_device, mesh=mesh, in_specs=in_specs, out_specs=out_specs, check_vma=False
    )
```

```python
import functools
import math

import jax
import jax.numpy as jnp
import numpy as np
from jax import lax
from jax.experimental import pallas as pl
from jax.experimental.pallas import tpu as pltpu
from jax.sharding import PartitionSpec as P

M = 1280
NLON = 5120
HALF = NLON // 2
FIELDS = 4
NSTEN = 16
RIM = 3
COLS = 8
GROUP = 8
WIDE = GROUP * 4 * COLS
RUN = 5
SUB = 8
REACH = RUN + 2 * RIM
TILES = 10
CHUNK = 512
FINE = CHUNK // 128
CHUNKS = NLON // CHUNK
STEP = 8
F32 = jnp.float32
BF16 = jnp.bfloat16
VMEM_LIMIT = 60 * 2**20


def dot_nt(left, right):
    return lax.dot_general(left, right, (((1,), (1,)), ((), ())), preferred_element_type=F32)


def lane_order():
    index = np.arange(WIDE).reshape(GROUP, 2, 2, FIELDS, 2).transpose(1, 2, 3, 4, 0).reshape(-1)
    matrix = np.zeros((WIDE, WIDE), np.float32)
    matrix[index, np.arange(WIDE)] = 1.0
    return jnp.asarray(matrix, BF16)


def longitude_order():
    position = np.arange(CHUNK)
    longitude = FINE * (position % 128) + position // 128
    matrix = np.zeros((CHUNK, CHUNK), np.float32)
    matrix[longitude, position] = 1.0
    return jnp.asarray(np.stack([matrix, matrix.T]), BF16)


def row_masks(pair, rows):
    row = lax.broadcasted_iota(jnp.int32, (1, rows), 1)
    low_count = M - pair
    higher = row >= low_count
    degree = jnp.where(higher, row - low_count, row)
    sign = (1 - 2 * (degree & 1)).astype(F32)
    in_use = row <= M
    side = jnp.where(higher, 1, 0) ^ (pair & 1)
    even = jnp.where(in_use & (side == 0), 1.0, 0.0)
    odd = jnp.where(in_use & (side == 1), 1.0, 0.0)
    return even, odd, sign


def forward_kernel(height, base, pair_ref, spec_ref, leg_ref, out_ref, acc_ref):
    group, step = pl.program_id(0) + base, pl.program_id(1)
    rows = spec_ref.shape[2]
    sub = height // RUN

    pieces = []
    for u in range(STEP):
        even, odd, sign = row_masks(pair_ref[group * GROUP + step * STEP + u], rows)
        spec = spec_ref[u].astype(F32)
        south = spec * sign
        parts = [spec * even, south * even, spec * odd, south * odd]
        masked = jnp.concatenate(parts, axis=0).astype(BF16)
        pieces.append(dot_nt(leg_ref[u], masked))
    for half in range(STEP // 4):
        acc_ref[step * (STEP // 4) + half] = jnp.concatenate(pieces[4 * half : 4 * half + 4], axis=1)

    @pl.when(step == GROUP // STEP - 1)
    def _():
        for dest in range(out_ref.shape[0]):
            halves = []
            for half in range(2):
                pieces = [
                    acc_ref[half, pl.ds(dest * height + k, sub, stride=RUN), :]
                    for k in range(RUN)
                ]
                halves.append(jnp.concatenate(pieces, axis=0))
            out_ref[dest, 0] = jnp.concatenate(halves, axis=1).astype(BF16)


def legendre_forward(pairs, spec, legendre, waves, part, parts):
    slots, lats, rows = legendre.shape
    groups = slots // GROUP // parts
    base = part * groups
    height = lats // waves
    return pl.pallas_call(
        functools.partial(forward_kernel, height, base),
        out_shape=jax.ShapeDtypeStruct((waves, groups, height, WIDE), BF16),
        grid=(groups, GROUP // STEP),
        in_specs=[
            pl.BlockSpec(memory_space=pltpu.SMEM),
            pl.BlockSpec((STEP, COLS, rows), lambda g, t: (GROUP // STEP * (g + base) + t, 0, 0)),
            pl.BlockSpec((STEP, lats, rows), lambda g, t: (GROUP // STEP * (g + base) + t, 0, 0)),
        ],
        out_specs=pl.BlockSpec((waves, 1, height, WIDE), lambda g, t: (0, g, 0, 0)),
        scratch_shapes=[pltpu.VMEM((2, lats, 128), F32)],
        compiler_params=pltpu.CompilerParams(vmem_limit_bytes=VMEM_LIMIT),
        cost_estimate=pl.CostEstimate(
            flops=2 * groups * GROUP * lats * rows * 32,
            bytes_accessed=2 * groups * GROUP * lats * rows,
            transcendentals=0,
        ),
        name="legendre_forward",
    )(pairs, spec, legendre)


def backward_kernel(
    height, base, pair_ref, perm_ref, coef_ref, leg_ref, out_ref, rows_ref, turned_ref
):
    group, step = pl.program_id(0) + base, pl.program_id(1)
    rows = leg_ref.shape[2]
    sub = height // RUN

    @pl.when(step == 0)
    def _():
        for source in range(coef_ref.shape[0]):
            block = coef_ref[source, 0].astype(F32)
            for k in range(RUN):
                for half in range(2):
                    rows_ref[half, pl.ds(source * height + k, sub, stride=RUN), :] = block[
                        k * sub : (k + 1) * sub, 128 * half : 128 * half + 128
                    ]
        natural = jnp.concatenate([rows_ref[0], rows_ref[1]], axis=1).astype(BF16)
        turned_ref[...] = dot_nt(perm_ref[...], natural).astype(BF16)

    sums = []
    for u in range(STEP):
        even, odd, sign = row_masks(pair_ref[group * GROUP + step * STEP + u], rows)
        at = pl.ds(pl.multiple_of(step * (32 * STEP) + 32 * u, 32), 32)
        raw = jnp.dot(turned_ref[at, :], leg_ref[u], preferred_element_type=F32)
        low = raw[0:8] + sign * raw[8:16]
        high = raw[16:24] + sign * raw[24:32]
        sums.append(low * even + high * odd)
    out_ref[...] = jnp.concatenate(sums, axis=0).astype(BF16)


def legendre_backward(pairs, perm, coefs, legendre, part):
    _, lats, rows = legendre.shape
    waves, groups, height, _ = coefs.shape
    slots = groups * GROUP
    base = part * groups
    return pl.pallas_call(
        functools.partial(backward_kernel, height, base),
        out_shape=jax.ShapeDtypeStruct((slots * COLS, rows), BF16),
        grid=(groups, GROUP // STEP),
        in_specs=[
            pl.BlockSpec(memory_space=pltpu.SMEM),
            pl.BlockSpec((WIDE, WIDE), lambda g, t: (0, 0)),
            pl.BlockSpec((waves, 1, height, WIDE), lambda g, t: (0, g, 0, 0)),
            pl.BlockSpec((STEP, lats, rows), lambda g, t: (GROUP // STEP * (g + base) + t, 0, 0)),
        ],
        out_specs=pl.BlockSpec((STEP * COLS, rows), lambda g, t: (GROUP // STEP * g + t, 0)),
        scratch_shapes=[pltpu.VMEM((2, lats, 128), F32), pltpu.VMEM((WIDE, lats), BF16)],
        compiler_params=pltpu.CompilerParams(vmem_limit_bytes=VMEM_LIMIT),
        cost_estimate=pl.CostEstimate(
            flops=2 * slots * lats * rows * 32,
            bytes_accessed=2 * slots * lats * rows,
            transcendentals=0,
        ),
        name="legendre_backward",
    )(pairs, perm, coefs, legendre)


def table_kernel(cos_ref, sin_ref, step_ref, out_ref):
    batch = 4 * GROUP

    def rotate(c, s, step_c, step_s):
        return c * step_c - s * step_s, s * step_c + c * step_s

    def body(i, carry):
        rows = pl.ds(pl.multiple_of(i * batch, batch), batch)
        steps = step_ref[rows, :]
        steps = [jnp.broadcast_to(steps[:, n : n + 1], (batch, 128)) for n in range(4)]
        first = cos_ref[rows, :], sin_ref[rows, :]
        for j in range(FINE):
            c, s = first
            for chunk in range(HALF // CHUNK):
                at = chunk * CHUNK + j * 128
                parts = []
                for g in range(batch // GROUP):
                    parts += [c[GROUP * g : GROUP * g + GROUP], -s[GROUP * g : GROUP * g + GROUP]]
                to = pl.ds(pl.multiple_of(i * 2 * batch, 2 * batch), 2 * batch)
                out_ref[to, at : at + 128] = jnp.concatenate(parts, axis=0).astype(BF16)
                if chunk < HALF // CHUNK - 1:
                    c, s = rotate(c, s, *steps[2:])
            if j < FINE - 1:
                first = rotate(*first, *steps[:2])
        return carry

    lax.fori_loop(0, cos_ref.shape[0] // batch, body, 0)


def angle_tables(slot_pair):
    flipped = M - 1 - slot_pair
    odd = slot_pair % 2 == 1
    waves = jnp.concatenate([jnp.where(odd, flipped, slot_pair), jnp.where(odd, slot_pair, flipped)])
    factor = jnp.where(waves == 0, 1.0, 2.0).astype(F32)
    unit = 2.0 * math.pi / NLON

    def angle(columns):
        columns = jnp.asarray(columns, jnp.int32)
        return (waves[:, None] * columns[None, :] % NLON).astype(F32) * unit

    lanes = angle(FINE * np.arange(128))
    first_cos = factor[:, None] * jnp.cos(lanes)
    first_sin = factor[:, None] * jnp.sin(lanes)
    moves = angle([1, 1, CHUNK, CHUNK])
    steps = jnp.where(jnp.arange(4) % 2 == 0, jnp.cos(moves), jnp.sin(moves))
    count = waves.shape[0]
    table = pl.pallas_call(
        table_kernel,
        out_shape=jax.ShapeDtypeStruct((2 * count, HALF), BF16),
        grid=(count // 128,),
        in_specs=[
            pl.BlockSpec((128, 128), lambda i: (i, 0)),
            pl.BlockSpec((128, 128), lambda i: (i, 0)),
            pl.BlockSpec((128, 4), lambda i: (i, 0)),
        ],
        out_specs=pl.BlockSpec((256, HALF), lambda i: (i, 0)),
        cost_estimate=pl.CostEstimate(
            flops=6 * count * HALF, bytes_accessed=4 * count * HALF, transcendentals=0
        ),
        name="angle_tables",
    )(first_cos, first_sin, steps)
    scale = (1.0 / (factor * math.sqrt(NLON))).reshape(2, 1, -1, 1, GROUP)
    scale = jnp.broadcast_to(scale, (2, 8, count // 2 // GROUP, 2, GROUP))
    return table.reshape(2, count, HALF), scale.reshape(2, 8, count)


def swap_blocks(tiles, lane):
    tiles = list(tiles)
    for d in (4, 2, 1):
        low = (lane // (16 * d)) % 2 == 0
        for i in range(8):
            if i & d:
                continue
            a, b = tiles[i], tiles[i + d]
            tiles[i] = jnp.where(low, a, pltpu.roll(b, 16 * d, 1))
            tiles[i + d] = jnp.where(low, pltpu.roll(a, 128 - 16 * d, 1), b)
    return tiles


def middle_kernel(
    sub, parts, edge_ref, halo_ref, perm_ref, order_ref, taps_ref, scale_ref, weight_ref,
    table_hbm, depart_hbm, pick_hbm, *refs,
):
    recv_refs, arrival_ref, coef_refs = refs[:parts], refs[parts], refs[parts + 1 : 2 * parts + 1]
    (
        table_ref, depart_ref, pick_ref, left_ref, plus_ref, minus_ref, grid_ref, near_ref,
        stage_ref, code_ref, moved_ref, pair_ref, sums_ref, sems,
    ) = refs[2 * parts + 1 :]
    per_part = TILES // parts
    copies = [
        pltpu.make_async_copy(table_hbm, table_ref, sems.at[0]),
        pltpu.make_async_copy(depart_hbm, depart_ref, sems.at[1]),
        pltpu.make_async_copy(pick_hbm, pick_ref, sems.at[2]),
    ]
    for copy in copies:
        copy.start()
    own = FIELDS * RUN * 16
    is_first, is_last = edge_ref[0], edge_ref[1]

    def gather_rows(part, step, carry):
        tile = part * per_part + step
        lane = lax.broadcasted_iota(jnp.int32, (1, 128), 1)
        lanes = pl.ds(pl.multiple_of(tile * 128, 128), 128)
        height = RUN * SUB
        rows = pl.ds(pl.multiple_of(step * 8 * height, 8 * height), 8 * height)
        mixed = jnp.dot(recv_refs[part][rows, :], perm_ref[...], preferred_element_type=F32)
        edge_rows = pl.ds(pl.multiple_of(tile * 64, 64), 64)
        edges = jnp.dot(halo_ref[edge_rows, :], perm_ref[...], preferred_element_type=F32)
        for par in range(2):
            cols = slice(128 * par, 128 * par + 128)
            tiles = swap_blocks([mixed[b * height : (b + 1) * height, cols] for b in range(8)], lane)
            for f in range(FIELDS):
                for k in range(RUN):
                    at = (f * RUN + k) * 16
                    block = [tiles[h * 4 + f][8 * k : 8 * k + 8] for h in range(2)]
                    left_ref[par, at : at + 16, lanes] = jnp.concatenate(block, axis=0).astype(BF16)
            ends = swap_blocks([edges[8 * b : 8 * b + 8, cols] for b in range(8)], lane)
            row = lax.broadcasted_iota(jnp.int32, (8, 128), 0)
            if par == 1:
                sign = jnp.where((row < RIM) & (is_first == 1), -1.0, 1.0)
                ends = [end * sign for end in ends]
            across = (row >= RIM) & (is_last == 1)
            for f in range(FIELDS):
                block = [jnp.where(across, ends[(1 - h) * 4 + f], ends[h * 4 + f]) for h in range(2)]
                at = own + f * 16
                left_ref[par, at : at + 16, lanes] = jnp.concatenate(block, axis=0).astype(BF16)
        return carry

    for part in range(parts):
        lax.fori_loop(0, per_part, functools.partial(gather_rows, part), 0)
    copies[0].wait()

    def to_grid(tile, carry):
        cols = pl.ds(pl.multiple_of(tile * 256, 256), 256)
        even = jnp.dot(left_ref[0], table_ref[0, :, cols], preferred_element_type=F32)
        odd = jnp.dot(left_ref[1], table_ref[1, :, cols], preferred_element_type=F32)
        plus_ref[...] = even + odd
        minus_ref[...] = even - odd
        place = lax.broadcasted_iota(jnp.int32, (8, 256), 0)
        for side, ref in enumerate((plus_ref, minus_ref)):
            to = pl.ds(pl.multiple_of(side * HALF + tile * 256, 256), 256)
            for f in range(FIELDS):
                for k in range(RUN):
                    at = (f * RUN + k) * 16
                    grid_ref[f * REACH + RIM + k, :, to] = ref[at : at + 16, :]
                for k in range(RIM):
                    before, after = [], []
                    for h in range(2):
                        end = own + f * 16 + 8 * h
                        at = (f * RUN + k + RUN - RIM) * 16 + 8 * h
                        rolled = pltpu.roll(ref[at : at + 8, :], 1, 0)
                        before.append(jnp.where(place == 0, ref[end + k : end + k + 1, :], rolled))
                        at = (f * RUN + k) * 16 + 8 * h
                        rolled = pltpu.roll(ref[at : at + 8, :], 7, 0)
                        end = end + RIM
                        after.append(
                            jnp.where(place == sub - 1, ref[end + k : end + k + 1, :], rolled)
                        )
                    grid_ref[f * REACH + k, :, to] = jnp.concatenate(before, 0)
                    grid_ref[f * REACH + RIM + RUN + k, :, to] = jnp.concatenate(after, 0)
        return carry

    lax.fori_loop(0, HALF // 256, to_grid, 0)
    copies[1].wait()
    copies[2].wait()

    def interpolate(chunk, carry):
        lanes = pl.ds(pl.multiple_of(chunk * CHUNK, CHUNK), CHUNK)
        lane = lax.broadcasted_iota(jnp.int32, (16, 128), 1)
        previous = jnp.where(chunk == 0, CHUNKS - 1, chunk - 1)
        following = jnp.where(chunk == CHUNKS - 1, 0, chunk + 1)

        def neighbours(row, carry):
            for j in range(FINE):
                here = grid_ref[row, :, pl.ds(pl.multiple_of(chunk * CHUNK + j * 128, 128), 128)]
                near_ref[row, :, (RIM + j) * 128 : (RIM + j + 1) * 128] = here
                if j >= FINE - RIM:
                    at = pl.ds(pl.multiple_of(previous * CHUNK + j * 128, 128), 128)
                    mixed = pltpu.roll(jnp.where(lane == 127, grid_ref[row, :, at], here), 1, 1)
                    to = (j - (FINE - RIM)) * 128
                    near_ref[row, :, to : to + 128] = mixed
                if j < RIM:
                    at = pl.ds(pl.multiple_of(following * CHUNK + j * 128, 128), 128)
                    mixed = pltpu.roll(jnp.where(lane == 0, grid_ref[row, :, at], here), 127, 1)
                    to = (RIM + FINE + j) * 128
                    near_ref[row, :, to : to + 128] = mixed
            return carry

        lax.fori_loop(0, FIELDS * REACH, neighbours, 0, unroll=4)
        code = pick_ref[:, :, lanes] * 16 + depart_ref[:, :, lanes]
        code = code.reshape(2 * RUN * SUB, CHUNK).astype(F32).astype(BF16)
        code = jnp.dot(code, order_ref[0], preferred_element_type=F32).astype(jnp.int32)
        for j in range(FINE):
            code_ref[j] = code[:, 128 * j : 128 * j + 128]

        def points(j, carry):
            at_lanes = pl.ds(pl.multiple_of(chunk * CHUNK + j * 128, 128), 128)
            for ks in ((0, 1), (2, 3), (4,)):
                index, hits = {}, {}
                for k in ks:
                    codes = [
                        code_ref[j, pl.ds(h * RUN * SUB + k, SUB, stride=RUN), :] for h in range(2)
                    ]
                    index[k] = [code >> 2 for code in codes]
                    column = jnp.concatenate(codes, axis=0) & 3
                    hits[k] = [column == d for d in range(4)]
                totals = {}
                for row in range(ks[0], ks[-1] + 7):
                    factors = {}
                    for k in ks:
                        r = row - k
                        if not 0 <= r < 7:
                            continue
                        weights = []
                        for b in range(4):
                            entry = taps_ref[r * 4 + b]
                            found = [jnp.take_along_axis(entry, index[k][h], axis=1) for h in range(2)]
                            weights.append(jnp.concatenate(found, axis=0))
                        factors[k] = []
                        for c in range(-RIM, RIM + 1):
                            factor = jnp.zeros((16, 128), F32)
                            for d in range(4):
                                b = c - (d - 2) + 1
                                if 0 <= b < 4:
                                    factor = jnp.where(hits[k][d], weights[b], factor)
                            factors[k].append(factor)
                    for f in range(FIELDS):
                        for c in range(7):
                            lanes_c = pl.ds(pl.multiple_of((j + c) * 128, 128), 128)
                            near = near_ref[f * REACH + row, :, lanes_c]
                            for k in factors:
                                term = factors[k][c] * near
                                totals[f, k] = totals[f, k] + term if (f, k) in totals else term
                for f in range(FIELDS):
                    for k in ks:
                        at = (f * RUN + k) * 16
                        moved_ref[at : at + 16, at_lanes] = totals[f, k].astype(BF16)
            return carry

        lax.fori_loop(0, FINE, points, 0)
        natural = jnp.dot(moved_ref[:, lanes], order_ref[1], preferred_element_type=F32)
        for j in range(FINE):
            for f in range(FIELDS):
                for k in range(RUN):
                    for h in range(2):
                        at = (f * RUN + k) * 16 + 8 * h
                        stage_ref[j, f * 2 + h, pl.ds(k, SUB, stride=RUN), :] = natural[
                            at : at + 8, 128 * j : 128 * j + 128
                        ]
        for f in range(FIELDS):
            for h in range(2):
                rows = [stage_ref[j, f * 2 + h] for j in range(FINE)]
                arrival_ref[f, h, :, lanes] = jnp.concatenate(rows, axis=1).astype(BF16)
        return carry

    lax.fori_loop(0, CHUNKS, interpolate, 0)

    def fold(tile, carry):
        lanes = pl.ds(pl.multiple_of(tile * 128, 128), 128)
        other = pl.ds(pl.multiple_of(tile * 128 + HALF, 128), 128)
        a, b = moved_ref[:, lanes].astype(F32), moved_ref[:, other].astype(F32)
        pair_ref[0, :, lanes] = (a + b).astype(BF16)
        pair_ref[1, :, lanes] = (a - b).astype(BF16)
        return carry

    lax.fori_loop(0, HALF // 128, fold, 0)

    def to_waves(tile, carry):
        cols = pl.ds(pl.multiple_of(tile * 256, 256), 256)
        for par in range(2):
            out = dot_nt(pair_ref[par], table_ref[par, cols, :])
            out = out * scale_ref[par, 0:1, cols]
            for half in range(2):
                part = out[:, 128 * half : 128 * half + 128] * weight_ref[...]
                sums_ref[par, tile * 2 + half] = part
        return carry

    lax.fori_loop(0, TILES // 2, to_waves, 0)

    def scatter_rows(part, step, carry):
        tile = part * per_part + step
        lane = lax.broadcasted_iota(jnp.int32, (1, 128), 1)
        height = RUN * SUB
        halves = []
        for par in range(2):
            tiles = []
            for h in range(2):
                for f in range(FIELDS):
                    pieces = []
                    for k in range(RUN):
                        at = (f * RUN + k) * 16 + 8 * h
                        pieces.append(sums_ref[par, tile, at : at + 8, :])
                    tiles.append(jnp.concatenate(pieces, axis=0))
            halves.append(jnp.concatenate(swap_blocks(tiles, lane), axis=0))
        rows = pl.ds(pl.multiple_of(step * 8 * height, 8 * height), 8 * height)
        coef_refs[part][rows, :] = jnp.concatenate(halves, axis=1).astype(BF16)
        return carry

    for part in range(parts):
        lax.fori_loop(0, per_part, functools.partial(scatter_rows, part), 0)


def transport(sub, edge, recv, halo, perm, order, taps, scale, weight, table, depart, pick):
    parts = len(recv)
    rows, width = recv[0].shape
    lats = RUN * SUB
    left = FIELDS * (RUN + 1) * 16
    own = FIELDS * RUN * 16
    slots2 = table.shape[1]
    vmem = pl.BlockSpec(memory_space=pltpu.VMEM)
    anywhere = pl.BlockSpec(memory_space=pl.ANY)
    return pl.pallas_call(
        functools.partial(middle_kernel, sub, parts),
        out_shape=(
            jax.ShapeDtypeStruct((FIELDS, 2, lats, NLON), BF16),
            *[jax.ShapeDtypeStruct((rows, width), BF16)] * parts,
        ),
        in_specs=[pl.BlockSpec(memory_space=pltpu.SMEM)] + [vmem] * 6 + [anywhere] * 3 + [vmem] * parts,
        out_specs=(vmem,) * (parts + 1),
        scratch_shapes=[
            pltpu.VMEM((2, slots2, HALF), BF16),
            pltpu.VMEM((2, lats, NLON), jnp.int32),
            pltpu.VMEM((2, lats, NLON), jnp.int32),
            pltpu.VMEM((2, left, slots2), BF16),
            pltpu.VMEM((left, 256), F32),
            pltpu.VMEM((left, 256), F32),
            pltpu.VMEM((FIELDS * REACH, 16, NLON), F32),
            pltpu.VMEM((FIELDS * REACH, 16, CHUNK + 2 * RIM * 128), F32),
            pltpu.VMEM((FINE, FIELDS * 2, lats, 128), F32),
            pltpu.VMEM((FINE, 2 * lats, 128), jnp.int32),
            pltpu.VMEM((own, NLON), BF16),
            pltpu.VMEM((2, own, HALF), BF16),
            pltpu.VMEM((2, TILES, own, 128), F32),
            pltpu.SemaphoreType.DMA((3,)),
        ],
        compiler_params=pltpu.CompilerParams(vmem_limit_bytes=VMEM_LIMIT),
        cost_estimate=pl.CostEstimate(
            flops=8 * left * slots2 * HALF,
            bytes_accessed=2 * rows * width * 8 + 4 * slots2 * HALF,
            transcendentals=0,
        ),
        name="transport",
    )(edge, halo, perm, order, taps, scale, weight, table, depart, pick, *recv)


def tap_tables(stencil_weight):
    choose = np.zeros((16, 7, 4, 4), np.float32)
    for r in range(7):
        for d in range(4):
            a = (r - 3) - (d - 2) + 1
            if 0 <= a < 4:
                for b in range(4):
                    choose[4 * a + b, r, b, d] = 1.0
    table = jnp.einsum("tw,wnd->ntd", stencil_weight, choose.reshape(16, 28, 4), precision="highest")
    table = jnp.pad(table.reshape(28, 4 * NSTEN), ((0, 0), (0, 128 - 4 * NSTEN)))
    return jnp.broadcast_to(table[:, None, :], (28, 8, 128))


def exchange(array, axis, distance):
    devices = lax.axis_size(axis)
    return lax.ppermute(array, axis, [(i, i ^ distance) for i in range(devices)])


def gather_rows(spectral):
    devices = lax.axis_size("band")
    band = lax.axis_index("band")
    turned = spectral.transpose(0, 2, 1)
    pieces = [turned] + [exchange(turned, "band", d) for d in range(1, devices)]
    stacked = jnp.stack(pieces)
    ordered = [
        lax.dynamic_index_in_dim(stacked, band ^ b, 0, keepdims=False) for b in range(devices)
    ]
    return jnp.concatenate(ordered, axis=2)


def scatter_sums(sums, slots, row_local):
    devices = lax.axis_size("band")
    band = lax.axis_index("band")
    shaped = sums.reshape(slots, COLS, -1)
    parts = jnp.stack(
        [shaped[:, :, b * row_local : (b + 1) * row_local] for b in range(devices)]
    )
    total = lax.dynamic_index_in_dim(parts, band, 0, keepdims=False).astype(F32)
    for d in range(1, devices):
        piece = lax.dynamic_index_in_dim(parts, band ^ d, 0, keepdims=False)
        total = total + exchange(piece, "band", d).astype(F32)
    return total.astype(BF16).transpose(0, 2, 1)


def per_device(
    spectral, legendre, slot_pair, quad_weight, depart_code, stencil_pick, stencil_weight
):
    slots, row_local, _ = spectral.shape
    height = depart_code.shape[2]
    waves = lax.axis_size("wave")
    sub = height // RUN
    groups = slots // GROUP
    wave_rank = lax.axis_index("wave")
    lat_rank = lax.axis_index(("band", "wave"))
    lat_devices = lax.axis_size(("band", "wave"))
    my_pairs = lax.dynamic_slice_in_dim(slot_pair, wave_rank * slots, slots)
    perm = lane_order()

    parts = 2 if groups % 2 == 0 else 1
    blocks = waves * groups
    arriving = slot_pair.reshape(waves, parts, -1).swapaxes(0, 1).reshape(-1)

    spec = gather_rows(spectral)
    table, scale = angle_tables(arriving)
    taps = tap_tables(stencil_weight)
    my_weight = lax.dynamic_slice_in_dim(quad_weight, wave_rank * height, height)
    weight = my_weight.reshape(sub, RUN).T
    if sub != SUB:
        weight = jnp.pad(weight, ((0, 0), (0, SUB - sub)))
    weight = jnp.broadcast_to(weight[None, :, None, :, None], (FIELDS, RUN, 2, SUB, 128))
    weight = weight.reshape(-1, 128)
    is_first, is_last = lat_rank == 0, lat_rank == lat_devices - 1
    edge = jnp.stack([is_first, is_last]).astype(jnp.int32)
    spec, table, scale, taps, weight, edge, my_pairs = lax.optimization_barrier(
        (spec, table, scale, taps, weight, edge, my_pairs)
    )
    received = []
    for part in range(parts):
        sent = legendre_forward(my_pairs, spec, legendre, waves, part, parts)
        if received:
            sent, received[-1] = lax.optimization_barrier((sent, received[-1]))
        received.append(
            lax.all_to_all(sent, "wave", split_axis=0, concat_axis=0, tiled=True)
        )
    recv = [r.reshape(-1, height, WIDE) for r in received]
    first = jnp.concatenate([r[:, 0 : RIM * sub : sub] for r in recv])
    last = jnp.concatenate([r[:, (RUN - RIM + 1) * sub - 1 :: sub] for r in recv])
    up = [(i, i + 1) for i in range(lat_devices - 1)]
    down = [(i + 1, i) for i in range(lat_devices - 1)]
    before = lax.ppermute(last, ("band", "wave"), up)
    after = lax.ppermute(first, ("band", "wave"), down)
    halo = [jnp.where(is_first, first[:, RIM - 1 - i], before[:, i]) for i in range(RIM)]
    halo += [jnp.where(is_last, last[:, RIM - 1 - i], after[:, i]) for i in range(RIM)]
    halo += [jnp.zeros_like(halo[0])] * (8 - 2 * RIM)
    halo = jnp.stack(halo, axis=1).reshape(blocks * 8, WIDE)

    depart, pick = depart_code[0], stencil_pick[0]
    if sub != SUB:
        gap = SUB - sub
        recv = [r.reshape(-1, RUN, sub, WIDE) for r in recv]
        recv = [jnp.pad(r, ((0, 0), (0, 0), (0, gap), (0, 0))) for r in recv]
        depart = jnp.pad(depart, ((0, 0), (0, RUN * gap), (0, 0)))
        pick = jnp.pad(pick, ((0, 0), (0, RUN * gap), (0, 0)))
    arrival, *coefs = transport(
        sub,
        edge,
        [r.reshape(-1, WIDE) for r in recv],
        halo,
        perm,
        longitude_order(),
        taps,
        scale,
        weight,
        table,
        depart,
        pick,
    )
    arrival = arrival[None, :, :, :height]
    coefs = [c.reshape(-1, RUN, SUB, WIDE)[:, :, :sub] for c in coefs]
    outs, by_wave = [], None
    for part in range(parts):
        leaving = coefs[part].reshape(waves, groups // parts, height, WIDE)
        if part:
            leaving, by_wave = lax.optimization_barrier((leaving, by_wave))
        ready = by_wave
        by_wave = lax.all_to_all(leaving, "wave", split_axis=0, concat_axis=0, tiled=True)
        if part:
            outs.append(legendre_backward(my_pairs, perm, ready, legendre, part - 1))
    outs.append(legendre_backward(my_pairs, perm, by_wave, legendre, parts - 1))
    outs = [scatter_sums(sums, slots // parts, row_local) for sums in outs]
    return (arrival, jnp.concatenate(outs))


def solution(mesh):
    in_specs = (
        P("wave", "band", None),
        P("wave", "band", None),
        P(),
        P("band"),
        P(None, None, ("band", "wave"), None),
        P(None, None, ("band", "wave"), None),
        P(),
    )
    out_specs = (P(None, None, None, ("band", "wave"), None), P("wave", "band", None))
    return jax.shard_map(
        per_device, mesh=mesh, in_specs=in_specs, out_specs=out_specs, check_vma=False
    )
```

```python
import functools
import math

import jax
import jax.numpy as jnp
import numpy as np
from jax import lax
from jax.experimental import pallas as pl
from jax.experimental.pallas import tpu as pltpu
from jax.sharding import PartitionSpec as P

M = 1280
NLON = 5120
HALF = NLON // 2
FIELDS = 4
NSTEN = 16
RIM = 3
COLS = 8
GROUP = 8
WIDE = GROUP * 4 * COLS
RUN = 5
SUB = 8
REACH = RUN + 2 * RIM
TILES = 10
CHUNK = 512
FINE = CHUNK // 128
CHUNKS = NLON // CHUNK
STEP = 8
F32 = jnp.float32
BF16 = jnp.bfloat16
VMEM_LIMIT = 60 * 2**20


def dot_nt(left, right):
    return lax.dot_general(left, right, (((1,), (1,)), ((), ())), preferred_element_type=F32)


def lane_order():
    index = np.arange(WIDE).reshape(GROUP, 2, 2, FIELDS, 2).transpose(1, 2, 3, 4, 0).reshape(-1)
    matrix = np.zeros((WIDE, WIDE), np.float32)
    matrix[index, np.arange(WIDE)] = 1.0
    return jnp.asarray(matrix, BF16)


def longitude_order():
    position = np.arange(CHUNK)
    longitude = FINE * (position % 128) + position // 128
    matrix = np.zeros((CHUNK, CHUNK), np.float32)
    matrix[longitude, position] = 1.0
    return jnp.asarray(np.stack([matrix, matrix.T]), BF16)


def row_masks(pair, rows):
    row = lax.broadcasted_iota(jnp.int32, (1, rows), 1)
    low_count = M - pair
    higher = row >= low_count
    degree = jnp.where(higher, row - low_count, row)
    sign = (1 - 2 * (degree & 1)).astype(F32)
    in_use = row <= M
    side = jnp.where(higher, 1, 0) ^ (pair & 1)
    even = jnp.where(in_use & (side == 0), 1.0, 0.0)
    odd = jnp.where(in_use & (side == 1), 1.0, 0.0)
    return even, odd, sign


def forward_kernel(height, base, pair_ref, spec_ref, leg_ref, out_ref, acc_ref):
    group, step = pl.program_id(0) + base, pl.program_id(1)
    rows = spec_ref.shape[2]
    sub = height // RUN

    pieces = []
    for u in range(STEP):
        even, odd, sign = row_masks(pair_ref[group * GROUP + step * STEP + u], rows)
        spec = spec_ref[u].astype(F32)
        south = spec * sign
        parts = [spec * even, south * even, spec * odd, south * odd]
        masked = jnp.concatenate(parts, axis=0).astype(BF16)
        pieces.append(dot_nt(leg_ref[u], masked))
    for half in range(STEP // 4):
        acc_ref[step * (STEP // 4) + half] = jnp.concatenate(pieces[4 * half : 4 * half + 4], axis=1)

    @pl.when(step == GROUP // STEP - 1)
    def _():
        for dest in range(out_ref.shape[0]):
            halves = []
            for half in range(2):
                pieces = [
                    acc_ref[half, pl.ds(dest * height + k, sub, stride=RUN), :]
                    for k in range(RUN)
                ]
                halves.append(jnp.concatenate(pieces, axis=0))
            out_ref[dest, 0] = jnp.concatenate(halves, axis=1).astype(BF16)


def legendre_forward(pairs, spec, legendre, waves, part, parts):
    slots, lats, rows = legendre.shape
    groups = slots // GROUP // parts
    base = part * groups
    height = lats // waves
    return pl.pallas_call(
        functools.partial(forward_kernel, height, base),
        out_shape=jax.ShapeDtypeStruct((waves, groups, height, WIDE), BF16),
        grid=(groups, GROUP // STEP),
        in_specs=[
            pl.BlockSpec(memory_space=pltpu.SMEM),
            pl.BlockSpec((STEP, COLS, rows), lambda g, t: (GROUP // STEP * (g + base) + t, 0, 0)),
            pl.BlockSpec((STEP, lats, rows), lambda g, t: (GROUP // STEP * (g + base) + t, 0, 0)),
        ],
        out_specs=pl.BlockSpec((waves, 1, height, WIDE), lambda g, t: (0, g, 0, 0)),
        scratch_shapes=[pltpu.VMEM((2, lats, 128), F32)],
        compiler_params=pltpu.CompilerParams(vmem_limit_bytes=VMEM_LIMIT),
        cost_estimate=pl.CostEstimate(
            flops=2 * groups * GROUP * lats * rows * 32,
            bytes_accessed=2 * groups * GROUP * lats * rows,
            transcendentals=0,
        ),
        name="legendre_forward",
    )(pairs, spec, legendre)


def backward_kernel(
    height, base, pair_ref, perm_ref, coef_ref, leg_ref, out_ref, rows_ref, turned_ref
):
    group, step = pl.program_id(0) + base, pl.program_id(1)
    rows = leg_ref.shape[2]
    sub = height // RUN

    @pl.when(step == 0)
    def _():
        for source in range(coef_ref.shape[0]):
            block = coef_ref[source, 0].astype(F32)
            for k in range(RUN):
                for half in range(2):
                    rows_ref[half, pl.ds(source * height + k, sub, stride=RUN), :] = block[
                        k * sub : (k + 1) * sub, 128 * half : 128 * half + 128
                    ]
        natural = jnp.concatenate([rows_ref[0], rows_ref[1]], axis=1).astype(BF16)
        turned_ref[...] = dot_nt(perm_ref[...], natural).astype(BF16)

    sums = []
    for u in range(STEP):
        even, odd, sign = row_masks(pair_ref[group * GROUP + step * STEP + u], rows)
        at = pl.ds(pl.multiple_of(step * (32 * STEP) + 32 * u, 32), 32)
        raw = jnp.dot(turned_ref[at, :], leg_ref[u], preferred_element_type=F32)
        low = raw[0:8] + sign * raw[8:16]
        high = raw[16:24] + sign * raw[24:32]
        sums.append(low * even + high * odd)
    out_ref[...] = jnp.concatenate(sums, axis=0).astype(BF16)


def legendre_backward(pairs, perm, coefs, legendre, part):
    _, lats, rows = legendre.shape
    waves, groups, height, _ = coefs.shape
    slots = groups * GROUP
    base = part * groups
    return pl.pallas_call(
        functools.partial(backward_kernel, height, base),
        out_shape=jax.ShapeDtypeStruct((slots * COLS, rows), BF16),
        grid=(groups, GROUP // STEP),
        in_specs=[
            pl.BlockSpec(memory_space=pltpu.SMEM),
            pl.BlockSpec((WIDE, WIDE), lambda g, t: (0, 0)),
            pl.BlockSpec((waves, 1, height, WIDE), lambda g, t: (0, g, 0, 0)),
            pl.BlockSpec((STEP, lats, rows), lambda g, t: (GROUP // STEP * (g + base) + t, 0, 0)),
        ],
        out_specs=pl.BlockSpec((STEP * COLS, rows), lambda g, t: (GROUP // STEP * g + t, 0)),
        scratch_shapes=[pltpu.VMEM((2, lats, 128), F32), pltpu.VMEM((WIDE, lats), BF16)],
        compiler_params=pltpu.CompilerParams(vmem_limit_bytes=VMEM_LIMIT),
        cost_estimate=pl.CostEstimate(
            flops=2 * slots * lats * rows * 32,
            bytes_accessed=2 * slots * lats * rows,
            transcendentals=0,
        ),
        name="legendre_backward",
    )(pairs, perm, coefs, legendre)


def table_kernel(cos_ref, sin_ref, step_ref, out_ref):
    batch = 4 * GROUP

    def rotate(c, s, step_c, step_s):
        return c * step_c - s * step_s, s * step_c + c * step_s

    def body(i, carry):
        rows = pl.ds(pl.multiple_of(i * batch, batch), batch)
        steps = step_ref[rows, :]
        steps = [jnp.broadcast_to(steps[:, n : n + 1], (batch, 128)) for n in range(4)]
        first = cos_ref[rows, :], sin_ref[rows, :]
        for j in range(FINE):
            c, s = first
            for chunk in range(HALF // CHUNK):
                at = chunk * CHUNK + j * 128
                parts = []
                for g in range(batch // GROUP):
                    parts += [c[GROUP * g : GROUP * g + GROUP], -s[GROUP * g : GROUP * g + GROUP]]
                to = pl.ds(pl.multiple_of(i * 2 * batch, 2 * batch), 2 * batch)
                out_ref[to, at : at + 128] = jnp.concatenate(parts, axis=0).astype(BF16)
                if chunk < HALF // CHUNK - 1:
                    c, s = rotate(c, s, *steps[2:])
            if j < FINE - 1:
                first = rotate(*first, *steps[:2])
        return carry

    lax.fori_loop(0, cos_ref.shape[0] // batch, body, 0)


def angle_tables(slot_pair):
    flipped = M - 1 - slot_pair
    odd = slot_pair % 2 == 1
    waves = jnp.concatenate([jnp.where(odd, flipped, slot_pair), jnp.where(odd, slot_pair, flipped)])
    factor = jnp.where(waves == 0, 1.0, 2.0).astype(F32)
    unit = 2.0 * math.pi / NLON

    def angle(columns):
        columns = jnp.asarray(columns, jnp.int32)
        return (waves[:, None] * columns[None, :] % NLON).astype(F32) * unit

    lanes = angle(FINE * np.arange(128))
    first_cos = factor[:, None] * jnp.cos(lanes)
    first_sin = factor[:, None] * jnp.sin(lanes)
    moves = angle([1, 1, CHUNK, CHUNK])
    steps = jnp.where(jnp.arange(4) % 2 == 0, jnp.cos(moves), jnp.sin(moves))
    count = waves.shape[0]
    table = pl.pallas_call(
        table_kernel,
        out_shape=jax.ShapeDtypeStruct((2 * count, HALF), BF16),
        grid=(count // 128,),
        in_specs=[
            pl.BlockSpec((128, 128), lambda i: (i, 0)),
            pl.BlockSpec((128, 128), lambda i: (i, 0)),
            pl.BlockSpec((128, 4), lambda i: (i, 0)),
        ],
        out_specs=pl.BlockSpec((256, HALF), lambda i: (i, 0)),
        cost_estimate=pl.CostEstimate(
            flops=6 * count * HALF, bytes_accessed=4 * count * HALF, transcendentals=0
        ),
        name="angle_tables",
    )(first_cos, first_sin, steps)
    scale = (1.0 / (factor * math.sqrt(NLON))).reshape(2, 1, -1, 1, GROUP)
    scale = jnp.broadcast_to(scale, (2, 8, count // 2 // GROUP, 2, GROUP))
    return table.reshape(2, count, HALF), scale.reshape(2, 8, count)


def swap_blocks(tiles, lane):
    tiles = list(tiles)
    for d in (4, 2, 1):
        low = (lane // (16 * d)) % 2 == 0
        for i in range(8):
            if i & d:
                continue
            a, b = tiles[i], tiles[i + d]
            tiles[i] = jnp.where(low, a, pltpu.roll(b, 16 * d, 1))
            tiles[i + d] = jnp.where(low, pltpu.roll(a, 128 - 16 * d, 1), b)
    return tiles


def middle_kernel(
    sub, parts, edge_ref, halo_ref, perm_ref, order_ref, taps_ref, scale_ref, weight_ref,
    table_hbm, depart_hbm, pick_hbm, *refs,
):
    recv_refs, arrival_ref, coef_refs = refs[:parts], refs[parts], refs[parts + 1 : 2 * parts + 1]
    (
        table_ref, depart_ref, pick_ref, left_ref, plus_ref, minus_ref, grid_ref, near_ref,
        stage_ref, code_ref, tap_ref, shift_ref, moved_ref, pair_ref, sums_ref, sems,
    ) = refs[2 * parts + 1 :]
    per_part = TILES // parts
    copies = [
        pltpu.make_async_copy(table_hbm, table_ref, sems.at[0]),
        pltpu.make_async_copy(depart_hbm, depart_ref, sems.at[1]),
        pltpu.make_async_copy(pick_hbm, pick_ref, sems.at[2]),
    ]
    for copy in copies:
        copy.start()
    own = FIELDS * RUN * 16
    is_first, is_last = edge_ref[0], edge_ref[1]

    def gather_rows(part, step, carry):
        tile = part * per_part + step
        lane = lax.broadcasted_iota(jnp.int32, (1, 128), 1)
        lanes = pl.ds(pl.multiple_of(tile * 128, 128), 128)
        height = RUN * SUB
        rows = pl.ds(pl.multiple_of(step * 8 * height, 8 * height), 8 * height)
        mixed = jnp.dot(recv_refs[part][rows, :], perm_ref[...], preferred_element_type=F32)
        edge_rows = pl.ds(pl.multiple_of(tile * 64, 64), 64)
        edges = jnp.dot(halo_ref[edge_rows, :], perm_ref[...], preferred_element_type=F32)
        for par in range(2):
            cols = slice(128 * par, 128 * par + 128)
            tiles = swap_blocks([mixed[b * height : (b + 1) * height, cols] for b in range(8)], lane)
            for f in range(FIELDS):
                for k in range(RUN):
                    at = (f * RUN + k) * 16
                    block = [tiles[h * 4 + f][8 * k : 8 * k + 8] for h in range(2)]
                    left_ref[par, at : at + 16, lanes] = jnp.concatenate(block, axis=0).astype(BF16)
            ends = swap_blocks([edges[8 * b : 8 * b + 8, cols] for b in range(8)], lane)
            row = lax.broadcasted_iota(jnp.int32, (8, 128), 0)
            if par == 1:
                sign = jnp.where((row < RIM) & (is_first == 1), -1.0, 1.0)
                ends = [end * sign for end in ends]
            across = (row >= RIM) & (is_last == 1)
            for f in range(FIELDS):
                block = [jnp.where(across, ends[(1 - h) * 4 + f], ends[h * 4 + f]) for h in range(2)]
                at = own + f * 16
                left_ref[par, at : at + 16, lanes] = jnp.concatenate(block, axis=0).astype(BF16)
        return carry

    for part in range(parts):
        lax.fori_loop(0, per_part, functools.partial(gather_rows, part), 0)
    copies[0].wait()

    def to_grid(tile, carry):
        cols = pl.ds(pl.multiple_of(tile * 256, 256), 256)
        even = jnp.dot(left_ref[0], table_ref[0, :, cols], preferred_element_type=F32)
        odd = jnp.dot(left_ref[1], table_ref[1, :, cols], preferred_element_type=F32)
        plus_ref[...] = even + odd
        minus_ref[...] = even - odd
        place = lax.broadcasted_iota(jnp.int32, (8, 256), 0)
        for side, ref in enumerate((plus_ref, minus_ref)):
            to = pl.ds(pl.multiple_of(side * HALF + tile * 256, 256), 256)
            for f in range(FIELDS):
                for k in range(RUN):
                    at = (f * RUN + k) * 16
                    grid_ref[f * REACH + RIM + k, :, to] = ref[at : at + 16, :].astype(BF16)
                for k in range(RIM):
                    before, after = [], []
                    for h in range(2):
                        end = own + f * 16 + 8 * h
                        at = (f * RUN + k + RUN - RIM) * 16 + 8 * h
                        rolled = pltpu.roll(ref[at : at + 8, :], 1, 0)
                        before.append(jnp.where(place == 0, ref[end + k : end + k + 1, :], rolled))
                        at = (f * RUN + k) * 16 + 8 * h
                        rolled = pltpu.roll(ref[at : at + 8, :], 7, 0)
                        end = end + RIM
                        after.append(
                            jnp.where(place == sub - 1, ref[end + k : end + k + 1, :], rolled)
                        )
                    grid_ref[f * REACH + k, :, to] = jnp.concatenate(before, 0).astype(BF16)
                    grid_ref[f * REACH + RIM + RUN + k, :, to] = jnp.concatenate(after, 0).astype(
                        BF16
                    )
        return carry

    lax.fori_loop(0, HALF // 256, to_grid, 0)
    copies[1].wait()
    copies[2].wait()

    def interpolate(chunk, carry):
        lanes = pl.ds(pl.multiple_of(chunk * CHUNK, CHUNK), CHUNK)
        lane = lax.broadcasted_iota(jnp.int32, (16, 128), 1)
        previous = jnp.where(chunk == 0, CHUNKS - 1, chunk - 1)
        following = jnp.where(chunk == CHUNKS - 1, 0, chunk + 1)

        def neighbours(row, carry):
            for j in range(FINE):
                here = grid_ref[row, :, pl.ds(pl.multiple_of(chunk * CHUNK + j * 128, 128), 128)]
                near_ref[row, :, (RIM + j) * 128 : (RIM + j + 1) * 128] = here
                here = here.astype(F32)
                if j >= FINE - RIM:
                    at = pl.ds(pl.multiple_of(previous * CHUNK + j * 128, 128), 128)
                    there = grid_ref[row, :, at].astype(F32)
                    mixed = pltpu.roll(jnp.where(lane == 127, there, here), 1, 1)
                    slot = j - (FINE - RIM)
                    near_ref[row, :, slot * 128 : slot * 128 + 128] = mixed.astype(BF16)
                if j < RIM:
                    at = pl.ds(pl.multiple_of(following * CHUNK + j * 128, 128), 128)
                    there = grid_ref[row, :, at].astype(F32)
                    mixed = pltpu.roll(jnp.where(lane == 0, there, here), 127, 1)
                    slot = RIM + FINE + j
                    near_ref[row, :, slot * 128 : slot * 128 + 128] = mixed.astype(BF16)
            return carry

        lax.fori_loop(0, FIELDS * REACH, neighbours, 0, unroll=4)
        code = pick_ref[:, :, lanes] * 16 + depart_ref[:, :, lanes]
        code = code.reshape(2 * RUN * SUB, CHUNK).astype(F32).astype(BF16)
        code = jnp.dot(code, order_ref[0], preferred_element_type=F32).astype(jnp.int32)
        for j in range(FINE):
            code_ref[j] = code[:, 128 * j : 128 * j + 128]

        def weigh(j, carry):
            for k in range(RUN):
                codes = [
                    code_ref[j, pl.ds(h * RUN * SUB + k, SUB, stride=RUN), :] for h in range(2)
                ]
                codes = jnp.concatenate(codes, axis=0)
                pick = (codes >> 4).astype(F32).astype(BF16)
                one, zero = jnp.ones((16, 128), BF16), jnp.zeros((16, 128), BF16)
                picked = [jnp.where(pick == jnp.asarray(t, BF16), one, zero) for t in range(NSTEN)]
                found = jnp.dot(
                    taps_ref[...], jnp.concatenate(picked, axis=0), preferred_element_type=F32
                )
                tap_ref[j, k] = found.astype(BF16)
                shift_ref[j, k, 0] = ((codes >> 2) & 3).astype(F32).astype(BF16)
                shift_ref[j, k, 1] = (codes & 3).astype(F32).astype(BF16)
            return carry

        lax.fori_loop(0, FINE, weigh, 0)

        def choose(hits, values):
            if len(values) == 4:
                result, rest = values[3][1], values[:3]
            else:
                result, rest = jnp.zeros((16, 128), BF16), values
            for d, value in rest:
                result = jnp.where(hits[d], value, result)
            return result

        def points(j, carry):
            at_lanes = pl.ds(pl.multiple_of(chunk * CHUNK + j * 128, 128), 128)
            for k in range(RUN):
                row_step, column_step = shift_ref[j, k, 0], shift_ref[j, k, 1]
                row_hits = [row_step == jnp.asarray(d, BF16) for d in range(4)]
                hits = [column_step == jnp.asarray(d, BF16) for d in range(4)]
                totals = [jnp.zeros((16, 128), F32) for _ in range(FIELDS)]
                for r in range(7):
                    weights = []
                    for b in range(4):
                        values = []
                        for d in range(4):
                            a = r - d
                            if 0 <= a < 4:
                                at = (4 * a + b) * 16
                                values.append((d, tap_ref[j, k, at : at + 16, :]))
                        weights.append(choose(row_hits, values))
                    factors = []
                    for c in range(7):
                        values = [(d, weights[c - d]) for d in range(4) if 0 <= c - d < 4]
                        factors.append(choose(hits, values))
                    for f in range(FIELDS):
                        row = f * REACH + k + r
                        part = None
                        for c in range(7):
                            near = near_ref[row, :, pl.ds(pl.multiple_of((j + c) * 128, 128), 128)]
                            part = factors[c] * near if part is None else part + factors[c] * near
                        totals[f] = totals[f] + part.astype(F32)
                for f in range(FIELDS):
                    at = (f * RUN + k) * 16
                    moved_ref[at : at + 16, at_lanes] = totals[f].astype(BF16)
            return carry

        lax.fori_loop(0, FINE, points, 0)
        natural = jnp.dot(moved_ref[:, lanes], order_ref[1], preferred_element_type=F32)
        for j in range(FINE):
            for f in range(FIELDS):
                for k in range(RUN):
                    for h in range(2):
                        at = (f * RUN + k) * 16 + 8 * h
                        stage_ref[j, f * 2 + h, pl.ds(k, SUB, stride=RUN), :] = natural[
                            at : at + 8, 128 * j : 128 * j + 128
                        ]
        for f in range(FIELDS):
            for h in range(2):
                rows = [stage_ref[j, f * 2 + h] for j in range(FINE)]
                arrival_ref[f, h, :, lanes] = jnp.concatenate(rows, axis=1).astype(BF16)
        return carry

    lax.fori_loop(0, CHUNKS, interpolate, 0)

    def fold(tile, carry):
        lanes = pl.ds(pl.multiple_of(tile * 128, 128), 128)
        other = pl.ds(pl.multiple_of(tile * 128 + HALF, 128), 128)
        a, b = moved_ref[:, lanes].astype(F32), moved_ref[:, other].astype(F32)
        pair_ref[0, :, lanes] = (a + b).astype(BF16)
        pair_ref[1, :, lanes] = (a - b).astype(BF16)
        return carry

    lax.fori_loop(0, HALF // 128, fold, 0)

    def to_waves(tile, carry):
        cols = pl.ds(pl.multiple_of(tile * 256, 256), 256)
        for par in range(2):
            out = dot_nt(pair_ref[par], table_ref[par, cols, :])
            out = out * scale_ref[par, 0:1, cols]
            for half in range(2):
                part = out[:, 128 * half : 128 * half + 128] * weight_ref[...]
                sums_ref[par, tile * 2 + half] = part
        return carry

    lax.fori_loop(0, TILES // 2, to_waves, 0)

    def scatter_rows(part, step, carry):
        tile = part * per_part + step
        lane = lax.broadcasted_iota(jnp.int32, (1, 128), 1)
        height = RUN * SUB
        halves = []
        for par in range(2):
            tiles = []
            for h in range(2):
                for f in range(FIELDS):
                    pieces = []
                    for k in range(RUN):
                        at = (f * RUN + k) * 16 + 8 * h
                        pieces.append(sums_ref[par, tile, at : at + 8, :])
                    tiles.append(jnp.concatenate(pieces, axis=0))
            halves.append(jnp.concatenate(swap_blocks(tiles, lane), axis=0))
        rows = pl.ds(pl.multiple_of(step * 8 * height, 8 * height), 8 * height)
        coef_refs[part][rows, :] = jnp.concatenate(halves, axis=1).astype(BF16)
        return carry

    for part in range(parts):
        lax.fori_loop(0, per_part, functools.partial(scatter_rows, part), 0)


def transport(sub, edge, recv, halo, perm, order, taps, scale, weight, table, depart, pick):
    parts = len(recv)
    rows, width = recv[0].shape
    lats = RUN * SUB
    left = FIELDS * (RUN + 1) * 16
    own = FIELDS * RUN * 16
    slots2 = table.shape[1]
    vmem = pl.BlockSpec(memory_space=pltpu.VMEM)
    anywhere = pl.BlockSpec(memory_space=pl.ANY)
    return pl.pallas_call(
        functools.partial(middle_kernel, sub, parts),
        out_shape=(
            jax.ShapeDtypeStruct((FIELDS, 2, lats, NLON), BF16),
            *[jax.ShapeDtypeStruct((rows, width), BF16)] * parts,
        ),
        in_specs=[pl.BlockSpec(memory_space=pltpu.SMEM)] + [vmem] * 6 + [anywhere] * 3 + [vmem] * parts,
        out_specs=(vmem,) * (parts + 1),
        scratch_shapes=[
            pltpu.VMEM((2, slots2, HALF), BF16),
            pltpu.VMEM((2, lats, NLON), jnp.int32),
            pltpu.VMEM((2, lats, NLON), jnp.int32),
            pltpu.VMEM((2, left, slots2), BF16),
            pltpu.VMEM((left, 256), F32),
            pltpu.VMEM((left, 256), F32),
            pltpu.VMEM((FIELDS * REACH, 16, NLON), BF16),
            pltpu.VMEM((FIELDS * REACH, 16, CHUNK + 2 * RIM * 128), BF16),
            pltpu.VMEM((FINE, FIELDS * 2, lats, 128), F32),
            pltpu.VMEM((FINE, 2 * lats, 128), jnp.int32),
            pltpu.VMEM((FINE, RUN, WIDE, 128), BF16),
            pltpu.VMEM((FINE, RUN, 2, 16, 128), BF16),
            pltpu.VMEM((own, NLON), BF16),
            pltpu.VMEM((2, own, HALF), BF16),
            pltpu.VMEM((2, TILES, own, 128), F32),
            pltpu.SemaphoreType.DMA((3,)),
        ],
        compiler_params=pltpu.CompilerParams(vmem_limit_bytes=VMEM_LIMIT),
        cost_estimate=pl.CostEstimate(
            flops=8 * left * slots2 * HALF,
            bytes_accessed=2 * rows * width * 8 + 4 * slots2 * HALF,
            transcendentals=0,
        ),
        name="transport",
    )(edge, halo, perm, order, taps, scale, weight, table, depart, pick, *recv)


def tap_tables(stencil_weight):
    same = jnp.eye(16, dtype=F32)
    table = stencil_weight.T[:, None, :, None] * same[None, :, None, :]
    return table.reshape(16 * 16, NSTEN * 16).astype(BF16)


def exchange(array, axis, distance):
    devices = lax.axis_size(axis)
    return lax.ppermute(array, axis, [(i, i ^ distance) for i in range(devices)])


def gather_rows(spectral):
    devices = lax.axis_size("band")
    band = lax.axis_index("band")
    turned = spectral.transpose(0, 2, 1)
    pieces = [turned] + [exchange(turned, "band", d) for d in range(1, devices)]
    stacked = jnp.stack(pieces)
    ordered = [
        lax.dynamic_index_in_dim(stacked, band ^ b, 0, keepdims=False) for b in range(devices)
    ]
    return jnp.concatenate(ordered, axis=2)


def scatter_sums(sums, slots, row_local):
    devices = lax.axis_size("band")
    band = lax.axis_index("band")
    shaped = sums.reshape(slots, COLS, -1)
    parts = jnp.stack(
        [shaped[:, :, b * row_local : (b + 1) * row_local] for b in range(devices)]
    )
    total = lax.dynamic_index_in_dim(parts, band, 0, keepdims=False).astype(F32)
    for d in range(1, devices):
        piece = lax.dynamic_index_in_dim(parts, band ^ d, 0, keepdims=False)
        total = total + exchange(piece, "band", d).astype(F32)
    return total.astype(BF16).transpose(0, 2, 1)


def per_device(
    spectral, legendre, slot_pair, quad_weight, depart_code, stencil_pick, stencil_weight
):
    slots, row_local, _ = spectral.shape
    height = depart_code.shape[2]
    waves = lax.axis_size("wave")
    sub = height // RUN
    groups = slots // GROUP
    wave_rank = lax.axis_index("wave")
    lat_rank = lax.axis_index(("band", "wave"))
    lat_devices = lax.axis_size(("band", "wave"))
    my_pairs = lax.dynamic_slice_in_dim(slot_pair, wave_rank * slots, slots)
    perm = lane_order()

    parts = 2 if groups % 2 == 0 else 1
    blocks = waves * groups
    arriving = slot_pair.reshape(waves, parts, -1).swapaxes(0, 1).reshape(-1)

    spec = gather_rows(spectral)
    table, scale = angle_tables(arriving)
    taps = tap_tables(stencil_weight)
    my_weight = lax.dynamic_slice_in_dim(quad_weight, wave_rank * height, height)
    weight = my_weight.reshape(sub, RUN).T
    if sub != SUB:
        weight = jnp.pad(weight, ((0, 0), (0, SUB - sub)))
    weight = jnp.broadcast_to(weight[None, :, None, :, None], (FIELDS, RUN, 2, SUB, 128))
    weight = weight.reshape(-1, 128)
    is_first, is_last = lat_rank == 0, lat_rank == lat_devices - 1
    edge = jnp.stack([is_first, is_last]).astype(jnp.int32)
    spec, table, scale, taps, weight, edge, my_pairs = lax.optimization_barrier(
        (spec, table, scale, taps, weight, edge, my_pairs)
    )
    received = []
    for part in range(parts):
        sent = legendre_forward(my_pairs, spec, legendre, waves, part, parts)
        if received:
            sent, received[-1] = lax.optimization_barrier((sent, received[-1]))
        received.append(
            lax.all_to_all(sent, "wave", split_axis=0, concat_axis=0, tiled=True)
        )
    recv = [r.reshape(-1, height, WIDE) for r in received]
    first = jnp.concatenate([r[:, 0 : RIM * sub : sub] for r in recv])
    last = jnp.concatenate([r[:, (RUN - RIM + 1) * sub - 1 :: sub] for r in recv])
    up = [(i, i + 1) for i in range(lat_devices - 1)]
    down = [(i + 1, i) for i in range(lat_devices - 1)]
    before = lax.ppermute(last, ("band", "wave"), up)
    after = lax.ppermute(first, ("band", "wave"), down)
    halo = [jnp.where(is_first, first[:, RIM - 1 - i], before[:, i]) for i in range(RIM)]
    halo += [jnp.where(is_last, last[:, RIM - 1 - i], after[:, i]) for i in range(RIM)]
    halo += [jnp.zeros_like(halo[0])] * (8 - 2 * RIM)
    halo = jnp.stack(halo, axis=1).reshape(blocks * 8, WIDE)

    depart, pick = depart_code[0], stencil_pick[0]
    if sub != SUB:
        gap = SUB - sub
        recv = [r.reshape(-1, RUN, sub, WIDE) for r in recv]
        recv = [jnp.pad(r, ((0, 0), (0, 0), (0, gap), (0, 0))) for r in recv]
        depart = jnp.pad(depart, ((0, 0), (0, RUN * gap), (0, 0)))
        pick = jnp.pad(pick, ((0, 0), (0, RUN * gap), (0, 0)))
    arrival, *coefs = transport(
        sub,
        edge,
        [r.reshape(-1, WIDE) for r in recv],
        halo,
        perm,
        longitude_order(),
        taps,
        scale,
        weight,
        table,
        depart,
        pick,
    )
    arrival = arrival[None, :, :, :height]
    coefs = [c.reshape(-1, RUN, SUB, WIDE)[:, :, :sub] for c in coefs]
    outs, by_wave = [], None
    for part in range(parts):
        leaving = coefs[part].reshape(waves, groups // parts, height, WIDE)
        if part:
            leaving, by_wave = lax.optimization_barrier((leaving, by_wave))
        ready = by_wave
        by_wave = lax.all_to_all(leaving, "wave", split_axis=0, concat_axis=0, tiled=True)
        if part:
            outs.append(legendre_backward(my_pairs, perm, ready, legendre, part - 1))
    outs.append(legendre_backward(my_pairs, perm, by_wave, legendre, parts - 1))
    outs = [scatter_sums(sums, slots // parts, row_local) for sums in outs]
    return (arrival, jnp.concatenate(outs))


def solution(mesh):
    in_specs = (
        P("wave", "band", None),
        P("wave", "band", None),
        P(),
        P("band"),
        P(None, None, ("band", "wave"), None),
        P(None, None, ("band", "wave"), None),
        P(),
    )
    out_specs = (P(None, None, None, ("band", "wave"), None), P("wave", "band", None))
    return jax.shard_map(
        per_device, mesh=mesh, in_specs=in_specs, out_specs=out_specs, check_vma=False
    )
```

```python
import functools
import math

import jax
import jax.numpy as jnp
import numpy as np
from jax import lax
from jax.experimental import pallas as pl
from jax.experimental.pallas import tpu as pltpu
from jax.sharding import PartitionSpec as P

M = 1280
NLON = 5120
HALF = NLON // 2
FIELDS = 4
NSTEN = 16
RIM = 3
COLS = 8
GROUP = 8
WIDE = GROUP * 4 * COLS
RUN = 5
SUB = 8
REACH = RUN + 2 * RIM
TILES = 10
CHUNK = 512
FINE = CHUNK // 128
CHUNKS = NLON // CHUNK
STEP = 8
F32 = jnp.float32
BF16 = jnp.bfloat16
VMEM_LIMIT = 60 * 2**20


def dot_nt(left, right):
    return lax.dot_general(left, right, (((1,), (1,)), ((), ())), preferred_element_type=F32)


def lane_order():
    index = np.arange(WIDE).reshape(GROUP, 2, 2, FIELDS, 2).transpose(1, 2, 3, 4, 0).reshape(-1)
    matrix = np.zeros((WIDE, WIDE), np.float32)
    matrix[index, np.arange(WIDE)] = 1.0
    return jnp.asarray(matrix, BF16)


def longitude_order():
    position = np.arange(CHUNK)
    longitude = FINE * (position % 128) + position // 128
    matrix = np.zeros((CHUNK, CHUNK), np.float32)
    matrix[longitude, position] = 1.0
    return jnp.asarray(np.stack([matrix, matrix.T]), BF16)


def row_masks(pair, rows):
    row = lax.broadcasted_iota(jnp.int32, (1, rows), 1)
    low_count = M - pair
    higher = row >= low_count
    degree = jnp.where(higher, row - low_count, row)
    sign = (1 - 2 * (degree & 1)).astype(F32)
    in_use = row <= M
    side = jnp.where(higher, 1, 0) ^ (pair & 1)
    even = jnp.where(in_use & (side == 0), 1.0, 0.0)
    odd = jnp.where(in_use & (side == 1), 1.0, 0.0)
    return even, odd, sign


def forward_kernel(height, base, pair_ref, spec_ref, leg_ref, out_ref, acc_ref):
    group, step = pl.program_id(0) + base, pl.program_id(1)
    rows = spec_ref.shape[2]
    sub = height // RUN

    pieces = []
    for u in range(STEP):
        even, odd, sign = row_masks(pair_ref[group * GROUP + step * STEP + u], rows)
        spec = spec_ref[u].astype(F32)
        south = spec * sign
        parts = [spec * even, south * even, spec * odd, south * odd]
        masked = jnp.concatenate(parts, axis=0).astype(BF16)
        pieces.append(dot_nt(leg_ref[u], masked))
    for half in range(STEP // 4):
        acc_ref[step * (STEP // 4) + half] = jnp.concatenate(pieces[4 * half : 4 * half + 4], axis=1)

    @pl.when(step == GROUP // STEP - 1)
    def _():
        for dest in range(out_ref.shape[0]):
            halves = []
            for half in range(2):
                pieces = [
                    acc_ref[half, pl.ds(dest * height + k, sub, stride=RUN), :]
                    for k in range(RUN)
                ]
                halves.append(jnp.concatenate(pieces, axis=0))
            out_ref[dest, 0] = jnp.concatenate(halves, axis=1).astype(BF16)


def legendre_forward(pairs, spec, legendre, waves, part, parts):
    slots, lats, rows = legendre.shape
    groups = slots // GROUP // parts
    base = part * groups
    height = lats // waves
    return pl.pallas_call(
        functools.partial(forward_kernel, height, base),
        out_shape=jax.ShapeDtypeStruct((waves, groups, height, WIDE), BF16),
        grid=(groups, GROUP // STEP),
        in_specs=[
            pl.BlockSpec(memory_space=pltpu.SMEM),
            pl.BlockSpec((STEP, COLS, rows), lambda g, t: (GROUP // STEP * (g + base) + t, 0, 0)),
            pl.BlockSpec((STEP, lats, rows), lambda g, t: (GROUP // STEP * (g + base) + t, 0, 0)),
        ],
        out_specs=pl.BlockSpec((waves, 1, height, WIDE), lambda g, t: (0, g, 0, 0)),
        scratch_shapes=[pltpu.VMEM((2, lats, 128), F32)],
        compiler_params=pltpu.CompilerParams(vmem_limit_bytes=VMEM_LIMIT),
        cost_estimate=pl.CostEstimate(
            flops=2 * groups * GROUP * lats * rows * 32,
            bytes_accessed=2 * groups * GROUP * lats * rows,
            transcendentals=0,
        ),
        name="legendre_forward",
    )(pairs, spec, legendre)


def backward_kernel(
    height, base, pair_ref, perm_ref, coef_ref, leg_ref, out_ref, rows_ref, turned_ref
):
    group, step = pl.program_id(0) + base, pl.program_id(1)
    rows = leg_ref.shape[2]
    sub = height // RUN

    @pl.when(step == 0)
    def _():
        for source in range(coef_ref.shape[0]):
            block = coef_ref[source, 0].astype(F32)
            for k in range(RUN):
                for half in range(2):
                    rows_ref[half, pl.ds(source * height + k, sub, stride=RUN), :] = block[
                        k * sub : (k + 1) * sub, 128 * half : 128 * half + 128
                    ]
        natural = jnp.concatenate([rows_ref[0], rows_ref[1]], axis=1).astype(BF16)
        turned_ref[...] = dot_nt(perm_ref[...], natural).astype(BF16)

    sums = []
    for u in range(STEP):
        even, odd, sign = row_masks(pair_ref[group * GROUP + step * STEP + u], rows)
        at = pl.ds(pl.multiple_of(step * (32 * STEP) + 32 * u, 32), 32)
        raw = jnp.dot(turned_ref[at, :], leg_ref[u], preferred_element_type=F32)
        low = raw[0:8] + sign * raw[8:16]
        high = raw[16:24] + sign * raw[24:32]
        sums.append(low * even + high * odd)
    out_ref[...] = jnp.concatenate(sums, axis=0).astype(BF16)


def legendre_backward(pairs, perm, coefs, legendre, part):
    _, lats, rows = legendre.shape
    waves, groups, height, _ = coefs.shape
    slots = groups * GROUP
    base = part * groups
    return pl.pallas_call(
        functools.partial(backward_kernel, height, base),
        out_shape=jax.ShapeDtypeStruct((slots * COLS, rows), BF16),
        grid=(groups, GROUP // STEP),
        in_specs=[
            pl.BlockSpec(memory_space=pltpu.SMEM),
            pl.BlockSpec((WIDE, WIDE), lambda g, t: (0, 0)),
            pl.BlockSpec((waves, 1, height, WIDE), lambda g, t: (0, g, 0, 0)),
            pl.BlockSpec((STEP, lats, rows), lambda g, t: (GROUP // STEP * (g + base) + t, 0, 0)),
        ],
        out_specs=pl.BlockSpec((STEP * COLS, rows), lambda g, t: (GROUP // STEP * g + t, 0)),
        scratch_shapes=[pltpu.VMEM((2, lats, 128), F32), pltpu.VMEM((WIDE, lats), BF16)],
        compiler_params=pltpu.CompilerParams(vmem_limit_bytes=VMEM_LIMIT),
        cost_estimate=pl.CostEstimate(
            flops=2 * slots * lats * rows * 32,
            bytes_accessed=2 * slots * lats * rows,
            transcendentals=0,
        ),
        name="legendre_backward",
    )(pairs, perm, coefs, legendre)


def table_kernel(cos_ref, sin_ref, step_ref, out_ref):
    batch = 4 * GROUP

    def rotate(c, s, step_c, step_s):
        return c * step_c - s * step_s, s * step_c + c * step_s

    def body(i, carry):
        rows = pl.ds(pl.multiple_of(i * batch, batch), batch)
        steps = step_ref[rows, :]
        steps = [jnp.broadcast_to(steps[:, n : n + 1], (batch, 128)) for n in range(4)]
        first = cos_ref[rows, :], sin_ref[rows, :]
        for j in range(FINE):
            c, s = first
            for chunk in range(HALF // CHUNK):
                at = chunk * CHUNK + j * 128
                parts = []
                for g in range(batch // GROUP):
                    parts += [c[GROUP * g : GROUP * g + GROUP], -s[GROUP * g : GROUP * g + GROUP]]
                to = pl.ds(pl.multiple_of(i * 2 * batch, 2 * batch), 2 * batch)
                out_ref[to, at : at + 128] = jnp.concatenate(parts, axis=0).astype(BF16)
                if chunk < HALF // CHUNK - 1:
                    c, s = rotate(c, s, *steps[2:])
            if j < FINE - 1:
                first = rotate(*first, *steps[:2])
        return carry

    lax.fori_loop(0, cos_ref.shape[0] // batch, body, 0)


def angle_tables(slot_pair):
    flipped = M - 1 - slot_pair
    odd = slot_pair % 2 == 1
    waves = jnp.concatenate([jnp.where(odd, flipped, slot_pair), jnp.where(odd, slot_pair, flipped)])
    factor = jnp.where(waves == 0, 1.0, 2.0).astype(F32)
    unit = 2.0 * math.pi / NLON

    def angle(columns):
        columns = jnp.asarray(columns, jnp.int32)
        return (waves[:, None] * columns[None, :] % NLON).astype(F32) * unit

    lanes = angle(FINE * np.arange(128))
    first_cos = factor[:, None] * jnp.cos(lanes)
    first_sin = factor[:, None] * jnp.sin(lanes)
    moves = angle([1, 1, CHUNK, CHUNK])
    steps = jnp.where(jnp.arange(4) % 2 == 0, jnp.cos(moves), jnp.sin(moves))
    count = waves.shape[0]
    table = pl.pallas_call(
        table_kernel,
        out_shape=jax.ShapeDtypeStruct((2 * count, HALF), BF16),
        grid=(count // 128,),
        in_specs=[
            pl.BlockSpec((128, 128), lambda i: (i, 0)),
            pl.BlockSpec((128, 128), lambda i: (i, 0)),
            pl.BlockSpec((128, 4), lambda i: (i, 0)),
        ],
        out_specs=pl.BlockSpec((256, HALF), lambda i: (i, 0)),
        cost_estimate=pl.CostEstimate(
            flops=6 * count * HALF, bytes_accessed=4 * count * HALF, transcendentals=0
        ),
        name="angle_tables",
    )(first_cos, first_sin, steps)
    scale = (1.0 / (factor * math.sqrt(NLON))).reshape(2, 1, -1, 1, GROUP)
    scale = jnp.broadcast_to(scale, (2, 8, count // 2 // GROUP, 2, GROUP))
    return table.reshape(2, count, HALF), scale.reshape(2, 8, count)


def swap_blocks(tiles, lane):
    tiles = list(tiles)
    for d in (4, 2, 1):
        low = (lane // (16 * d)) % 2 == 0
        for i in range(8):
            if i & d:
                continue
            a, b = tiles[i], tiles[i + d]
            tiles[i] = jnp.where(low, a, pltpu.roll(b, 16 * d, 1))
            tiles[i + d] = jnp.where(low, pltpu.roll(a, 128 - 16 * d, 1), b)
    return tiles


def middle_kernel(
    sub, parts, edge_ref, halo_ref, perm_ref, order_ref, taps_ref, scale_ref, weight_ref,
    table_hbm, depart_hbm, pick_hbm, *refs,
):
    recv_refs, arrival_ref, coef_refs = refs[:parts], refs[parts], refs[parts + 1 : 2 * parts + 1]
    (
        table_ref, depart_ref, pick_ref, left_ref, plus_ref, minus_ref, grid_ref, near_ref,
        stage_ref, code_ref, moved_ref, pair_ref, sums_ref, sems,
    ) = refs[2 * parts + 1 :]
    per_part = TILES // parts
    copies = [
        pltpu.make_async_copy(table_hbm, table_ref, sems.at[0]),
        pltpu.make_async_copy(depart_hbm, depart_ref, sems.at[1]),
        pltpu.make_async_copy(pick_hbm, pick_ref, sems.at[2]),
    ]
    for copy in copies:
        copy.start()
    own = FIELDS * RUN * 16
    is_first, is_last = edge_ref[0], edge_ref[1]

    def gather_rows(part, step, carry):
        tile = part * per_part + step
        lane = lax.broadcasted_iota(jnp.int32, (1, 128), 1)
        lanes = pl.ds(pl.multiple_of(tile * 128, 128), 128)
        height = RUN * SUB
        rows = pl.ds(pl.multiple_of(step * 8 * height, 8 * height), 8 * height)
        mixed = jnp.dot(recv_refs[part][rows, :], perm_ref[...], preferred_element_type=F32)
        edge_rows = pl.ds(pl.multiple_of(tile * 64, 64), 64)
        edges = jnp.dot(halo_ref[edge_rows, :], perm_ref[...], preferred_element_type=F32)
        for par in range(2):
            cols = slice(128 * par, 128 * par + 128)
            tiles = swap_blocks([mixed[b * height : (b + 1) * height, cols] for b in range(8)], lane)
            for f in range(FIELDS):
                for k in range(RUN):
                    at = (f * RUN + k) * 16
                    block = [tiles[h * 4 + f][8 * k : 8 * k + 8] for h in range(2)]
                    left_ref[par, at : at + 16, lanes] = jnp.concatenate(block, axis=0).astype(BF16)
            ends = swap_blocks([edges[8 * b : 8 * b + 8, cols] for b in range(8)], lane)
            row = lax.broadcasted_iota(jnp.int32, (8, 128), 0)
            if par == 1:
                sign = jnp.where((row < RIM) & (is_first == 1), -1.0, 1.0)
                ends = [end * sign for end in ends]
            across = (row >= RIM) & (is_last == 1)
            for f in range(FIELDS):
                block = [jnp.where(across, ends[(1 - h) * 4 + f], ends[h * 4 + f]) for h in range(2)]
                at = own + f * 16
                left_ref[par, at : at + 16, lanes] = jnp.concatenate(block, axis=0).astype(BF16)
        return carry

    for part in range(parts):
        lax.fori_loop(0, per_part, functools.partial(gather_rows, part), 0)
    copies[0].wait()

    def to_grid(tile, carry):
        cols = pl.ds(pl.multiple_of(tile * 256, 256), 256)
        even = jnp.dot(left_ref[0], table_ref[0, :, cols], preferred_element_type=F32)
        odd = jnp.dot(left_ref[1], table_ref[1, :, cols], preferred_element_type=F32)
        plus_ref[...] = even + odd
        minus_ref[...] = even - odd
        place = lax.broadcasted_iota(jnp.int32, (8, 256), 0)
        for side, ref in enumerate((plus_ref, minus_ref)):
            to = pl.ds(pl.multiple_of(side * HALF + tile * 256, 256), 256)
            for f in range(FIELDS):
                for k in range(RUN):
                    at = (f * RUN + k) * 16
                    grid_ref[f * REACH + RIM + k, :, to] = ref[at : at + 16, :].astype(BF16)
                for k in range(RIM):
                    before, after = [], []
                    for h in range(2):
                        end = own + f * 16 + 8 * h
                        at = (f * RUN + k + RUN - RIM) * 16 + 8 * h
                        rolled = pltpu.roll(ref[at : at + 8, :], 1, 0)
                        before.append(jnp.where(place == 0, ref[end + k : end + k + 1, :], rolled))
                        at = (f * RUN + k) * 16 + 8 * h
                        rolled = pltpu.roll(ref[at : at + 8, :], 7, 0)
                        end = end + RIM
                        after.append(
                            jnp.where(place == sub - 1, ref[end + k : end + k + 1, :], rolled)
                        )
                    grid_ref[f * REACH + k, :, to] = jnp.concatenate(before, 0).astype(BF16)
                    grid_ref[f * REACH + RIM + RUN + k, :, to] = jnp.concatenate(after, 0).astype(
                        BF16
                    )
        return carry

    lax.fori_loop(0, HALF // 256, to_grid, 0)
    copies[1].wait()
    copies[2].wait()

    def interpolate(chunk, carry):
        lanes = pl.ds(pl.multiple_of(chunk * CHUNK, CHUNK), CHUNK)
        lane = lax.broadcasted_iota(jnp.int32, (16, 128), 1)
        previous = jnp.where(chunk == 0, CHUNKS - 1, chunk - 1)
        following = jnp.where(chunk == CHUNKS - 1, 0, chunk + 1)

        def neighbours(row, carry):
            for j in range(FINE):
                here = grid_ref[row, :, pl.ds(pl.multiple_of(chunk * CHUNK + j * 128, 128), 128)]
                near_ref[row, :, (RIM + j) * 128 : (RIM + j + 1) * 128] = here
                here = here.astype(F32)
                if j >= FINE - RIM:
                    at = pl.ds(pl.multiple_of(previous * CHUNK + j * 128, 128), 128)
                    there = grid_ref[row, :, at].astype(F32)
                    mixed = pltpu.roll(jnp.where(lane == 127, there, here), 1, 1)
                    slot = j - (FINE - RIM)
                    near_ref[row, :, slot * 128 : slot * 128 + 128] = mixed.astype(BF16)
                if j < RIM:
                    at = pl.ds(pl.multiple_of(following * CHUNK + j * 128, 128), 128)
                    there = grid_ref[row, :, at].astype(F32)
                    mixed = pltpu.roll(jnp.where(lane == 0, there, here), 127, 1)
                    slot = RIM + FINE + j
                    near_ref[row, :, slot * 128 : slot * 128 + 128] = mixed.astype(BF16)
            return carry

        lax.fori_loop(0, FIELDS * REACH, neighbours, 0, unroll=4)
        code = pick_ref[:, :, lanes] * 16 + depart_ref[:, :, lanes]
        code = code.reshape(2 * RUN * SUB, CHUNK).astype(F32).astype(BF16)
        code = jnp.dot(code, order_ref[0], preferred_element_type=F32).astype(jnp.int32)
        for j in range(FINE):
            code_ref[j] = code[:, 128 * j : 128 * j + 128]

        def points(j, carry):
            at_lanes = pl.ds(pl.multiple_of(chunk * CHUNK + j * 128, 128), 128)
            for ks in ((0, 1), (2, 3), (4,)):
                index, hits = {}, {}
                for k in ks:
                    codes = [
                        code_ref[j, pl.ds(h * RUN * SUB + k, SUB, stride=RUN), :] for h in range(2)
                    ]
                    index[k] = [code >> 2 for code in codes]
                    column = jnp.concatenate([code & 3 for code in codes], axis=0)
                    column = column.astype(F32).astype(BF16)
                    hits[k] = [column == jnp.asarray(d, BF16) for d in range(4)]
                totals = {}
                for row in range(ks[0], ks[-1] + 7):
                    factors = {}
                    for k in ks:
                        r = row - k
                        if not 0 <= r < 7:
                            continue
                        weights = []
                        for b in range(4):
                            entry = taps_ref[r * 4 + b]
                            found = [jnp.take_along_axis(entry, index[k][h], axis=1) for h in range(2)]
                            weights.append(jnp.concatenate(found, axis=0).astype(BF16))
                        factors[k] = []
                        for c in range(7):
                            values = [(d, weights[c - d]) for d in range(4) if 0 <= c - d < 4]
                            if len(values) == 4:
                                factor, values = values[3][1], values[:3]
                            else:
                                factor = jnp.zeros((16, 128), BF16)
                            for d, value in values:
                                factor = jnp.where(hits[k][d], value, factor)
                            factors[k].append(factor)
                    for f in range(FIELDS):
                        part = {}
                        for c in range(7):
                            lanes_c = pl.ds(pl.multiple_of((j + c) * 128, 128), 128)
                            near = near_ref[f * REACH + row, :, lanes_c]
                            for k in factors:
                                term = factors[k][c] * near
                                part[k] = part[k] + term if k in part else term
                        for k in part:
                            wide = part[k].astype(F32)
                            totals[f, k] = totals[f, k] + wide if (f, k) in totals else wide
                for f in range(FIELDS):
                    for k in ks:
                        at = (f * RUN + k) * 16
                        moved_ref[at : at + 16, at_lanes] = totals[f, k].astype(BF16)
            return carry

        lax.fori_loop(0, FINE, points, 0)
        natural = jnp.dot(moved_ref[:, lanes], order_ref[1], preferred_element_type=F32)
        for j in range(FINE):
            for f in range(FIELDS):
                for k in range(RUN):
                    for h in range(2):
                        at = (f * RUN + k) * 16 + 8 * h
                        stage_ref[j, f * 2 + h, pl.ds(k, SUB, stride=RUN), :] = natural[
                            at : at + 8, 128 * j : 128 * j + 128
                        ]
        for f in range(FIELDS):
            for h in range(2):
                rows = [stage_ref[j, f * 2 + h] for j in range(FINE)]
                arrival_ref[f, h, :, lanes] = jnp.concatenate(rows, axis=1).astype(BF16)
        return carry

    lax.fori_loop(0, CHUNKS, interpolate, 0)

    def fold(tile, carry):
        lanes = pl.ds(pl.multiple_of(tile * 128, 128), 128)
        other = pl.ds(pl.multiple_of(tile * 128 + HALF, 128), 128)
        a, b = moved_ref[:, lanes].astype(F32), moved_ref[:, other].astype(F32)
        pair_ref[0, :, lanes] = (a + b).astype(BF16)
        pair_ref[1, :, lanes] = (a - b).astype(BF16)
        return carry

    lax.fori_loop(0, HALF // 128, fold, 0)

    def to_waves(tile, carry):
        cols = pl.ds(pl.multiple_of(tile * 256, 256), 256)
        for par in range(2):
            out = dot_nt(pair_ref[par], table_ref[par, cols, :])
            out = out * scale_ref[par, 0:1, cols]
            for half in range(2):
                part = out[:, 128 * half : 128 * half + 128] * weight_ref[...]
                sums_ref[par, tile * 2 + half] = part
        return carry

    lax.fori_loop(0, TILES // 2, to_waves, 0)

    def scatter_rows(part, step, carry):
        tile = part * per_part + step
        lane = lax.broadcasted_iota(jnp.int32, (1, 128), 1)
        height = RUN * SUB
        halves = []
        for par in range(2):
            tiles = []
            for h in range(2):
                for f in range(FIELDS):
                    pieces = []
                    for k in range(RUN):
                        at = (f * RUN + k) * 16 + 8 * h
                        pieces.append(sums_ref[par, tile, at : at + 8, :])
                    tiles.append(jnp.concatenate(pieces, axis=0))
            halves.append(jnp.concatenate(swap_blocks(tiles, lane), axis=0))
        rows = pl.ds(pl.multiple_of(step * 8 * height, 8 * height), 8 * height)
        coef_refs[part][rows, :] = jnp.concatenate(halves, axis=1).astype(BF16)
        return carry

    for part in range(parts):
        lax.fori_loop(0, per_part, functools.partial(scatter_rows, part), 0)


def transport(sub, edge, recv, halo, perm, order, taps, scale, weight, table, depart, pick):
    parts = len(recv)
    rows, width = recv[0].shape
    lats = RUN * SUB
    left = FIELDS * (RUN + 1) * 16
    own = FIELDS * RUN * 16
    slots2 = table.shape[1]
    vmem = pl.BlockSpec(memory_space=pltpu.VMEM)
    anywhere = pl.BlockSpec(memory_space=pl.ANY)
    return pl.pallas_call(
        functools.partial(middle_kernel, sub, parts),
        out_shape=(
            jax.ShapeDtypeStruct((FIELDS, 2, lats, NLON), BF16),
            *[jax.ShapeDtypeStruct((rows, width), BF16)] * parts,
        ),
        in_specs=[pl.BlockSpec(memory_space=pltpu.SMEM)] + [vmem] * 6 + [anywhere] * 3 + [vmem] * parts,
        out_specs=(vmem,) * (parts + 1),
        scratch_shapes=[
            pltpu.VMEM((2, slots2, HALF), BF16),
            pltpu.VMEM((2, lats, NLON), jnp.int32),
            pltpu.VMEM((2, lats, NLON), jnp.int32),
            pltpu.VMEM((2, left, slots2), BF16),
            pltpu.VMEM((left, 256), F32),
            pltpu.VMEM((left, 256), F32),
            pltpu.VMEM((FIELDS * REACH, 16, NLON), BF16),
            pltpu.VMEM((FIELDS * REACH, 16, CHUNK + 2 * RIM * 128), BF16),
            pltpu.VMEM((FINE, FIELDS * 2, lats, 128), F32),
            pltpu.VMEM((FINE, 2 * lats, 128), jnp.int32),
            pltpu.VMEM((own, NLON), BF16),
            pltpu.VMEM((2, own, HALF), BF16),
            pltpu.VMEM((2, TILES, own, 128), F32),
            pltpu.SemaphoreType.DMA((3,)),
        ],
        compiler_params=pltpu.CompilerParams(vmem_limit_bytes=VMEM_LIMIT),
        cost_estimate=pl.CostEstimate(
            flops=8 * left * slots2 * HALF,
            bytes_accessed=2 * rows * width * 8 + 4 * slots2 * HALF,
            transcendentals=0,
        ),
        name="transport",
    )(edge, halo, perm, order, taps, scale, weight, table, depart, pick, *recv)


def tap_tables(stencil_weight):
    choose = np.zeros((16, 7, 4, 4), np.float32)
    for r in range(7):
        for d in range(4):
            a = (r - 3) - (d - 2) + 1
            if 0 <= a < 4:
                for b in range(4):
                    choose[4 * a + b, r, b, d] = 1.0
    table = jnp.einsum("tw,wnd->ntd", stencil_weight, choose.reshape(16, 28, 4), precision="highest")
    table = jnp.pad(table.reshape(28, 4 * NSTEN), ((0, 0), (0, 128 - 4 * NSTEN)))
    return jnp.broadcast_to(table[:, None, :], (28, 8, 128))


def exchange(array, axis, distance):
    devices = lax.axis_size(axis)
    return lax.ppermute(array, axis, [(i, i ^ distance) for i in range(devices)])


def gather_rows(spectral):
    devices = lax.axis_size("band")
    band = lax.axis_index("band")
    turned = spectral.transpose(0, 2, 1)
    pieces = [turned] + [exchange(turned, "band", d) for d in range(1, devices)]
    stacked = jnp.stack(pieces)
    ordered = [
        lax.dynamic_index_in_dim(stacked, band ^ b, 0, keepdims=False) for b in range(devices)
    ]
    return jnp.concatenate(ordered, axis=2)


def scatter_sums(sums, slots, row_local):
    devices = lax.axis_size("band")
    band = lax.axis_index("band")
    shaped = sums.reshape(slots, COLS, -1)
    parts = jnp.stack(
        [shaped[:, :, b * row_local : (b + 1) * row_local] for b in range(devices)]
    )
    total = lax.dynamic_index_in_dim(parts, band, 0, keepdims=False).astype(F32)
    for d in range(1, devices):
        piece = lax.dynamic_index_in_dim(parts, band ^ d, 0, keepdims=False)
        total = total + exchange(piece, "band", d).astype(F32)
    return total.astype(BF16).transpose(0, 2, 1)


def per_device(
    spectral, legendre, slot_pair, quad_weight, depart_code, stencil_pick, stencil_weight
):
    slots, row_local, _ = spectral.shape
    height = depart_code.shape[2]
    waves = lax.axis_size("wave")
    sub = height // RUN
    groups = slots // GROUP
    wave_rank = lax.axis_index("wave")
    lat_rank = lax.axis_index(("band", "wave"))
    lat_devices = lax.axis_size(("band", "wave"))
    my_pairs = lax.dynamic_slice_in_dim(slot_pair, wave_rank * slots, slots)
    perm = lane_order()

    parts = 2 if groups % 2 == 0 else 1
    blocks = waves * groups
    arriving = slot_pair.reshape(waves, parts, -1).swapaxes(0, 1).reshape(-1)

    spec = gather_rows(spectral)
    table, scale = angle_tables(arriving)
    taps = tap_tables(stencil_weight)
    my_weight = lax.dynamic_slice_in_dim(quad_weight, wave_rank * height, height)
    weight = my_weight.reshape(sub, RUN).T
    if sub != SUB:
        weight = jnp.pad(weight, ((0, 0), (0, SUB - sub)))
    weight = jnp.broadcast_to(weight[None, :, None, :, None], (FIELDS, RUN, 2, SUB, 128))
    weight = weight.reshape(-1, 128)
    is_first, is_last = lat_rank == 0, lat_rank == lat_devices - 1
    edge = jnp.stack([is_first, is_last]).astype(jnp.int32)
    spec, table, scale, taps, weight, edge, my_pairs = lax.optimization_barrier(
        (spec, table, scale, taps, weight, edge, my_pairs)
    )
    received = []
    for part in range(parts):
        sent = legendre_forward(my_pairs, spec, legendre, waves, part, parts)
        if received:
            sent, received[-1] = lax.optimization_barrier((sent, received[-1]))
        received.append(
            lax.all_to_all(sent, "wave", split_axis=0, concat_axis=0, tiled=True)
        )
    recv = [r.reshape(-1, height, WIDE) for r in received]
    first = jnp.concatenate([r[:, 0 : RIM * sub : sub] for r in recv])
    last = jnp.concatenate([r[:, (RUN - RIM + 1) * sub - 1 :: sub] for r in recv])
    up = [(i, i + 1) for i in range(lat_devices - 1)]
    down = [(i + 1, i) for i in range(lat_devices - 1)]
    before = lax.ppermute(last, ("band", "wave"), up)
    after = lax.ppermute(first, ("band", "wave"), down)
    halo = [jnp.where(is_first, first[:, RIM - 1 - i], before[:, i]) for i in range(RIM)]
    halo += [jnp.where(is_last, last[:, RIM - 1 - i], after[:, i]) for i in range(RIM)]
    halo += [jnp.zeros_like(halo[0])] * (8 - 2 * RIM)
    halo = jnp.stack(halo, axis=1).reshape(blocks * 8, WIDE)

    depart, pick = depart_code[0], stencil_pick[0]
    if sub != SUB:
        gap = SUB - sub
        recv = [r.reshape(-1, RUN, sub, WIDE) for r in recv]
        recv = [jnp.pad(r, ((0, 0), (0, 0), (0, gap), (0, 0))) for r in recv]
        depart = jnp.pad(depart, ((0, 0), (0, RUN * gap), (0, 0)))
        pick = jnp.pad(pick, ((0, 0), (0, RUN * gap), (0, 0)))
    arrival, *coefs = transport(
        sub,
        edge,
        [r.reshape(-1, WIDE) for r in recv],
        halo,
        perm,
        longitude_order(),
        taps,
        scale,
        weight,
        table,
        depart,
        pick,
    )
    arrival = arrival[None, :, :, :height]
    coefs = [c.reshape(-1, RUN, SUB, WIDE)[:, :, :sub] for c in coefs]
    outs, by_wave = [], None
    for part in range(parts):
        leaving = coefs[part].reshape(waves, groups // parts, height, WIDE)
        if part:
            leaving, by_wave = lax.optimization_barrier((leaving, by_wave))
        ready = by_wave
        by_wave = lax.all_to_all(leaving, "wave", split_axis=0, concat_axis=0, tiled=True)
        if part:
            outs.append(legendre_backward(my_pairs, perm, ready, legendre, part - 1))
    outs.append(legendre_backward(my_pairs, perm, by_wave, legendre, parts - 1))
    outs = [scatter_sums(sums, slots // parts, row_local) for sums in outs]
    return (arrival, jnp.concatenate(outs))


def solution(mesh):
    in_specs = (
        P("wave", "band", None),
        P("wave", "band", None),
        P(),
        P("band"),
        P(None, None, ("band", "wave"), None),
        P(None, None, ("band", "wave"), None),
        P(),
    )
    out_specs = (P(None, None, None, ("band", "wave"), None), P("wave", "band", None))
    return jax.shard_map(
        per_device, mesh=mesh, in_specs=in_specs, out_specs=out_specs, check_vma=False
    )
```

```python
import functools
import math

import jax
import jax.numpy as jnp
import numpy as np
from jax import lax
from jax.experimental import pallas as pl
from jax.experimental.pallas import tpu as pltpu
from jax.sharding import PartitionSpec as P

M = 1280
NLON = 5120
HALF = NLON // 2
FIELDS = 4
NSTEN = 16
RIM = 3
COLS = 8
GROUP = 8
WIDE = GROUP * 4 * COLS
RUN = 5
SUB = 8
REACH = RUN + 2 * RIM
TILES = 10
CHUNK = 512
FINE = CHUNK // 128
CHUNKS = NLON // CHUNK
STEP = 8
F32 = jnp.float32
BF16 = jnp.bfloat16
VMEM_LIMIT = 60 * 2**20


def dot_nt(left, right):
    return lax.dot_general(left, right, (((1,), (1,)), ((), ())), preferred_element_type=F32)


def lane_order():
    index = np.arange(WIDE).reshape(GROUP, 2, 2, FIELDS, 2).transpose(1, 2, 3, 4, 0).reshape(-1)
    matrix = np.zeros((WIDE, WIDE), np.float32)
    matrix[index, np.arange(WIDE)] = 1.0
    return jnp.asarray(matrix, BF16)


def longitude_order():
    position = np.arange(CHUNK)
    longitude = FINE * (position % 128) + position // 128
    matrix = np.zeros((CHUNK, CHUNK), np.float32)
    matrix[longitude, position] = 1.0
    return jnp.asarray(np.stack([matrix, matrix.T]), BF16)


def row_masks(pair, rows):
    row = lax.broadcasted_iota(jnp.int32, (1, rows), 1)
    low_count = M - pair
    higher = row >= low_count
    degree = jnp.where(higher, row - low_count, row)
    sign = (1 - 2 * (degree & 1)).astype(F32)
    in_use = row <= M
    side = jnp.where(higher, 1, 0) ^ (pair & 1)
    even = jnp.where(in_use & (side == 0), 1.0, 0.0)
    odd = jnp.where(in_use & (side == 1), 1.0, 0.0)
    return even, odd, sign


def forward_kernel(height, base, pair_ref, spec_ref, leg_ref, out_ref, acc_ref):
    group, step = pl.program_id(0) + base, pl.program_id(1)
    rows = spec_ref.shape[2]
    sub = height // RUN

    pieces = []
    for u in range(STEP):
        even, odd, sign = row_masks(pair_ref[group * GROUP + step * STEP + u], rows)
        spec = spec_ref[u].astype(F32)
        south = spec * sign
        parts = [spec * even, south * even, spec * odd, south * odd]
        masked = jnp.concatenate(parts, axis=0).astype(BF16)
        pieces.append(dot_nt(leg_ref[u], masked))
    for half in range(STEP // 4):
        acc_ref[step * (STEP // 4) + half] = jnp.concatenate(pieces[4 * half : 4 * half + 4], axis=1)

    @pl.when(step == GROUP // STEP - 1)
    def _():
        for dest in range(out_ref.shape[0]):
            halves = []
            for half in range(2):
                pieces = [
                    acc_ref[half, pl.ds(dest * height + k, sub, stride=RUN), :]
                    for k in range(RUN)
                ]
                halves.append(jnp.concatenate(pieces, axis=0))
            out_ref[dest, 0] = jnp.concatenate(halves, axis=1).astype(BF16)


def legendre_forward(pairs, spec, legendre, waves, part, parts):
    slots, lats, rows = legendre.shape
    groups = slots // GROUP // parts
    base = part * groups
    height = lats // waves
    return pl.pallas_call(
        functools.partial(forward_kernel, height, base),
        out_shape=jax.ShapeDtypeStruct((waves, groups, height, WIDE), BF16),
        grid=(groups, GROUP // STEP),
        in_specs=[
            pl.BlockSpec(memory_space=pltpu.SMEM),
            pl.BlockSpec((STEP, COLS, rows), lambda g, t: (GROUP // STEP * (g + base) + t, 0, 0)),
            pl.BlockSpec((STEP, lats, rows), lambda g, t: (GROUP // STEP * (g + base) + t, 0, 0)),
        ],
        out_specs=pl.BlockSpec((waves, 1, height, WIDE), lambda g, t: (0, g, 0, 0)),
        scratch_shapes=[pltpu.VMEM((2, lats, 128), F32)],
        compiler_params=pltpu.CompilerParams(vmem_limit_bytes=VMEM_LIMIT),
        cost_estimate=pl.CostEstimate(
            flops=2 * groups * GROUP * lats * rows * 32,
            bytes_accessed=2 * groups * GROUP * lats * rows,
            transcendentals=0,
        ),
        name="legendre_forward",
    )(pairs, spec, legendre)


def backward_kernel(
    height, base, pair_ref, perm_ref, coef_ref, leg_ref, out_ref, rows_ref, turned_ref
):
    group, step = pl.program_id(0) + base, pl.program_id(1)
    rows = leg_ref.shape[2]
    sub = height // RUN

    @pl.when(step == 0)
    def _():
        for source in range(coef_ref.shape[0]):
            block = coef_ref[source, 0].astype(F32)
            for k in range(RUN):
                for half in range(2):
                    rows_ref[half, pl.ds(source * height + k, sub, stride=RUN), :] = block[
                        k * sub : (k + 1) * sub, 128 * half : 128 * half + 128
                    ]
        natural = jnp.concatenate([rows_ref[0], rows_ref[1]], axis=1).astype(BF16)
        turned_ref[...] = dot_nt(perm_ref[...], natural).astype(BF16)

    sums = []
    for u in range(STEP):
        even, odd, sign = row_masks(pair_ref[group * GROUP + step * STEP + u], rows)
        at = pl.ds(pl.multiple_of(step * (32 * STEP) + 32 * u, 32), 32)
        raw = jnp.dot(turned_ref[at, :], leg_ref[u], preferred_element_type=F32)
        low = raw[0:8] + sign * raw[8:16]
        high = raw[16:24] + sign * raw[24:32]
        sums.append(low * even + high * odd)
    out_ref[...] = jnp.concatenate(sums, axis=0).astype(BF16)


def legendre_backward(pairs, perm, coefs, legendre, part):
    _, lats, rows = legendre.shape
    waves, groups, height, _ = coefs.shape
    slots = groups * GROUP
    base = part * groups
    return pl.pallas_call(
        functools.partial(backward_kernel, height, base),
        out_shape=jax.ShapeDtypeStruct((slots * COLS, rows), BF16),
        grid=(groups, GROUP // STEP),
        in_specs=[
            pl.BlockSpec(memory_space=pltpu.SMEM),
            pl.BlockSpec((WIDE, WIDE), lambda g, t: (0, 0)),
            pl.BlockSpec((waves, 1, height, WIDE), lambda g, t: (0, g, 0, 0)),
            pl.BlockSpec((STEP, lats, rows), lambda g, t: (GROUP // STEP * (g + base) + t, 0, 0)),
        ],
        out_specs=pl.BlockSpec((STEP * COLS, rows), lambda g, t: (GROUP // STEP * g + t, 0)),
        scratch_shapes=[pltpu.VMEM((2, lats, 128), F32), pltpu.VMEM((WIDE, lats), BF16)],
        compiler_params=pltpu.CompilerParams(vmem_limit_bytes=VMEM_LIMIT),
        cost_estimate=pl.CostEstimate(
            flops=2 * slots * lats * rows * 32,
            bytes_accessed=2 * slots * lats * rows,
            transcendentals=0,
        ),
        name="legendre_backward",
    )(pairs, perm, coefs, legendre)


def table_kernel(cos_ref, sin_ref, step_ref, out_ref):
    batch = 4 * GROUP

    def rotate(c, s, step_c, step_s):
        return c * step_c - s * step_s, s * step_c + c * step_s

    def body(i, carry):
        rows = pl.ds(pl.multiple_of(i * batch, batch), batch)
        steps = step_ref[rows, :]
        steps = [jnp.broadcast_to(steps[:, n : n + 1], (batch, 128)) for n in range(4)]
        first = cos_ref[rows, :], sin_ref[rows, :]
        for j in range(FINE):
            c, s = first
            for chunk in range(HALF // CHUNK):
                at = chunk * CHUNK + j * 128
                parts = []
                for g in range(batch // GROUP):
                    parts += [c[GROUP * g : GROUP * g + GROUP], -s[GROUP * g : GROUP * g + GROUP]]
                to = pl.ds(pl.multiple_of(i * 2 * batch, 2 * batch), 2 * batch)
                out_ref[to, at : at + 128] = jnp.concatenate(parts, axis=0).astype(BF16)
                if chunk < HALF // CHUNK - 1:
                    c, s = rotate(c, s, *steps[2:])
            if j < FINE - 1:
                first = rotate(*first, *steps[:2])
        return carry

    lax.fori_loop(0, cos_ref.shape[0] // batch, body, 0)


def angle_tables(slot_pair):
    flipped = M - 1 - slot_pair
    odd = slot_pair % 2 == 1
    waves = jnp.concatenate([jnp.where(odd, flipped, slot_pair), jnp.where(odd, slot_pair, flipped)])
    factor = jnp.where(waves == 0, 1.0, 2.0).astype(F32)
    unit = 2.0 * math.pi / NLON

    def angle(columns):
        columns = jnp.asarray(columns, jnp.int32)
        return (waves[:, None] * columns[None, :] % NLON).astype(F32) * unit

    lanes = angle(FINE * np.arange(128))
    first_cos = factor[:, None] * jnp.cos(lanes)
    first_sin = factor[:, None] * jnp.sin(lanes)
    moves = angle([1, 1, CHUNK, CHUNK])
    steps = jnp.where(jnp.arange(4) % 2 == 0, jnp.cos(moves), jnp.sin(moves))
    count = waves.shape[0]
    table = pl.pallas_call(
        table_kernel,
        out_shape=jax.ShapeDtypeStruct((2 * count, HALF), BF16),
        grid=(count // 128,),
        in_specs=[
            pl.BlockSpec((128, 128), lambda i: (i, 0)),
            pl.BlockSpec((128, 128), lambda i: (i, 0)),
            pl.BlockSpec((128, 4), lambda i: (i, 0)),
        ],
        out_specs=pl.BlockSpec((256, HALF), lambda i: (i, 0)),
        cost_estimate=pl.CostEstimate(
            flops=6 * count * HALF, bytes_accessed=4 * count * HALF, transcendentals=0
        ),
        name="angle_tables",
    )(first_cos, first_sin, steps)
    scale = (1.0 / (factor * math.sqrt(NLON))).reshape(2, 1, -1, 1, GROUP)
    scale = jnp.broadcast_to(scale, (2, 8, count // 2 // GROUP, 2, GROUP))
    return table.reshape(2, count, HALF), scale.reshape(2, 8, count)


def swap_blocks(tiles, lane):
    tiles = list(tiles)
    for d in (4, 2, 1):
        low = (lane // (16 * d)) % 2 == 0
        for i in range(8):
            if i & d:
                continue
            a, b = tiles[i], tiles[i + d]
            tiles[i] = jnp.where(low, a, pltpu.roll(b, 16 * d, 1))
            tiles[i + d] = jnp.where(low, pltpu.roll(a, 128 - 16 * d, 1), b)
    return tiles


def middle_kernel(
    sub, parts, edge_ref, halo_ref, perm_ref, order_ref, taps_ref, scale_ref, weight_ref,
    table_hbm, depart_hbm, pick_hbm, *refs,
):
    recv_refs, arrival_ref, coef_refs = refs[:parts], refs[parts], refs[parts + 1 : 2 * parts + 1]
    (
        table_ref, depart_ref, pick_ref, left_ref, plus_ref, minus_ref, grid_ref, near_ref,
        stage_ref, code_ref, moved_ref, pair_ref, sums_ref, sems,
    ) = refs[2 * parts + 1 :]
    per_part = TILES // parts
    copies = [
        pltpu.make_async_copy(table_hbm, table_ref, sems.at[0]),
        pltpu.make_async_copy(depart_hbm, depart_ref, sems.at[1]),
        pltpu.make_async_copy(pick_hbm, pick_ref, sems.at[2]),
    ]
    for copy in copies:
        copy.start()
    own = FIELDS * RUN * 16
    is_first, is_last = edge_ref[0], edge_ref[1]

    def gather_rows(part, step, carry):
        tile = part * per_part + step
        lane = lax.broadcasted_iota(jnp.int32, (1, 128), 1)
        lanes = pl.ds(pl.multiple_of(tile * 128, 128), 128)
        height = RUN * SUB
        rows = pl.ds(pl.multiple_of(step * 8 * height, 8 * height), 8 * height)
        mixed = jnp.dot(recv_refs[part][rows, :], perm_ref[...], preferred_element_type=F32)
        edge_rows = pl.ds(pl.multiple_of(tile * 64, 64), 64)
        edges = jnp.dot(halo_ref[edge_rows, :], perm_ref[...], preferred_element_type=F32)
        for par in range(2):
            cols = slice(128 * par, 128 * par + 128)
            tiles = swap_blocks([mixed[b * height : (b + 1) * height, cols] for b in range(8)], lane)
            for f in range(FIELDS):
                for k in range(RUN):
                    at = (f * RUN + k) * 16
                    block = [tiles[h * 4 + f][8 * k : 8 * k + 8] for h in range(2)]
                    left_ref[par, at : at + 16, lanes] = jnp.concatenate(block, axis=0).astype(BF16)
            ends = swap_blocks([edges[8 * b : 8 * b + 8, cols] for b in range(8)], lane)
            row = lax.broadcasted_iota(jnp.int32, (8, 128), 0)
            if par == 1:
                sign = jnp.where((row < RIM) & (is_first == 1), -1.0, 1.0)
                ends = [end * sign for end in ends]
            across = (row >= RIM) & (is_last == 1)
            for f in range(FIELDS):
                block = [jnp.where(across, ends[(1 - h) * 4 + f], ends[h * 4 + f]) for h in range(2)]
                at = own + f * 16
                left_ref[par, at : at + 16, lanes] = jnp.concatenate(block, axis=0).astype(BF16)
        return carry

    for part in range(parts):
        lax.fori_loop(0, per_part, functools.partial(gather_rows, part), 0)
    copies[0].wait()

    def to_grid(tile, carry):
        cols = pl.ds(pl.multiple_of(tile * 256, 256), 256)
        even = jnp.dot(left_ref[0], table_ref[0, :, cols], preferred_element_type=F32)
        odd = jnp.dot(left_ref[1], table_ref[1, :, cols], preferred_element_type=F32)
        plus_ref[...] = even + odd
        minus_ref[...] = even - odd
        place = lax.broadcasted_iota(jnp.int32, (8, 256), 0)
        for side, ref in enumerate((plus_ref, minus_ref)):
            to = pl.ds(pl.multiple_of(side * HALF + tile * 256, 256), 256)
            for f in range(FIELDS):
                for k in range(RUN):
                    at = (f * RUN + k) * 16
                    grid_ref[f * REACH + RIM + k, :, to] = ref[at : at + 16, :].astype(BF16)
                for k in range(RIM):
                    before, after = [], []
                    for h in range(2):
                        end = own + f * 16 + 8 * h
                        at = (f * RUN + k + RUN - RIM) * 16 + 8 * h
                        rolled = pltpu.roll(ref[at : at + 8, :], 1, 0)
                        before.append(jnp.where(place == 0, ref[end + k : end + k + 1, :], rolled))
                        at = (f * RUN + k) * 16 + 8 * h
                        rolled = pltpu.roll(ref[at : at + 8, :], 7, 0)
                        end = end + RIM
                        after.append(
                            jnp.where(place == sub - 1, ref[end + k : end + k + 1, :], rolled)
                        )
                    grid_ref[f * REACH + k, :, to] = jnp.concatenate(before, 0).astype(BF16)
                    grid_ref[f * REACH + RIM + RUN + k, :, to] = jnp.concatenate(after, 0).astype(
                        BF16
                    )
        return carry

    lax.fori_loop(0, HALF // 256, to_grid, 0)
    copies[1].wait()
    copies[2].wait()

    def interpolate(chunk, carry):
        lanes = pl.ds(pl.multiple_of(chunk * CHUNK, CHUNK), CHUNK)
        lane = lax.broadcasted_iota(jnp.int32, (16, 128), 1)
        previous = jnp.where(chunk == 0, CHUNKS - 1, chunk - 1)
        following = jnp.where(chunk == CHUNKS - 1, 0, chunk + 1)

        def neighbours(row, carry):
            for j in range(FINE):
                here = grid_ref[row, :, pl.ds(pl.multiple_of(chunk * CHUNK + j * 128, 128), 128)]
                here = here.astype(F32)
                near_ref[row, :, (RIM + j) * 128 : (RIM + j + 1) * 128] = here
                if j >= FINE - RIM:
                    at = pl.ds(pl.multiple_of(previous * CHUNK + j * 128, 128), 128)
                    there = grid_ref[row, :, at].astype(F32)
                    mixed = pltpu.roll(jnp.where(lane == 127, there, here), 1, 1)
                    slot = j - (FINE - RIM)
                    near_ref[row, :, slot * 128 : slot * 128 + 128] = mixed
                if j < RIM:
                    at = pl.ds(pl.multiple_of(following * CHUNK + j * 128, 128), 128)
                    there = grid_ref[row, :, at].astype(F32)
                    mixed = pltpu.roll(jnp.where(lane == 0, there, here), 127, 1)
                    slot = RIM + FINE + j
                    near_ref[row, :, slot * 128 : slot * 128 + 128] = mixed
            return carry

        lax.fori_loop(0, FIELDS * REACH, neighbours, 0, unroll=4)
        code = pick_ref[:, :, lanes] * 16 + depart_ref[:, :, lanes]
        code = code.reshape(2 * RUN * SUB, CHUNK).astype(F32).astype(BF16)
        code = jnp.dot(code, order_ref[0], preferred_element_type=F32).astype(jnp.int32)
        for j in range(FINE):
            code_ref[j] = code[:, 128 * j : 128 * j + 128]

        def points(j, carry):
            at_lanes = pl.ds(pl.multiple_of(chunk * CHUNK + j * 128, 128), 128)
            for ks in ((0, 1), (2, 3), (4,)):
                index, hits = {}, {}
                for k in ks:
                    codes = [
                        code_ref[j, pl.ds(h * RUN * SUB + k, SUB, stride=RUN), :] for h in range(2)
                    ]
                    index[k] = [code >> 2 for code in codes]
                    column = jnp.concatenate([code & 3 for code in codes], axis=0)
                    column = column.astype(F32).astype(BF16)
                    hits[k] = [column == jnp.asarray(d, BF16) for d in range(4)]
                totals = {}
                for row in range(ks[0], ks[-1] + 7):
                    factors = {}
                    for k in ks:
                        r = row - k
                        if not 0 <= r < 7:
                            continue
                        weights = []
                        for b in range(4):
                            entry = taps_ref[r * 4 + b]
                            found = [jnp.take_along_axis(entry, index[k][h], axis=1) for h in range(2)]
                            weights.append(jnp.concatenate(found, axis=0).astype(BF16))
                        factors[k] = []
                        for c in range(7):
                            values = [(d, weights[c - d]) for d in range(4) if 0 <= c - d < 4]
                            if len(values) == 4:
                                factor, values = values[3][1], values[:3]
                            else:
                                factor = jnp.zeros((16, 128), BF16)
                            for d, value in values:
                                factor = jnp.where(hits[k][d], value, factor)
                            factors[k].append(factor)
                    for f in range(FIELDS):
                        part = {}
                        for c in range(7):
                            lanes_c = pl.ds(pl.multiple_of((j + c) * 128, 128), 128)
                            near = near_ref[f * REACH + row, :, lanes_c].astype(BF16)
                            for k in factors:
                                term = factors[k][c] * near
                                part[k] = part[k] + term if k in part else term
                        for k in part:
                            wide = part[k].astype(F32)
                            totals[f, k] = totals[f, k] + wide if (f, k) in totals else wide
                for f in range(FIELDS):
                    for k in ks:
                        at = (f * RUN + k) * 16
                        moved_ref[at : at + 16, at_lanes] = totals[f, k].astype(BF16)
            return carry

        lax.fori_loop(0, FINE, points, 0)
        natural = jnp.dot(moved_ref[:, lanes], order_ref[1], preferred_element_type=F32)
        for j in range(FINE):
            for f in range(FIELDS):
                for k in range(RUN):
                    for h in range(2):
                        at = (f * RUN + k) * 16 + 8 * h
                        stage_ref[j, f * 2 + h, pl.ds(k, SUB, stride=RUN), :] = natural[
                            at : at + 8, 128 * j : 128 * j + 128
                        ]
        for f in range(FIELDS):
            for h in range(2):
                rows = [stage_ref[j, f * 2 + h] for j in range(FINE)]
                arrival_ref[f, h, :, lanes] = jnp.concatenate(rows, axis=1).astype(BF16)
        return carry

    lax.fori_loop(0, CHUNKS, interpolate, 0)

    def fold(tile, carry):
        lanes = pl.ds(pl.multiple_of(tile * 128, 128), 128)
        other = pl.ds(pl.multiple_of(tile * 128 + HALF, 128), 128)
        a, b = moved_ref[:, lanes].astype(F32), moved_ref[:, other].astype(F32)
        pair_ref[0, :, lanes] = (a + b).astype(BF16)
        pair_ref[1, :, lanes] = (a - b).astype(BF16)
        return carry

    lax.fori_loop(0, HALF // 128, fold, 0)

    def to_waves(tile, carry):
        cols = pl.ds(pl.multiple_of(tile * 256, 256), 256)
        for par in range(2):
            out = dot_nt(pair_ref[par], table_ref[par, cols, :])
            out = out * scale_ref[par, 0:1, cols]
            for half in range(2):
                part = out[:, 128 * half : 128 * half + 128] * weight_ref[...]
                sums_ref[par, tile * 2 + half] = part
        return carry

    lax.fori_loop(0, TILES // 2, to_waves, 0)

    def scatter_rows(part, step, carry):
        tile = part * per_part + step
        lane = lax.broadcasted_iota(jnp.int32, (1, 128), 1)
        height = RUN * SUB
        halves = []
        for par in range(2):
            tiles = []
            for h in range(2):
                for f in range(FIELDS):
                    pieces = []
                    for k in range(RUN):
                        at = (f * RUN + k) * 16 + 8 * h
                        pieces.append(sums_ref[par, tile, at : at + 8, :])
                    tiles.append(jnp.concatenate(pieces, axis=0))
            halves.append(jnp.concatenate(swap_blocks(tiles, lane), axis=0))
        rows = pl.ds(pl.multiple_of(step * 8 * height, 8 * height), 8 * height)
        coef_refs[part][rows, :] = jnp.concatenate(halves, axis=1).astype(BF16)
        return carry

    for part in range(parts):
        lax.fori_loop(0, per_part, functools.partial(scatter_rows, part), 0)


def transport(sub, edge, recv, halo, perm, order, taps, scale, weight, table, depart, pick):
    parts = len(recv)
    rows, width = recv[0].shape
    lats = RUN * SUB
    left = FIELDS * (RUN + 1) * 16
    own = FIELDS * RUN * 16
    slots2 = table.shape[1]
    vmem = pl.BlockSpec(memory_space=pltpu.VMEM)
    anywhere = pl.BlockSpec(memory_space=pl.ANY)
    return pl.pallas_call(
        functools.partial(middle_kernel, sub, parts),
        out_shape=(
            jax.ShapeDtypeStruct((FIELDS, 2, lats, NLON), BF16),
            *[jax.ShapeDtypeStruct((rows, width), BF16)] * parts,
        ),
        in_specs=[pl.BlockSpec(memory_space=pltpu.SMEM)] + [vmem] * 6 + [anywhere] * 3 + [vmem] * parts,
        out_specs=(vmem,) * (parts + 1),
        scratch_shapes=[
            pltpu.VMEM((2, slots2, HALF), BF16),
            pltpu.VMEM((2, lats, NLON), jnp.int32),
            pltpu.VMEM((2, lats, NLON), jnp.int32),
            pltpu.VMEM((2, left, slots2), BF16),
            pltpu.VMEM((left, 256), F32),
            pltpu.VMEM((left, 256), F32),
            pltpu.VMEM((FIELDS * REACH, 16, NLON), BF16),
            pltpu.VMEM((FIELDS * REACH, 16, CHUNK + 2 * RIM * 128), F32),
            pltpu.VMEM((FINE, FIELDS * 2, lats, 128), F32),
            pltpu.VMEM((FINE, 2 * lats, 128), jnp.int32),
            pltpu.VMEM((own, NLON), BF16),
            pltpu.VMEM((2, own, HALF), BF16),
            pltpu.VMEM((2, TILES, own, 128), F32),
            pltpu.SemaphoreType.DMA((3,)),
        ],
        compiler_params=pltpu.CompilerParams(vmem_limit_bytes=VMEM_LIMIT),
        cost_estimate=pl.CostEstimate(
            flops=8 * left * slots2 * HALF,
            bytes_accessed=2 * rows * width * 8 + 4 * slots2 * HALF,
            transcendentals=0,
        ),
        name="transport",
    )(edge, halo, perm, order, taps, scale, weight, table, depart, pick, *recv)


def tap_tables(stencil_weight):
    choose = np.zeros((16, 7, 4, 4), np.float32)
    for r in range(7):
        for d in range(4):
            a = (r - 3) - (d - 2) + 1
            if 0 <= a < 4:
                for b in range(4):
                    choose[4 * a + b, r, b, d] = 1.0
    table = jnp.einsum("tw,wnd->ntd", stencil_weight, choose.reshape(16, 28, 4), precision="highest")
    table = jnp.pad(table.reshape(28, 4 * NSTEN), ((0, 0), (0, 128 - 4 * NSTEN)))
    return jnp.broadcast_to(table[:, None, :], (28, 8, 128))


def exchange(array, axis, distance):
    devices = lax.axis_size(axis)
    return lax.ppermute(array, axis, [(i, i ^ distance) for i in range(devices)])


def gather_rows(spectral):
    devices = lax.axis_size("band")
    band = lax.axis_index("band")
    turned = spectral.transpose(0, 2, 1)
    pieces = [turned] + [exchange(turned, "band", d) for d in range(1, devices)]
    stacked = jnp.stack(pieces)
    ordered = [
        lax.dynamic_index_in_dim(stacked, band ^ b, 0, keepdims=False) for b in range(devices)
    ]
    return jnp.concatenate(ordered, axis=2)


def scatter_sums(sums, slots, row_local):
    devices = lax.axis_size("band")
    band = lax.axis_index("band")
    shaped = sums.reshape(slots, COLS, -1)
    parts = jnp.stack(
        [shaped[:, :, b * row_local : (b + 1) * row_local] for b in range(devices)]
    )
    total = lax.dynamic_index_in_dim(parts, band, 0, keepdims=False).astype(F32)
    for d in range(1, devices):
        piece = lax.dynamic_index_in_dim(parts, band ^ d, 0, keepdims=False)
        total = total + exchange(piece, "band", d).astype(F32)
    return total.astype(BF16).transpose(0, 2, 1)


def per_device(
    spectral, legendre, slot_pair, quad_weight, depart_code, stencil_pick, stencil_weight
):
    slots, row_local, _ = spectral.shape
    height = depart_code.shape[2]
    waves = lax.axis_size("wave")
    sub = height // RUN
    groups = slots // GROUP
    wave_rank = lax.axis_index("wave")
    lat_rank = lax.axis_index(("band", "wave"))
    lat_devices = lax.axis_size(("band", "wave"))
    my_pairs = lax.dynamic_slice_in_dim(slot_pair, wave_rank * slots, slots)
    perm = lane_order()

    parts = 2 if groups % 2 == 0 else 1
    blocks = waves * groups
    arriving = slot_pair.reshape(waves, parts, -1).swapaxes(0, 1).reshape(-1)

    spec = gather_rows(spectral)
    table, scale = angle_tables(arriving)
    taps = tap_tables(stencil_weight)
    my_weight = lax.dynamic_slice_in_dim(quad_weight, wave_rank * height, height)
    weight = my_weight.reshape(sub, RUN).T
    if sub != SUB:
        weight = jnp.pad(weight, ((0, 0), (0, SUB - sub)))
    weight = jnp.broadcast_to(weight[None, :, None, :, None], (FIELDS, RUN, 2, SUB, 128))
    weight = weight.reshape(-1, 128)
    is_first, is_last = lat_rank == 0, lat_rank == lat_devices - 1
    edge = jnp.stack([is_first, is_last]).astype(jnp.int32)
    spec, table, scale, taps, weight, edge, my_pairs = lax.optimization_barrier(
        (spec, table, scale, taps, weight, edge, my_pairs)
    )
    received = []
    for part in range(parts):
        sent = legendre_forward(my_pairs, spec, legendre, waves, part, parts)
        if received:
            sent, received[-1] = lax.optimization_barrier((sent, received[-1]))
        received.append(
            lax.all_to_all(sent, "wave", split_axis=0, concat_axis=0, tiled=True)
        )
    recv = [r.reshape(-1, height, WIDE) for r in received]
    first = jnp.concatenate([r[:, 0 : RIM * sub : sub] for r in recv])
    last = jnp.concatenate([r[:, (RUN - RIM + 1) * sub - 1 :: sub] for r in recv])
    up = [(i, i + 1) for i in range(lat_devices - 1)]
    down = [(i + 1, i) for i in range(lat_devices - 1)]
    before = lax.ppermute(last, ("band", "wave"), up)
    after = lax.ppermute(first, ("band", "wave"), down)
    halo = [jnp.where(is_first, first[:, RIM - 1 - i], before[:, i]) for i in range(RIM)]
    halo += [jnp.where(is_last, last[:, RIM - 1 - i], after[:, i]) for i in range(RIM)]
    halo += [jnp.zeros_like(halo[0])] * (8 - 2 * RIM)
    halo = jnp.stack(halo, axis=1).reshape(blocks * 8, WIDE)

    depart, pick = depart_code[0], stencil_pick[0]
    if sub != SUB:
        gap = SUB - sub
        recv = [r.reshape(-1, RUN, sub, WIDE) for r in recv]
        recv = [jnp.pad(r, ((0, 0), (0, 0), (0, gap), (0, 0))) for r in recv]
        depart = jnp.pad(depart, ((0, 0), (0, RUN * gap), (0, 0)))
        pick = jnp.pad(pick, ((0, 0), (0, RUN * gap), (0, 0)))
    arrival, *coefs = transport(
        sub,
        edge,
        [r.reshape(-1, WIDE) for r in recv],
        halo,
        perm,
        longitude_order(),
        taps,
        scale,
        weight,
        table,
        depart,
        pick,
    )
    arrival = arrival[None, :, :, :height]
    coefs = [c.reshape(-1, RUN, SUB, WIDE)[:, :, :sub] for c in coefs]
    outs, by_wave = [], None
    for part in range(parts):
        leaving = coefs[part].reshape(waves, groups // parts, height, WIDE)
        if part:
            leaving, by_wave = lax.optimization_barrier((leaving, by_wave))
        ready = by_wave
        by_wave = lax.all_to_all(leaving, "wave", split_axis=0, concat_axis=0, tiled=True)
        if part:
            outs.append(legendre_backward(my_pairs, perm, ready, legendre, part - 1))
    outs.append(legendre_backward(my_pairs, perm, by_wave, legendre, parts - 1))
    outs = [scatter_sums(sums, slots // parts, row_local) for sums in outs]
    return (arrival, jnp.concatenate(outs))


def solution(mesh):
    in_specs = (
        P("wave", "band", None),
        P("wave", "band", None),
        P(),
        P("band"),
        P(None, None, ("band", "wave"), None),
        P(None, None, ("band", "wave"), None),
        P(),
    )
    out_specs = (P(None, None, None, ("band", "wave"), None), P("wave", "band", None))
    return jax.shard_map(
        per_device, mesh=mesh, in_specs=in_specs, out_specs=out_specs, check_vma=False
    )
```
